32 devices in a mesh: cells: 8 (over z, x), slots: 4 (over y, core).
Axes of the slice: x: 2, y: 2, z: 4, core: 2. Of those that a mesh axis runs over, the one named last changes fastest.
Arguments:
- tokens: bfloat16 [16, 2048, 256], P('cells', 'slots'), may hold values from -6 to 6
- valid_len: int32 [16], P('cells'), may hold values from 256 to 2048, as said below
- library: int32 [16], P('cells'), may hold values from 512 to 33279
- gene_slot: int32 [16, 2048], P('cells'), may hold values from 0 to 2047, as said below
- counts: int32 [16, 2048], P('cells', 'slots'), may hold values from 0 to 71, as said below
- norm1_gain: float32 [256], replicated, may hold values from 0.5 to 1.5
- w_qkv: bfloat16 [256, 768], replicated, may hold values from -0.375 to 0.375
- w_out: bfloat16 [256, 256], replicated, may hold values from -1.5 to 1.5
- norm2_gain: float32 [256], replicated, may hold values from 0.5 to 1.5
- w_up: bfloat16 [256, 1024], replicated, may hold values from -0.375 to 0.375
- w_down: bfloat16 [1024, 256], replicated, may hold values from -0.1875 to 0.1875
- w_decoder: bfloat16 [3, 256], replicated, may hold values from -0.375 to 0.375
Outputs:
- grad_tokens: float32 [16, 2048, 256], P('cells', 'slots')
- grad_norm1_gain: float32 [256], replicated
- grad_w_qkv: float32 [256, 768], replicated
- grad_w_out: float32 [256, 256], replicated
- grad_norm2_gain: float32 [256], replicated
- grad_w_up: float32 [256, 1024], replicated
- grad_w_down: float32 [1024, 256], replicated
- grad_w_decoder: float32 [3, 256], replicated
- summary: float32 [4], replicated
The draws below stay inside these ranges and needn't reach their ends.
Inputs may be any that keep to these rules, and one draw needn't show every extreme that they name: `valid_len`: in each aligned block of 2 cells one cell has all 2048 slots valid. `gene_slot`: each row is a permutation of the gene numbers 0 to 2047; the 512 slots of an aligned block hold exactly 128 gene numbers of each aligned block of 512 gene numbers. `counts`: indexed by cell and gene number.
All inputs are finite; a program needn't handle non-finite values.
Results may differ from the reference program's by a relative error of at most 0.0055.
Values may be sent and summed in bfloat16 or wider, within the bound.
No kernel may reach another device: no remote copies, remote signals or barrier semaphores. Data moves between devices by JAX's collectives and lax.ppermute only.
A program may use at most 128 MiB of HBM per device.

```python
import jax
import jax.numpy as jnp
from jax import lax

D = 256
FF = 1024
HEADS = 4
CELL_DEV = 2
L = 2048
CELLS = 16
LQ = 512
SHARE = 128


def draw_valid_len(key, part):
    key = jax.random.fold_in(key, 11)
    first_key, second_key, third_key = jax.random.split(key, 3)
    lengths = jax.random.randint(first_key, (CELLS,), L // 8, L + 1)
    chosen = jax.random.randint(second_key, (CELLS // CELL_DEV,), 0, CELL_DEV)
    full = jnp.arange(CELLS) % CELL_DEV == jnp.repeat(chosen, CELL_DEV)
    picked_block = jax.random.randint(third_key, (), 0, CELLS // CELL_DEV)
    other = (chosen[picked_block] + 1) % CELL_DEV
    shortest = jnp.arange(CELLS) == picked_block * CELL_DEV + other
    lengths = jnp.where(shortest, L // 8, lengths)
    return jnp.where(full, L, lengths).astype(jnp.int32)


def draw_library(key, part):
    key = jax.random.fold_in(key, 12)
    first_key, second_key, third_key = jax.random.split(key, 3)
    exponent = jax.random.randint(first_key, (CELLS,), 9, 16)
    extra = jax.random.randint(second_key, (CELLS,), 0, 512)
    values = jnp.left_shift(jnp.ones((CELLS,), jnp.int32), exponent) + extra
    order = jax.random.permutation(third_key, CELLS)
    places = jnp.arange(CELLS)
    values = jnp.where(places == order[0], 512, values)
    values = jnp.where(places == order[1], 33279, values)
    return values.astype(jnp.int32)


def draw_counts(key, part):
    key = jax.random.fold_in(key, 13)
    first_key, second_key, third_key, fourth_key = jax.random.split(key, 4)
    silent = jax.random.randint(first_key, (CELLS, L), 0, 3) == 0
    exponent = jax.random.randint(second_key, (CELLS, L), 0, 7)
    extra = jax.random.randint(third_key, (CELLS, L), 0, 8)
    level = jnp.left_shift(jnp.ones((CELLS, L), jnp.int32), exponent) + extra
    values = jnp.where(silent, 0, level)
    spot = jax.random.randint(fourth_key, (), 0, CELLS * L)
    flat_place = jnp.arange(CELLS * L).reshape(CELLS, L)
    return jnp.where(flat_place == spot, 71, values).astype(jnp.int32)


def draw_gene_slot(key, part):
    key = jax.random.fold_in(key, 14)
    owners = L // LQ
    several = jax.random.split(key, CELLS * owners)
    orders = jax.vmap(lambda single: jax.random.permutation(single, LQ))(several).reshape(CELLS, owners, LQ)
    owner = jnp.arange(owners)[None, :, None]
    genes = orders // SHARE * LQ + owner * SHARE + orders % SHARE
    return genes.reshape(CELLS, L).astype(jnp.int32)


def block_scale(key, shape, cuts, low, high):
    loudness, own = 1.0, jax.random.fold_in(key, 6)
    for position, blocks in cuts:
        draws = jnp.exp(jax.random.uniform(jax.random.fold_in(own, position), (blocks,), jnp.float32, low / len(cuts), high / len(cuts)))
        loudness = loudness * jnp.repeat(draws, shape[position] // blocks).reshape([-1 if axis == position else 1 for axis in range(len(shape))])
    return loudness


def noise(stream_key, extent, scale, limit, cuts=(), kind=jnp.bfloat16):
    array = scale * jax.random.normal(stream_key, extent, jnp.float32)
    if cuts:
        array = array * block_scale(stream_key, extent, cuts, -0.22, 0.18)
    return jnp.clip(array, -limit, limit).astype(kind)


def setup_inputs(seed: int = 0) -> dict:
    keys = jax.random.split(jax.random.key(seed), 13)
    return {
        "tokens": noise(keys[0], (CELLS, L, D), 1.0, 6.0, ((0, 8), (1, 4))),
        "valid_len": draw_valid_len(jax.random.fold_in(keys[12], 71), 0),
        "library": draw_library(jax.random.fold_in(keys[12], 71), 0),
        "gene_slot": draw_gene_slot(jax.random.fold_in(keys[12], 71), 0),
        "counts": draw_counts(jax.random.fold_in(keys[12], 71), 0),
        "norm1_gain": jnp.clip(1.0 + 0.1 * jax.random.normal(keys[5], (D,), jnp.float32), 0.5, 1.5),
        "w_qkv": noise(keys[6], (D, 3 * D), D ** -0.5, 0.375),
        "w_out": noise(keys[7], (D, D), (D // 16) ** -0.5, 1.5),
        "norm2_gain": jnp.clip(1.0 + 0.1 * jax.random.normal(keys[8], (D,), jnp.float32), 0.5, 1.5),
        "w_up": noise(keys[9], (D, FF), D ** -0.5, 0.375),
        "w_down": noise(keys[10], (FF, D), FF ** -0.5, 0.1875),
        "w_decoder": noise(keys[11], (3, D), D ** -0.5, 0.375),
    }


@jax.custom_vjp
def low(v):
    return lax.optimization_barrier(v.astype(jnp.bfloat16)).astype(jnp.float32)

@jax.custom_vjp
def low_back(v):
    return v

def low_keep(v):
    return (low(v), None)

def low_pass(kept, grad):
    return (grad,)

def back_keep(v):
    return (v, None)

def back_low(kept, grad):
    return (low(grad),)
low.defvjp(low_keep, low_pass)
low_back.defvjp(back_keep, back_low)
EPS = 1e-05
HIGH_PRECISION = lax.Precision.HIGHEST

def layer_norm(hidden, gain):
    centre = lax.optimization_barrier(jnp.mean(hidden, axis=-1, keepdims=True))
    centred = hidden - centre
    spread = lax.optimization_barrier(jnp.mean(centred * centred, axis=-1, keepdims=True))
    return centred * lax.rsqrt(spread + EPS) * gain

def zinb_nll(decoder_output, observed, scale):
    mean_raw = decoder_output[..., 0]
    disp_raw = decoder_output[..., 1]
    drop_raw = decoder_output[..., 2]
    rate = scale * (jax.nn.softplus(mean_raw) + 0.05)
    theta = jax.nn.softplus(disp_raw) + 0.05
    log_total = jnp.log(theta + rate)
    log_zero_nb = theta * (jnp.log(theta) - log_total)
    dropout = jax.nn.sigmoid(drop_raw)
    zero_case = -jnp.log(dropout + (1.0 - dropout) * jnp.exp(log_zero_nb))
    observed_f = observed.astype(jnp.float32)
    log_nb = lax.lgamma(observed_f + theta) - lax.lgamma(theta) - lax.lgamma(observed_f + 1.0) + log_zero_nb + observed_f * (jnp.log(rate) - log_total)
    nonzero_case = jax.nn.softplus(drop_raw) - log_nb
    return jnp.where(observed > 0, nonzero_case, zero_case)

def forward(source, gain_one, w_qkv, w_out, gain_two, w_up, w_down, w_decoder, valid_len, observed, scale):
    group, length, width = source.shape
    head_dim = width // HEADS
    keep = jnp.arange(length)[None, :] < valid_len[:, None]
    normed = low(layer_norm(source, gain_one))
    mixed = low_back(low(jnp.einsum('gld,de->gle', normed, w_qkv, precision=HIGH_PRECISION)))
    query = mixed[..., :width].reshape(group, length, HEADS, head_dim)
    key_rows = mixed[..., width:2 * width].reshape(group, length, HEADS, head_dim)
    value_rows = mixed[..., 2 * width:].reshape(group, length, HEADS, head_dim)
    scores = low_back(jnp.einsum('gqhd,gkhd->ghqk', query, key_rows, precision=HIGH_PRECISION)) * head_dim ** (-0.5)
    scores = jnp.where(keep[:, None, None, :], scores, -1e+30)
    attention = jax.nn.softmax(scores, axis=-1)
    attended = jnp.einsum('ghqk,gkhd->gqhd', attention, value_rows, precision=HIGH_PRECISION).reshape(group, length, width)
    attended = low_back(low(attended))
    attn_out = low_back(jnp.einsum('gld,de->gle', attended, w_out, precision=HIGH_PRECISION))
    resid = source + attn_out
    normed_two = low(layer_norm(resid, gain_two))
    up = low_back(jnp.einsum('gld,df->glf', normed_two, w_up, precision=HIGH_PRECISION))
    act = low(jax.nn.gelu(up, approximate=False))
    mlp_out = low_back(jnp.einsum('glf,fd->gld', act, w_down, precision=HIGH_PRECISION))
    final = resid + mlp_out
    decoder_input = low_back(low(final))
    decoder_output = jnp.einsum('gld,kd->glk', decoder_input, w_decoder, precision=HIGH_PRECISION)
    nll = zinb_nll(decoder_output, observed, scale[:, None])
    valid = keep.astype(jnp.float32)
    total = jnp.sum(valid * nll)
    stats = jnp.stack([total, jnp.sum(valid), jnp.sum(valid[..., None] * final * final), jnp.sum(valid[..., None] * attn_out * attn_out), jnp.sum(valid[..., None] * mlp_out * mlp_out)])
    return (total, stats)

def reference(tokens, valid_len, library, gene_slot, counts, norm1_gain, w_qkv, w_out, norm2_gain, w_up, w_down, w_decoder):
    cell_total, length, width = tokens.shape
    observed = jnp.take_along_axis(counts, gene_slot.astype(jnp.int32), axis=1)
    scale = library.astype(jnp.float32) / length
    params = tuple((p.astype(jnp.float32) for p in (norm1_gain, w_qkv, w_out, norm2_gain, w_up, w_down, w_decoder)))
    steps_count = cell_total // CELL_DEV
    blocks = (tokens.astype(jnp.float32).reshape(steps_count, CELL_DEV, length, width), valid_len.reshape(steps_count, CELL_DEV), observed.reshape(steps_count, CELL_DEV, length), scale.reshape(steps_count, CELL_DEV))

    def step(carry, block):
        source, active_rows, observed_rows, scale_rows = block

        def objective(source, *weight_params):
            return forward(source, *weight_params, active_rows, observed_rows, scale_rows)
        total, pullback, stats = jax.vjp(objective, source, *params, has_aux=True)
        grads = pullback(jnp.ones_like(total))
        summed = tuple((c + g for c, g in zip(carry, tuple(grads[1:]) + (stats,))))
        return (summed, grads[0])
    init = tuple((jnp.zeros_like(p) for p in params)) + (jnp.zeros((5,), jnp.float32),)
    summed, grad_source = lax.scan(step, init, blocks)
    stats = summed[7]
    loss = stats[0] / stats[1]
    rms_final = jnp.sqrt(stats[2] / (stats[1] * width))
    rms_attn = jnp.sqrt(stats[3] / (stats[1] * width))
    rms_mlp = jnp.sqrt(stats[4] / (stats[1] * width))
    summary = jnp.stack([loss, rms_final, rms_attn, rms_mlp])
    return (grad_source.reshape(cell_total, length, width), summed[0], summed[1], summed[2], summed[3], summed[4], summed[5], summed[6], summary)
```

```python
import functools
import math

import jax
import jax.numpy as jnp
from jax import lax
from jax.experimental import pallas as pl
from jax.experimental.pallas import tpu as pltpu
from jax.sharding import PartitionSpec as P

HEADS = 4
EPS = 1e-05
BF16 = jnp.bfloat16
F32 = jnp.float32
NN = (((1,), (0,)), ((), ()))
NT = (((1,), (1,)), ((), ()))
TN = (((0,), (0,)), ((), ()))
VMEM_LIMIT = 56 * 2**20
SCORE_BOUND = 60.0
ERFC_P = 0.325
ERFC_C = (
    -5.927487965082223e-05,
    0.18467549445148965,
    0.1708094188150158,
    0.2414269376514742,
    -0.07282782022580145,
    0.6147421737182138,
    -0.5684607599983035,
    0.5878333184067656,
    -0.15813953377061551,
)


def dot(a, b, dims):
    return lax.dot_general(a, b, dims, preferred_element_type=F32)


def call(kernel, out_shape, flops=0, moved=0, **kw):
    return pl.pallas_call(
        kernel,
        out_shape=out_shape,
        compiler_params=pltpu.CompilerParams(vmem_limit_bytes=VMEM_LIMIT),
        cost_estimate=pl.CostEstimate(flops=int(flops), bytes_accessed=int(moved), transcendentals=0),
        **kw,
    )


def sds(shape, dtype):
    return jax.ShapeDtypeStruct(shape, dtype)


def norm_parts(x):
    centred = x - jnp.mean(x, axis=-1, keepdims=True)
    rstd = lax.rsqrt(jnp.mean(centred * centred, axis=-1, keepdims=True) + EPS)
    return centred * rstd, rstd


def norm_back(gy, xhat, rstd, gain):
    gx = gy * gain
    first = jnp.mean(gx, axis=-1, keepdims=True)
    second = jnp.mean(gx * xhat, axis=-1, keepdims=True)
    return rstd * (gx - first - xhat * second)


def head_ones(width):
    rows = lax.broadcasted_iota(jnp.int32, (width, width), 0) // (width // HEADS)
    cols = lax.broadcasted_iota(jnp.int32, (width, width), 1) // (width // HEADS)
    return (rows == cols).astype(BF16)


def qkv_kernel(info_ref, x_ref, gain_ref, w_ref, n_ref, q_ref, k_ref, v_ref, top_ref):
    block, width = x_ref.shape
    i = pl.program_id(0)
    xhat, _ = norm_parts(x_ref[...].astype(F32))
    normed = (xhat * gain_ref[...]).astype(BF16)
    n_ref[...] = normed
    mixed = dot(normed, w_ref[...], NN).astype(BF16)
    place = info_ref[1 + i] + lax.broadcasted_iota(jnp.int32, (block, 1), 0)
    live = (place < info_ref[0]).astype(BF16)
    q = mixed[:, :width] * BF16((width // HEADS) ** -0.5)
    k = mixed[:, width : 2 * width] * live
    q_ref[...] = q
    k_ref[...] = k
    v_ref[...] = mixed[:, 2 * width :] * live
    ones = head_ones(width)
    qq = q.astype(F32)
    kk = k.astype(F32)
    top_ref[...] = jnp.zeros_like(top_ref)
    top_ref[0, 0:1, :] = jnp.max(dot((qq * qq).astype(BF16), ones, NN), axis=0, keepdims=True)
    top_ref[0, 1:2, :] = jnp.max(dot((kk * kk).astype(BF16), ones, NN), axis=0, keepdims=True)


def qkv(info, x, gain, w):
    rows, width = x.shape
    block = rows // 4
    row = pl.BlockSpec((block, width), lambda i: (i, 0))
    whole = lambda a: pl.BlockSpec(a.shape, lambda i: (0, 0))
    return call(
        qkv_kernel,
        [sds((rows, width), BF16)] * 4 + [sds((rows // block, 8, width), F32)],
        flops=6 * rows * width * width,
        moved=10 * rows * width,
        grid=(rows // block,),
        in_specs=[pl.BlockSpec(memory_space=pltpu.SMEM), row, whole(gain), whole(w)],
        out_specs=[row] * 4 + [pl.BlockSpec((1, 8, width), lambda i: (i, 0, 0))],
    )(info, x, gain, w)


def attend_kernel(info_ref, place_ref, q_ref, k_ref, v_ref, top_ref, o_ref, linv_ref, p_ref, va_ref):
    keys = k_ref.shape[0]
    pair = q_ref.shape[1]
    half = pair // 2
    lane = lax.broadcasted_iota(jnp.int32, (1, pair), 1)
    live = place_ref[...] < info_ref[0]

    @pl.when(pl.program_id(1) == 0)
    def _():
        v = v_ref[...]
        mask = jnp.transpose(jnp.broadcast_to(live.astype(F32), (pair, keys))).astype(BF16)
        va_ref[0] = jnp.where(lane < half, v, mask)
        va_ref[1] = jnp.where(lane < half, mask, v)

    q = q_ref[...]
    zero = jnp.zeros_like(q)
    qs = (jnp.where(lane < half, q, zero), jnp.where(lane < half, zero, q))
    top = jnp.max(top_ref[...], axis=0)
    bound = jnp.max(top[0:1] * top[1:2])
    plain = bound * 1.05 < SCORE_BOUND * SCORE_BOUND

    def finish(outs):
        up = jnp.where(lane < half, outs[0], outs[1])
        down = pltpu.roll(jnp.where(lane < half, outs[1], outs[0]), half, 1)
        inverse = 1.0 / down
        o_ref[...] = up * inverse
        linv_ref[...] = inverse

    @pl.when(plain)
    def _():
        outs = []
        for h in range(2):
            p = jnp.exp(dot(qs[h], k_ref[...], NT)).astype(BF16)
            p_ref[h] = p
            outs.append(dot(p, va_ref[h], NN))
        finish(outs)

    @pl.when(jnp.logical_not(plain))
    def _():
        outs = []
        for h in range(2):
            s = jnp.where(live, dot(qs[h], k_ref[...], NT), -1e30)
            p = jnp.exp(s - jnp.max(s, axis=1, keepdims=True)).astype(BF16)
            p_ref[h] = p
            outs.append(dot(p, va_ref[h], NN))
        finish(outs)


def attend(info, place, q, k, v, top, rows, block=256):
    keys, width = k.shape
    pair = 2 * (width // HEADS)
    pairs = HEADS // 2
    qspec = pl.BlockSpec((block, pair), lambda h, i: (i, h))
    kspec = pl.BlockSpec((keys, pair), lambda h, i: (0, h))
    return call(
        attend_kernel,
        [sds((rows, width), F32), sds((rows, width), F32), sds((HEADS, rows, keys), BF16)],
        flops=16 * rows * keys * width,
        moved=2 * HEADS * rows * keys,
        grid=(pairs, rows // block),
        in_specs=[
            pl.BlockSpec(memory_space=pltpu.SMEM),
            pl.BlockSpec((1, keys), lambda h, i: (0, 0)),
            qspec,
            kspec,
            kspec,
            pl.BlockSpec((top.shape[0], 8, pair), lambda h, i: (0, 0, h)),
        ],
        out_specs=[qspec, qspec, pl.BlockSpec((2, block, keys), lambda h, i: (h, i, 0))],
        scratch_shapes=[pltpu.VMEM((2, keys, pair), BF16)],
    )(info, place, q, k, v, top)


def attend_back_kernel(place_ref, info_ref, q_ref, do_ref, dl_ref, delta_ref, linv_ref, k_ref, v_ref, p_ref,
                       dq_ref, dk_ref, dv_ref, ak_ref, av_ref, *, chunk):
    keys, pair = k_ref.shape
    half = pair // 2
    i = pl.program_id(0)
    lane = lax.broadcasted_iota(jnp.int32, (1, pair), 1)

    @pl.when(i == 0)
    def _():
        ak_ref[...] = jnp.zeros_like(ak_ref)
        av_ref[...] = jnp.zeros_like(av_ref)

    q = q_ref[...]
    do = do_ref[...]
    dl = dl_ref[...]
    zero = jnp.zeros_like(do)
    dq = []
    for h in range(2):
        own = (lane < half) if h == 0 else (lane >= half)
        doh = jnp.where(own, do, zero)
        lo = h * half
        delta = delta_ref[:, lo : lo + 1]
        linv = linv_ref[:, lo : lo + 1]
        total = None
        for c in range(keys // chunk):
            cut = slice(c * chunk, (c + 1) * chunk)
            kc = k_ref[cut, :]
            pc = p_ref[h, :, cut]
            dp = dot(doh, v_ref[cut, :], NT)
            ds = (pc.astype(F32) * (dp * linv - delta)).astype(BF16)
            part = dot(ds, kc, NN)
            total = part if total is None else total + part
            av_ref[lo : lo + half, cut] += dot(dl[:, lo : lo + half], pc, TN)
            ak_ref[lo : lo + half, cut] += dot(q[:, lo : lo + half], ds, TN)
        dq.append(total)
    dq_ref[...] = (jnp.where(lane < half, dq[0], dq[1]) * half**-0.5).astype(BF16)

    @pl.when(i == pl.num_programs(0) - 1)
    def _():
        live = place_ref[...] < info_ref[0]
        dk_ref[...] = jnp.where(live, ak_ref[...], 0.0).astype(BF16)
        dv_ref[...] = jnp.where(live, av_ref[...], 0.0).astype(BF16)


def attend_back(which, place, info, q, do, dl, delta, linv, k, v, p, block=512, chunk=512):
    rows = do.shape[0]
    keys, width = k.shape
    pair = 2 * (width // HEADS)
    qspec = pl.BlockSpec((block, pair), lambda i: (i, which))
    kspec = pl.BlockSpec((keys, pair), lambda i: (0, which))
    tspec = pl.BlockSpec((pair, keys), lambda i: (0, 0))
    return call(
        functools.partial(attend_back_kernel, chunk=chunk),
        [sds((rows, pair), BF16), sds((pair, keys), BF16), sds((pair, keys), BF16)],
        flops=16 * rows * keys * width,
        moved=rows * keys * HEADS,
        grid=(rows // block,),
        in_specs=[
            pl.BlockSpec((1, keys), lambda i: (0, 0)),
            pl.BlockSpec(memory_space=pltpu.SMEM),
            qspec,
            qspec,
            qspec,
            qspec,
            qspec,
            kspec,
            kspec,
            pl.BlockSpec((2, block, keys), lambda i: (which, i, 0)),
        ],
        out_specs=[pl.BlockSpec((block, pair), lambda i: (i, 0)), tspec, tspec],
        scratch_shapes=[pltpu.VMEM((pair, keys), F32), pltpu.VMEM((pair, keys), F32)],
    )(place, info, q, do, dl, delta, linv, k, v, p)


def gelu_parts(x):
    z = jnp.abs(x) * math.sqrt(0.5)
    t = 1.0 / (1.0 + ERFC_P * z)
    poly = jnp.full_like(t, ERFC_C[-1])
    for c in ERFC_C[-2::-1]:
        poly = poly * t + c
    bell = jnp.exp(-(z * z))
    tail = 0.5 * poly * bell
    cdf = jnp.where(x >= 0, 1.0 - tail, tail)
    return x * cdf, cdf + x * (bell * (1.0 / math.sqrt(2.0 * math.pi)))


def gamma_parts(x):
    large = x > 16.0
    small = jnp.minimum(x, 16.0)
    w = small * (small + 7.0)
    a, b, c = w + 6.0, w + 10.0, w + 12.0
    log_prod = jnp.log(w * a * (b * c))
    sum_inv = (2.0 * small + 7.0) * (1.0 / w + 1.0 / a + 1.0 / b + 1.0 / c)
    big = jnp.where(large, x, x + 8.0)
    log_big = jnp.log(big)
    inv = 1.0 / big
    inv2 = inv * inv
    lg = (big - 0.5) * log_big - big + 0.5 * math.log(2.0 * math.pi)
    lg = lg + inv * (1.0 / 12.0 - inv2 * (1.0 / 360.0 - inv2 * (1.0 / 1260.0)))
    dg = log_big - 0.5 * inv - inv2 * (1.0 / 12.0 - inv2 * (1.0 / 120.0 - inv2 * (1.0 / 252.0)))
    return jnp.where(large, lg, lg - log_prod), jnp.where(large, dg, dg - sum_inv)


def softplus(x):
    return jnp.maximum(x, 0.0) + jnp.log(1.0 + jnp.exp(-jnp.abs(x)))


def sigmoid(x):
    return 1.0 / (1.0 + jnp.exp(-x))


def zinb(m, t, p, y, scale):
    rate = scale * (softplus(m) + 0.05)
    theta = softplus(t) + 0.05
    total = theta + rate
    inv_total = 1.0 / total
    log_total = jnp.log(total)
    log_theta = jnp.log(theta)
    z0 = theta * (log_theta - log_total)
    pi = sigmoid(p)
    e0 = jnp.exp(z0)
    den = pi + (1.0 - pi) * e0
    inv_den = 1.0 / den
    some = y > 0
    yf = y.astype(F32)
    lg_sum, dg_sum = gamma_parts(yf + theta)
    lg_theta, dg_theta = gamma_parts(theta)
    lg_y, _ = gamma_parts(yf + 1.0)
    log_nb = lg_sum - lg_theta - lg_y + z0 + yf * (jnp.log(rate) - log_total)
    nll = jnp.where(some, softplus(p) - log_nb, -jnp.log(den))
    g_z0 = jnp.where(some, -1.0, -(1.0 - pi) * e0 * inv_den)
    share = theta * inv_total
    g_theta = g_z0 * (log_theta - log_total + 1.0 - share)
    g_theta = g_theta + jnp.where(some, dg_theta - dg_sum + yf * inv_total, 0.0)
    g_rate = jnp.where(some, yf * (inv_total - 1.0 / rate), 0.0) - g_z0 * share
    g_p = jnp.where(some, pi, -(1.0 - e0) * inv_den * pi * (1.0 - pi))
    return nll, g_rate * scale * sigmoid(m), g_theta * sigmoid(t), g_p


def split2(x):
    high = x.astype(BF16)
    return high, (x - high.astype(F32)).astype(BF16)


def middle_kernel(info_ref, scale_ref, o_ref, linv_ref, x_ref, gain_ref, w_out_ref, w_up_ref, w_down_ref,
                  w_dec_ref, gene_ref, table_ref,
                  gres_ref, do_ref, dl_ref, delta_ref, g_down_ref, g_up_ref, g_out_ref, small_ref,
                  res_s, n2_s, act_s, gp_s, dec_s, gd_s, ga_down, ga_up, ga_out, *, block):
    rows, width = o_ref.shape
    hidden = w_up_ref.shape[1]
    length = rows // 2
    valid_len = info_ref[0]
    gain = gain_ref[...]
    small_ref[...] = jnp.zeros_like(small_ref)
    ga_down[...] = jnp.zeros_like(ga_down)
    ga_up[...] = jnp.zeros_like(ga_up)
    ga_out[...] = jnp.zeros_like(ga_out)

    def rowsum(a):
        return jnp.sum(a, axis=0, keepdims=True)

    for b in range(rows // block):
        cut = slice(b * block, (b + 1) * block)
        base = info_ref[1 + b * block // length] + b * block % length
        valid = (base + lax.broadcasted_iota(jnp.int32, (block, 1), 0) < valid_len).astype(F32)
        attn_out = dot(o_ref[cut].astype(BF16), w_out_ref[...], NN)
        resid = x_ref[cut].astype(F32) + attn_out
        res_s[cut] = resid
        xhat, _ = norm_parts(resid)
        normed = (xhat * gain).astype(BF16)
        n2_s[cut] = normed
        act, slope = gelu_parts(dot(normed, w_up_ref[...], NN))
        act = act.astype(BF16)
        act_s[cut] = act
        gp_s[cut] = slope
        mlp_out = dot(act, w_down_ref[...], NN)
        final = resid + mlp_out
        dec_s[cut] = final.astype(BF16)
        small_ref[0:1, :] += rowsum(valid * final * final)
        small_ref[1:2, :] += rowsum(valid * attn_out * attn_out)
        small_ref[2:3, :] += rowsum(valid * mlp_out * mlp_out)

    decoded = dot(w_dec_ref[...], dec_s[...], NT)
    gene = gene_ref[...]
    high = (lax.broadcasted_iota(jnp.int32, (table_ref.shape[0], rows), 0) == gene // 128).astype(BF16)
    found = dot(table_ref[...], high, TN)
    low = lax.broadcasted_iota(jnp.int32, (128, rows), 0) == gene % 128
    observed = rowsum(jnp.where(low, found, 0.0))
    places = lax.broadcasted_iota(jnp.int32, (1, rows), 1)
    places = jnp.where(places < length, info_ref[1] + places, info_ref[2] + places - length)
    valid = (places < valid_len).astype(F32)
    nll, g_m, g_t, g_p = zinb(decoded[0:1], decoded[1:2], decoded[2:3], observed, scale_ref[0])
    nll = nll * valid
    for j in range(rows // width):
        small_ref[3:4, :] += nll[:, j * width : (j + 1) * width]
        small_ref[4:5, :] += valid[:, j * width : (j + 1) * width]
    gd_s[...] = jnp.zeros_like(gd_s)
    for j, g in enumerate((g_m, g_t, g_p)):
        gh, gl = split2(g * valid)
        gd_s[j : j + 1, :] = gh.astype(F32)
        gd_s[3 + j : 4 + j, :] = gl.astype(F32)
    gd = gd_s[...].astype(BF16)
    gw = dot(gd, dec_s[...], NN)
    small_ref[5:8, :] = gw[0:3] + gw[3:6]
    w_dec = w_dec_ref[...].astype(F32)
    w_twice = jnp.concatenate([w_dec[0:3], w_dec[0:3], jnp.zeros((10, width), F32)], axis=0).astype(BF16)

    ones = head_ones(width)
    for b in range(rows // block):
        cut = slice(b * block, (b + 1) * block)
        g_final = dot(gd[:, cut], w_twice, TN).astype(BF16)
        ga_down[...] += dot(act_s[cut], g_final, TN)
        g_up = (dot(g_final, w_down_ref[...], NT) * gp_s[cut]).astype(BF16)
        ga_up[...] += dot(n2_s[cut], g_up, TN)
        g_normed = dot(g_up, w_up_ref[...], NT)
        xhat, rstd = norm_parts(res_s[cut])
        small_ref[8:9, :] += rowsum(g_normed * xhat)
        g_res = g_final.astype(F32) + norm_back(g_normed, xhat, rstd, gain)
        gres_ref[cut] = g_res
        g_attn = g_res.astype(BF16)
        o = o_ref[cut]
        linv = linv_ref[cut]
        ga_out[...] += dot(o.astype(BF16), g_attn, TN)
        do = dot(g_attn, w_out_ref[...], NT).astype(BF16)
        do_ref[cut] = do
        dof = do.astype(F32)
        dl_ref[cut] = (dof * linv).astype(BF16)
        ph, pl_ = split2(dof * o)
        delta_ref[cut] = (dot(ph, ones, NN) + dot(pl_, ones, NN)) * linv

    g_down_ref[...] = ga_down[...].astype(BF16)
    for j in range(hidden // width):
        g_up_ref[j * width : (j + 1) * width, :] = ga_up[:, j * width : (j + 1) * width].astype(BF16)
    g_out_ref[...] = ga_out[...].astype(BF16)


def middle(info, scale, o, linv, x, gain, w_out, w_up, w_down, w_dec, gene, table, block=256):
    rows, width = o.shape
    hidden = w_up.shape[1]
    smem = pl.BlockSpec(memory_space=pltpu.SMEM)
    vmem = pl.BlockSpec(memory_space=pltpu.VMEM)
    return call(
        functools.partial(middle_kernel, block=block),
        [
            sds((rows, width), F32),
            sds((rows, width), BF16),
            sds((rows, width), BF16),
            sds((rows, width), F32),
            sds((hidden, width), BF16),
            sds((hidden, width), BF16),
            sds((width, width), BF16),
            sds((16, width), F32),
        ],
        flops=12 * rows * width * hidden,
        moved=20 * rows * width,
        in_specs=[smem, smem] + [vmem] * 10,
        out_specs=[vmem] * 8,
        scratch_shapes=[
            pltpu.VMEM((rows, width), F32),
            pltpu.VMEM((rows, width), BF16),
            pltpu.VMEM((rows, hidden), BF16),
            pltpu.VMEM((rows, hidden), F32),
            pltpu.VMEM((rows, width), BF16),
            pltpu.VMEM((16, rows), F32),
            pltpu.VMEM((hidden, width), F32),
            pltpu.VMEM((width, hidden), F32),
            pltpu.VMEM((width, width), F32),
        ],
    )(info, scale, o, linv, x, gain, w_out, w_up, w_down, w_dec, gene, table)


def last_kernel(x_ref, n_ref, gain_ref, w_ref, dq0_ref, dq1_ref, dk0_ref, dk1_ref, dv0_ref, dv1_ref,
                g_ref, gain_out_ref, own_ref, send_ref, *, block):
    keys, width = x_ref.shape
    rows = dq0_ref.shape[0]
    pair = dq0_ref.shape[1]
    n_own = n_ref[:rows]
    n_all = n_ref[...]
    for j, (dq, dk, dv) in enumerate(((dq0_ref, dk0_ref, dv0_ref), (dq1_ref, dk1_ref, dv1_ref))):
        cut = slice(j * pair, (j + 1) * pair)
        g_ref[0:width, cut] = dot(n_own, dq[...], TN).astype(BF16)
        g_ref[width : 2 * width, cut] = jnp.transpose(dot(dk[...], n_all, NN)).astype(BF16)
        g_ref[2 * width :, cut] = jnp.transpose(dot(dv[...], n_all, NN)).astype(BF16)
    total = jnp.zeros((1, width), F32)
    w = w_ref[...]
    for b in range(keys // block):
        cut = slice(b * block, (b + 1) * block)
        gn = jnp.zeros((block, width), F32)
        for j, (dq, dk, dv) in enumerate(((dq0_ref, dk0_ref, dv0_ref), (dq1_ref, dk1_ref, dv1_ref))):
            lo = j * pair
            if b * block < rows:
                gn += dot(dq[cut], w[:, lo : lo + pair], NT)
            tt = (((0,), (1,)), ((), ()))
            gn += dot(dk[:, cut], w[:, width + lo : width + lo + pair], tt)
            gn += dot(dv[:, cut], w[:, 2 * width + lo : 2 * width + lo + pair], tt)
        xhat, _ = norm_parts(x_ref[cut].astype(F32))
        total += jnp.sum(gn * xhat, axis=0, keepdims=True)
        if b * block < rows:
            own_ref[cut] = gn
        else:
            send_ref[b * block - rows : (b + 1) * block - rows] = gn.astype(BF16)
    gain_out_ref[...] = jnp.broadcast_to(total, gain_out_ref.shape)


def last(x, n, gain, w, dq, dk, dv, block=512):
    keys, width = x.shape
    rows = dq[0].shape[0]
    vmem = pl.BlockSpec(memory_space=pltpu.VMEM)
    return call(
        functools.partial(last_kernel, block=block),
        [sds((3 * width, width), BF16), sds((8, width), F32), sds((rows, width), F32), sds((keys - rows, width), BF16)],
        flops=12 * keys * width * width,
        moved=16 * keys * width,
        in_specs=[vmem] * 10,
        out_specs=[vmem] * 4,
    )(x, n, gain, w, dq[0], dq[1], dk[0], dk[1], dv[0], dv[1])


def tokens_kernel(x_ref, gain_ref, gres_ref, own_ref, got_ref, mine_ref, back_ref):
    length = mine_ref.shape[0]
    for b in range(2):
        cut = slice(b * length, (b + 1) * length)
        xhat, rstd = norm_parts(x_ref[cut].astype(F32))
        gn = own_ref[cut] + got_ref[cut].astype(F32)
        g = gres_ref[cut] + norm_back(gn, xhat, rstd, gain_ref[...])
        if b == 0:
            mine_ref[...] = g
        else:
            back_ref[...] = g.astype(BF16)


def tokens_back(x, gain, gres, own, got):
    rows, width = gres.shape
    vmem = pl.BlockSpec(memory_space=pltpu.VMEM)
    return call(
        tokens_kernel,
        [sds((rows // 2, width), F32), sds((rows // 2, width), BF16)],
        flops=30 * rows * width,
        moved=12 * rows * width,
        in_specs=[vmem] * 5,
        out_specs=[vmem] * 2,
    )(x, gain, gres, own, got)


def swap(x, axis, bit):
    size = lax.axis_size(axis)
    return lax.ppermute(x, axis, [(i, i ^ bit) for i in range(size)])


def split3(x):
    high = lax.reduce_precision(x, 8, 7)
    rest = x - high
    mid = lax.reduce_precision(rest, 8, 7)
    return jnp.concatenate([high, mid, rest - mid], axis=0).astype(BF16)


def join3(x):
    n = x.shape[0] // 3
    x = x.astype(F32)
    return x[:n] + x[n : 2 * n] + x[2 * n :]


def total_over_devices(main, small):
    steps = []
    for axis in ("slots", "cells"):
        bit = 1
        while bit < lax.axis_size(axis):
            steps.append((axis, bit))
            bit *= 2
    halving, rest = steps[:1] + steps[2:3], steps[1:2] + steps[3:]
    for axis, bit in halving:
        side = (lax.axis_index(axis) // bit) % 2
        n = main.shape[0] // 2
        keep = lax.dynamic_slice_in_dim(main, side * n, n, 0)
        send = lax.dynamic_slice_in_dim(main, (1 - side) * n, n, 0)
        got = swap(jnp.concatenate([send, split3(small)], axis=0), axis, bit)
        main = (keep.astype(F32) + got[:n].astype(F32)).astype(BF16)
        small = small + join3(got[n:])
    for axis, bit in rest:
        n = main.shape[0]
        got = swap(jnp.concatenate([main, split3(small)], axis=0), axis, bit)
        main = (main.astype(F32) + got[:n].astype(F32)).astype(BF16)
        small = small + join3(got[n:])
    for axis, bit in halving[::-1]:
        side = (lax.axis_index(axis) // bit) % 2
        got = swap(main, axis, bit)
        main = jnp.where(side == 0, jnp.concatenate([main, got], 0), jnp.concatenate([got, main], 0))
    return main, small


def per_device(
    tokens,
    valid_len,
    library,
    gene_slot,
    counts,
    norm1_gain,
    w_qkv,
    w_out,
    norm2_gain,
    w_up,
    w_down,
    w_decoder,
):
    cells, length, width = tokens.shape
    hidden = w_up.shape[1]
    slots = lax.axis_size("slots")
    me = lax.axis_index("slots")
    cell = me // 2
    pick = lambda a: lax.dynamic_index_in_dim(a, cell, 0, keepdims=False)
    other = lambda a: lax.dynamic_index_in_dim(a, 1 - cell, 0, keepdims=False)

    came = swap(other(tokens), "slots", 2)
    own = jnp.concatenate([pick(tokens), came], axis=0)
    x = jnp.concatenate([own, swap(own, "slots", 1)], axis=0)
    came_counts = swap(other(counts), "slots", 2)
    two = jnp.stack([pick(counts), came_counts])
    two_more = swap(two, "slots", 1)
    table = jnp.stack([two[0], two_more[0], two[1], two_more[1]]).reshape(-1, 128).astype(BF16)

    blocks = jnp.stack([me, me ^ 2, me ^ 1, me ^ 3]).astype(jnp.int32)
    info = jnp.concatenate([pick(valid_len)[None], blocks * length])
    place = (blocks[:, None] * length + jnp.arange(length, dtype=jnp.int32)[None]).reshape(1, -1)
    scale = (pick(library).astype(F32) / (slots * length))[None]
    gene = pick(gene_slot).reshape(slots, length)
    gene = jnp.stack([lax.dynamic_index_in_dim(gene, b, 0, keepdims=False) for b in (me, me ^ 2)])
    gene = (((gene // length) ^ me) * length + gene % length).reshape(1, -1)

    gain1 = norm1_gain[None]
    gain2 = norm2_gain[None]
    w_dec = jnp.concatenate([w_decoder, jnp.zeros((13, width), BF16)], axis=0)

    rows = 2 * length
    n, q, k, v, top = qkv(info, x, gain1, w_qkv)
    o, linv, p = attend(info, place, q, k, v, top, rows)
    gres, do, dl, delta, g_down, g_up, g_out, small = middle(
        info, scale, o, linv, x, gain2, w_out, w_up, w_down, w_dec, gene, table
    )
    back = [attend_back(h, place, info, q, do, dl, delta, linv, k, v, p) for h in range(HEADS // 2)]
    g_qkv, g_gain1, gn_own, gn_send = last(
        x, n, gain1, w_qkv, [b[0] for b in back], [b[1] for b in back], [b[2] for b in back]
    )
    gn_got = swap(gn_send, "slots", 1)
    mine, away = tokens_back(x, gain1, gres, gn_own, gn_got)
    returned = swap(away, "slots", 2).astype(F32)
    grad_tokens = jnp.where(cell == 0, jnp.stack([mine, returned]), jnp.stack([returned, mine]))

    main = jnp.concatenate([g_down, g_up, g_out, g_qkv], axis=0)
    small = jnp.concatenate([small[:9], g_gain1[:1]], axis=0)
    main, small = total_over_devices(main, small)
    main = main.astype(F32)
    at = 0
    parts = []
    for size in (hidden, hidden, width, 3 * width):
        parts.append(main[at : at + size])
        at += size
    unstack = lambda a: jnp.concatenate(list(a.reshape(-1, width, width)), axis=1)
    sums = jnp.sum(small, axis=1)
    count = sums[4]
    summary = jnp.stack(
        [
            sums[3] / count,
            jnp.sqrt(sums[0] / (count * width)),
            jnp.sqrt(sums[1] / (count * width)),
            jnp.sqrt(sums[2] / (count * width)),
        ]
    )
    return (
        grad_tokens,
        small[9],
        unstack(parts[3]),
        parts[2],
        small[8],
        unstack(parts[1]),
        parts[0],
        small[5:8],
        summary,
    )


def solution(mesh):
    in_specs = (
        P("cells", "slots", None),
        P("cells"),
        P("cells"),
        P("cells", None),
        P("cells", "slots"),
        P(),
        P(),
        P(),
        P(),
        P(),
        P(),
        P(),
    )
    out_specs = (P("cells", "slots", None), P(), P(), P(), P(), P(), P(), P(), P())
    return jax.shard_map(
        per_device, mesh=mesh, in_specs=in_specs, out_specs=out_specs, check_vma=False
    )
```

```python
import functools
import math

import jax
import jax.numpy as jnp
from jax import lax
from jax.experimental import pallas as pl
from jax.experimental.pallas import tpu as pltpu
from jax.sharding import PartitionSpec as P

HEADS = 4
EPS = 1e-05
BF16 = jnp.bfloat16
F32 = jnp.float32
NN = (((1,), (0,)), ((), ()))
NT = (((1,), (1,)), ((), ()))
TN = (((0,), (0,)), ((), ()))
SCORE_BOUND = 60.0
ERFC_P = 0.325
ERFC_C = (
    -5.927487965082223e-05,
    0.18467549445148965,
    0.1708094188150158,
    0.2414269376514742,
    -0.07282782022580145,
    0.6147421737182138,
    -0.5684607599983035,
    0.5878333184067656,
    -0.15813953377061551,
)


def dot(a, b, dims):
    return lax.dot_general(a, b, dims, preferred_element_type=F32)


def call(kernel, out_shape, flops=0, moved=0, vmem=48, **kw):
    return pl.pallas_call(
        kernel,
        out_shape=out_shape,
        compiler_params=pltpu.CompilerParams(vmem_limit_bytes=vmem * 2**20),
        cost_estimate=pl.CostEstimate(flops=int(flops), bytes_accessed=int(moved), transcendentals=0),
        **kw,
    )


def sds(shape, dtype):
    return jax.ShapeDtypeStruct(shape, dtype)


def norm_parts(x):
    centred = x - jnp.mean(x, axis=-1, keepdims=True)
    rstd = lax.rsqrt(jnp.mean(centred * centred, axis=-1, keepdims=True) + EPS)
    return centred * rstd, rstd


def norm_back(gy, xhat, rstd, gain):
    gx = gy * gain
    first = jnp.mean(gx, axis=-1, keepdims=True)
    second = jnp.mean(gx * xhat, axis=-1, keepdims=True)
    return rstd * (gx - first - xhat * second)


def head_ones(width, lanes=None, step=None):
    rows = lax.broadcasted_iota(jnp.int32, (width, lanes or width), 0) // (width // HEADS)
    cols = lax.broadcasted_iota(jnp.int32, (width, lanes or width), 1) // (step or width // HEADS)
    return (rows == cols).astype(F32).astype(BF16)


def live_rows(me_ref, len_ref, block, length):
    place = (me_ref[0] ^ block) * length + lax.broadcasted_iota(jnp.int32, (length, 1), 0)
    return place < len_ref[me_ref[0] // 2]


def qkv_kernel(me_ref, len_ref, own_ref, pair_ref, gain_ref, w_ref, n_out, q_ref, k_ref, v_ref, top_ref, n_ref, n_sem, *, first):
    length, width = pair_ref.shape
    ones = head_ones(width)
    top_ref[...] = jnp.zeros_like(top_ref)
    for j in range(2):
        cut = slice(j * length, (j + 1) * length)
        if j == 1:
            x = pair_ref[...]
        elif first == 0:
            x = own_ref[me_ref[0] // 2]
        else:
            x = own_ref[...]
        xhat, _ = norm_parts(x.astype(F32))
        normed = (xhat * gain_ref[...]).astype(BF16)
        n_ref[cut] = normed
        live = live_rows(me_ref, len_ref, first + j, length).astype(F32).astype(BF16)
        skip = width if j == 1 else 0
        mixed = dot(normed, w_ref[:, skip:], NN).astype(BF16)
        if j == 0:
            q = mixed[:, :width] * BF16((width // HEADS) ** -0.5)
            q_ref[...] = q
            qf = q.astype(F32)
            top_ref[0:1, :] = jnp.max(dot((qf * qf).astype(BF16), ones, NN), axis=0, keepdims=True)
        k = mixed[:, width - skip : 2 * width - skip] * live
        k_ref[cut] = k
        v_ref[cut] = mixed[:, 2 * width - skip :] * live
        kf = k.astype(F32)
        top_ref[1 + j : 2 + j, :] = jnp.max(dot((kf * kf).astype(BF16), ones, NN), axis=0, keepdims=True)
    keep_n = pltpu.make_async_copy(n_ref, n_out, n_sem)
    keep_n.start()
    if first == 0:
        keep_n.wait()


def qkv(me, valid_len, own, pair, gain, w, first):
    length, width = pair.shape
    smem = pl.BlockSpec(memory_space=pltpu.SMEM)
    vmem = pl.BlockSpec(memory_space=pltpu.VMEM)
    hbm = pl.BlockSpec(memory_space=pltpu.HBM)
    rows = 2 * length
    return call(
        functools.partial(qkv_kernel, first=first),
        [
            pltpu.HBM((rows, width), BF16),
            sds((length, width), BF16),
            sds((rows, width), BF16),
            sds((rows, width), BF16),
            sds((8, width), F32),
        ],
        flops=6 * rows * width * width,
        moved=10 * rows * width,
        vmem=16,
        in_specs=[smem, smem] + [vmem] * 4,
        out_specs=[hbm] + [vmem] * 4,
        scratch_shapes=[pltpu.VMEM((rows, width), BF16), pltpu.SemaphoreType.DMA],
    )(me, valid_len, own, pair, gain, w)


def live_keys(me_ref, len_ref, keys):
    lane = lax.broadcasted_iota(jnp.int32, (1, keys), 1)
    length = keys // 4
    place = ((lane // length) ^ me_ref[0]) * length + lane % length
    return place < len_ref[me_ref[0] // 2]


def gelu_parts(x):
    z = jnp.abs(x) * math.sqrt(0.5)
    t = 1.0 / (1.0 + ERFC_P * z)
    poly = jnp.full_like(t, ERFC_C[-1])
    for c in ERFC_C[-2::-1]:
        poly = poly * t + c
    bell = jnp.exp(-(z * z))
    tail = 0.5 * poly * bell
    cdf = jnp.where(x >= 0, 1.0 - tail, tail)
    return x * cdf, cdf + x * (bell * (1.0 / math.sqrt(2.0 * math.pi)))


def gamma_parts(x):
    large = x > 16.0
    small = jnp.minimum(x, 16.0)
    w = small * (small + 7.0)
    a, b, c = w + 6.0, w + 10.0, w + 12.0
    log_prod = jnp.log(w * a * (b * c))
    sum_inv = (2.0 * small + 7.0) * (1.0 / w + 1.0 / a + 1.0 / b + 1.0 / c)
    big = jnp.where(large, x, x + 8.0)
    log_big = jnp.log(big)
    inv = 1.0 / big
    inv2 = inv * inv
    lg = (big - 0.5) * log_big - big + 0.5 * math.log(2.0 * math.pi)
    lg = lg + inv * (1.0 / 12.0 - inv2 * (1.0 / 360.0 - inv2 * (1.0 / 1260.0)))
    dg = log_big - 0.5 * inv - inv2 * (1.0 / 12.0 - inv2 * (1.0 / 120.0 - inv2 * (1.0 / 252.0)))
    return jnp.where(large, lg, lg - log_prod), jnp.where(large, dg, dg - sum_inv)


def softplus(x):
    return jnp.maximum(x, 0.0) + jnp.log(1.0 + jnp.exp(-jnp.abs(x)))


def sigmoid(x):
    return 1.0 / (1.0 + jnp.exp(-x))


def zinb(m, t, p, y, scale):
    rate = scale * (softplus(m) + 0.05)
    theta = softplus(t) + 0.05
    total = theta + rate
    inv_total = 1.0 / total
    log_total = jnp.log(total)
    log_theta = jnp.log(theta)
    z0 = theta * (log_theta - log_total)
    pi = sigmoid(p)
    e0 = jnp.exp(z0)
    den = pi + (1.0 - pi) * e0
    inv_den = 1.0 / den
    some = y > 0
    yf = y.astype(F32)
    lg_sum, dg_sum = gamma_parts(yf + theta)
    lg_theta, dg_theta = gamma_parts(theta)
    lg_y, _ = gamma_parts(yf + 1.0)
    log_nb = lg_sum - lg_theta - lg_y + z0 + yf * (jnp.log(rate) - log_total)
    nll = jnp.where(some, softplus(p) - log_nb, -jnp.log(den))
    g_z0 = jnp.where(some, -1.0, -(1.0 - pi) * e0 * inv_den)
    share = theta * inv_total
    g_theta = g_z0 * (log_theta - log_total + 1.0 - share)
    g_theta = g_theta + jnp.where(some, dg_theta - dg_sum + yf * inv_total, 0.0)
    g_rate = jnp.where(some, yf * (inv_total - 1.0 / rate), 0.0) - g_z0 * share
    g_p = jnp.where(some, pi, -(1.0 - e0) * inv_den * pi * (1.0 - pi))
    return nll, g_rate * scale * sigmoid(m), g_theta * sigmoid(t), g_p


def split2(x):
    high = x.astype(BF16)
    return high, (x - high.astype(F32)).astype(BF16)


def layer_kernel(me_ref, len_ref, lib_ref, xa_ref, xb_ref, pb_ref, gain1_ref, w_ref, qa_ref, ka_ref, va_ref, ta_ref,
                 gain_ref, w_out_ref, w_up_ref, w_down_ref, w_dec_ref, gene_ref, c0_ref, c1_ref, c2_ref, c3_ref,
                 p_ref, nb_ref, gres_out, keep_out, qb_ref, kb_ref, vb_ref, tb_ref, do_ref, dl_ref, cols_ref, send_ref,
                 small_ref,
                 nb_s, nb_sem, gres_ref, keep_ref, out_sem, q_s, x_s, p_s, p_sem, gt_s, aug_s, o_s, linv_s, res_s, n2_s, act_s, gp_s, dec_s, gd_s, w_s, table_s, ga_down, ga_up, ga_out,
                 *, block):
    part, width = ka_ref.shape
    keys = 2 * part
    length = part // 2
    rows = part
    hidden = w_up_ref.shape[1]
    pair = 2 * (width // HEADS)
    half = pair // 2
    pairs = HEADS // 2
    me = me_ref[0]
    cell = me // 2
    valid_len = len_ref[cell]
    gain = gain_ref[...]
    small_ref[...] = jnp.zeros_like(small_ref)
    ga_down[...] = jnp.zeros_like(ga_down)
    ga_up[...] = jnp.zeros_like(ga_up)
    ga_out[...] = jnp.zeros_like(ga_out)
    lane = lax.broadcasted_iota(jnp.int32, (1, pair), 1)

    def rowsum(a):
        return jnp.sum(a, axis=0, keepdims=True)

    qkv_kernel(me_ref, len_ref, xb_ref, pb_ref, gain1_ref, w_ref, nb_ref, qb_ref, kb_ref, vb_ref, tb_ref, nb_s, nb_sem, first=2)

    live = live_keys(me_ref, len_ref, keys)
    mask = jnp.transpose(jnp.broadcast_to(live.astype(F32), (pair, keys))).astype(BF16)
    for j, ref in enumerate((va_ref, vb_ref)):
        cut = slice(j * part, (j + 1) * part)
        for g in range(pairs):
            v = ref[:, g * pair : (g + 1) * pair]
            aug_s[2 * g, cut] = jnp.where(lane < half, v, mask[cut])
            aug_s[2 * g + 1, cut] = jnp.where(lane < half, mask[cut], v)

    top_q = jnp.maximum(ta_ref[0:1], tb_ref[0:1])
    top_k = jnp.maximum(jnp.maximum(ta_ref[1:2], tb_ref[1:2]), jnp.maximum(ta_ref[2:3], tb_ref[2:3]))
    plain = jnp.max(top_q * top_k) * 1.05 < SCORE_BOUND * SCORE_BOUND

    q_s[0:length] = qa_ref[...]
    q_s[length:rows] = qb_ref[...]
    x_s[0:length] = xa_ref[cell]
    x_s[length:rows] = xb_ref[...]

    def copy(b, g):
        slot = (b * pairs + g) % 2
        return pltpu.make_async_copy(
            p_s.at[slot], p_ref.at[pl.ds(2 * g, 2), pl.ds(pl.multiple_of(b * block, block), block)], p_sem.at[slot]
        )

    def attend_block(b, g, safe):
        cut = pl.ds(pl.multiple_of(b * block, block), block)
        cols = slice(g * pair, (g + 1) * pair)
        slot = (b * pairs + g) % 2
        q = q_s[cut, cols]
        zero = jnp.zeros_like(q)
        outs = []
        for h in range(2):
            qh = jnp.where(lane < half, q, zero) if h == 0 else jnp.where(lane < half, zero, q)
            if safe:
                s = jnp.concatenate([dot(qh, ref[:, cols], NT) for ref in (ka_ref, kb_ref)], axis=1)
                s = jnp.where(live, s, -1e30)
                p = jnp.exp(s - jnp.max(s, axis=1, keepdims=True)).astype(BF16)
                p_s[slot, h] = p
                total = dot(p, aug_s[2 * g + h], NN)
            else:
                total = None
                for j, ref in enumerate((ka_ref, kb_ref)):
                    kcut = slice(j * part, (j + 1) * part)
                    p = jnp.exp(dot(qh, ref[:, cols], NT)).astype(BF16)
                    p_s[slot, h, :, kcut] = p
                    o = dot(p, aug_s[2 * g + h, kcut], NN)
                    total = o if total is None else total + o
            outs.append(total)
        up = jnp.where(lane < half, outs[0], outs[1])
        down = pltpu.roll(jnp.where(lane < half, outs[1], outs[0]), half, 1)
        inverse = 1.0 / down
        o_s[cut, cols] = up * inverse
        linv_s[cut, cols] = inverse

    @pl.loop(0, rows // block)
    def _(b):
        for g in range(pairs):

            @pl.when(b > 0)
            def _():
                copy(b - 1, g).wait()

            pl.when(plain)(functools.partial(attend_block, b, g, False))
            pl.when(jnp.logical_not(plain))(functools.partial(attend_block, b, g, True))
            copy(b, g).start()

    @pl.loop(0, rows // block)
    def _(b):
        start = pl.multiple_of(b * block, block)
        cut = pl.ds(start, block)
        base = jnp.where(start < length, me * length + start, (me ^ 2) * length + start - length)
        valid = (base + lax.broadcasted_iota(jnp.int32, (block, 1), 0) < valid_len).astype(F32)
        attn_out = dot(o_s[cut].astype(BF16), w_out_ref[...], NN)
        resid = x_s[cut].astype(F32) + attn_out
        res_s[cut] = resid
        xhat, _ = norm_parts(resid)
        normed = (xhat * gain).astype(BF16)
        n2_s[cut] = normed
        act, slope = gelu_parts(dot(normed, w_up_ref[...], NN))
        act = act.astype(BF16)
        act_s[cut] = act
        gp_s[cut] = slope
        mlp_out = dot(act, w_down_ref[...], NN)
        final = resid + mlp_out
        dec_s[cut] = final.astype(BF16)
        small_ref[0:1, :] += rowsum(valid * final * final)
        small_ref[1:2, :] += rowsum(valid * attn_out * attn_out)
        small_ref[2:3, :] += rowsum(valid * mlp_out * mlp_out)

    w_s[...] = jnp.zeros_like(w_s)
    w_s[0:3, :] = w_dec_ref[...].astype(F32)
    w_s[3:6, :] = w_dec_ref[...].astype(F32)
    w_twice = w_s[...].astype(BF16)
    decoded = dot(w_twice, dec_s[...], NT)
    for j, ref in enumerate((c0_ref, c1_ref, c2_ref, c3_ref)):
        for i in range(length // 128):
            table_s[j * (length // 128) + i : j * (length // 128) + i + 1, :] = ref[:, i * 128 : (i + 1) * 128].astype(F32)
    starts = (me * length, (me ^ 2) * length)
    gene = jnp.concatenate([gene_ref[pl.ds(cell, 1), pl.ds(pl.multiple_of(a, length), length)] for a in starts], axis=1)
    gene = ((gene // length) ^ me) * length + gene % length
    high = (lax.broadcasted_iota(jnp.int32, (table_s.shape[0], rows), 0) == gene // 128).astype(F32).astype(BF16)
    found = dot(table_s[...].astype(BF16), high, TN)
    low = lax.broadcasted_iota(jnp.int32, (128, rows), 0) == gene % 128
    observed = rowsum(jnp.where(low, found, 0.0))
    lane = lax.broadcasted_iota(jnp.int32, (1, rows), 1)
    places = jnp.where(lane < length, starts[0] + lane, starts[1] + lane - length)
    valid = (places < valid_len).astype(F32)
    scale = lib_ref[cell].astype(F32) / (4 * length)
    nll, g_m, g_t, g_p = zinb(decoded[0:1], decoded[1:2], decoded[2:3], observed, scale)
    nll = nll * valid
    for j in range(rows // width):
        small_ref[3:4, :] += nll[:, j * width : (j + 1) * width]
        small_ref[4:5, :] += valid[:, j * width : (j + 1) * width]
    gd_s[...] = jnp.zeros_like(gd_s)
    for j, g in enumerate((g_m, g_t, g_p)):
        gh, gl = split2(g * valid)
        gd_s[j : j + 1, :] = gh.astype(F32)
        gd_s[3 + j : 4 + j, :] = gl.astype(F32)
    gd = gd_s[...].astype(BF16)
    gw = dot(gd, dec_s[...], NN)
    small_ref[5:8, :] = gw[0:3] + gw[3:6]

    heads = head_ones(width, 128, 1)
    for j in range(rows // block):
        gt_s[j * 16 : (j + 1) * 16] = gd[:, j * block : (j + 1) * block]

    @pl.loop(0, rows // block)
    def _(b):
        cut = pl.ds(pl.multiple_of(b * block, block), block)
        g_final = dot(gt_s[pl.ds(pl.multiple_of(b * 16, 16), 16)], w_twice, TN).astype(BF16)
        ga_down[...] += dot(act_s[cut], g_final, TN)
        g_up = (dot(g_final, w_down_ref[...], NT) * gp_s[cut]).astype(BF16)
        ga_up[...] += dot(n2_s[cut], g_up, TN)
        g_normed = dot(g_up, w_up_ref[...], NT)
        xhat, rstd = norm_parts(res_s[cut])
        small_ref[8:9, :] += rowsum(g_normed * xhat)
        g_res = g_final.astype(F32) + norm_back(g_normed, xhat, rstd, gain)
        gres_ref[cut] = g_res
        g_attn = g_res.astype(BF16)
        o = o_s[cut]
        linv = linv_s[cut]
        ga_out[...] += dot(o.astype(BF16), g_attn, TN)
        do = dot(g_attn, w_out_ref[...], NT).astype(BF16)
        do_ref[cut] = do
        dof = do.astype(F32)
        dl_ref[cut] = (dof * linv).astype(BF16)
        ph, pl_ = split2(dof * o)
        cols_ref[cut, 0:HEADS] = ((dot(ph, heads, NN) + dot(pl_, heads, NN)))[:, 0:HEADS]
        for h in range(HEADS):
            cols_ref[cut, HEADS + h : HEADS + h + 1] = linv[:, h * half : h * half + 1]

    gres_copy = pltpu.make_async_copy(gres_ref, gres_out, out_sem.at[0])
    gres_copy.start()
    for g in range(pairs):
        copy(rows // block - 1, g).wait()
    pltpu.make_async_copy(nb_s, nb_ref, nb_sem).wait()

    def write(low_ref, high_ref):
        pieces = [ga_down[...]]
        pieces += [ga_up[:, j * width : (j + 1) * width] for j in range(hidden // width)]
        pieces += [ga_out[...]]
        at = 0
        half = low_ref.shape[0]
        for piece in pieces:
            n = piece.shape[0]
            first = max(0, min(n, half - at))
            if first:
                low_ref[at : at + first, :] = piece[:first].astype(BF16)
            if first < n:
                high_ref[at + first - half : at + n - half, :] = piece[first:].astype(BF16)
            at += n

    @pl.when(me % 2 == 0)
    def _():
        write(keep_ref, send_ref)

    @pl.when(me % 2 == 1)
    def _():
        write(send_ref, keep_ref)

    keep_copy = pltpu.make_async_copy(keep_ref, keep_out, out_sem.at[1])
    keep_copy.start()
    gres_copy.wait()
    keep_copy.wait()


def layer(me, valid_len, library, xa, xb, pb, gain1, w, qa, ka, va, ta, gain, w_out, w_up, w_down, w_dec, gene, tables, block=256):
    part, width = ka.shape
    rows, keys, length = part, 2 * part, part // 2
    hidden = w_up.shape[1]
    pair = 2 * (width // HEADS)
    smem = pl.BlockSpec(memory_space=pltpu.SMEM)
    vmem = pl.BlockSpec(memory_space=pltpu.VMEM)
    half = (2 * hidden + width) // 2
    return call(
        functools.partial(layer_kernel, block=block),
        [
            pltpu.HBM((HEADS, rows, keys), BF16),
            pltpu.HBM((part, width), BF16),
            pltpu.HBM((rows, width), F32),
            pltpu.HBM((half, width), BF16),
            sds((length, width), BF16),
            sds((part, width), BF16),
            sds((part, width), BF16),
            sds((8, width), F32),
            sds((rows, width), BF16),
            sds((rows, width), BF16),
            sds((rows, 128), F32),
            sds((half, width), BF16),
            sds((16, width), F32),
        ],
        flops=24 * rows * width * hidden + 16 * rows * keys * width,
        vmem=40,
        in_specs=[smem] * 3 + [vmem] * 19,
        out_specs=[pl.BlockSpec(memory_space=pltpu.HBM)] * 4 + [vmem] * 9,
        scratch_shapes=[
            pltpu.VMEM((part, width), BF16),
            pltpu.SemaphoreType.DMA,
            pltpu.VMEM((rows, width), F32),
            pltpu.VMEM((half, width), BF16),
            pltpu.SemaphoreType.DMA((2,)),
            pltpu.VMEM((rows, width), BF16),
            pltpu.VMEM((rows, width), BF16),
            pltpu.VMEM((2, 2, block, keys), BF16),
            pltpu.SemaphoreType.DMA((2,)),
            pltpu.VMEM((16 * rows // block, block), BF16),
            pltpu.VMEM((HEADS, keys, pair), BF16),
            pltpu.VMEM((rows, width), F32),
            pltpu.VMEM((rows, width), F32),
            pltpu.VMEM((rows, width), F32),
            pltpu.VMEM((rows, width), BF16),
            pltpu.VMEM((rows, hidden), BF16),
            pltpu.VMEM((rows, hidden), F32),
            pltpu.VMEM((rows, width), BF16),
            pltpu.VMEM((16, rows), F32),
            pltpu.VMEM((16, width), F32),
            pltpu.VMEM((rows // 64, 128), F32),
            pltpu.VMEM((hidden, width), F32),
            pltpu.VMEM((width, hidden), F32),
            pltpu.VMEM((width, width), F32),
        ],
    )(me, valid_len, library, xa, xb, pb, gain1, w, qa, ka, va, ta, gain, w_out, w_up, w_down, w_dec, gene, *tables)


def attend_back_kernel(me_ref, len_ref, qa_ref, qb_ref, do_ref, dl_ref, cols_ref, ka_ref, kb_ref,
                       va_ref, vb_ref, p_ref, dq_ref, dk_ref, dv_ref, ak_ref, av_ref, p_s, p_sem, *, head, block, chunk):
    part, width = ka_ref.shape
    keys = 2 * part
    rows = do_ref.shape[0]
    length = rows // 2
    half = width // HEADS
    pair = 2 * half
    lane = lax.broadcasted_iota(jnp.int32, (1, pair), 1)
    lo = (head % 2) * half
    own = (lane < half) if head % 2 == 0 else (lane >= half)
    at0 = head // 2 * pair
    cols = slice(at0, at0 + pair)
    mine = slice(at0 + lo, at0 + lo + half)

    def copy(b):
        rcut = pl.ds(b * block, block)
        return pltpu.make_async_copy(p_ref.at[head, rcut], p_s.at[rcut], p_sem.at[b])

    for b in range(rows // block):
        copy(b).start()
    for b in range(rows // block):
        cut = slice(b * block, (b + 1) * block)
        at = b * block % length
        q_ref = qa_ref if b * block < length else qb_ref
        q = q_ref[at : at + block, mine]
        do = do_ref[cut, cols]
        do = jnp.where(own, do, jnp.zeros_like(do))
        dl = dl_ref[cut, mine]
        delta = cols_ref[cut, head : head + 1]
        linv = cols_ref[cut, HEADS + head : HEADS + head + 1]
        total = None
        copy(b).wait()
        for c in range(keys // chunk):
            kcut = slice(c * chunk, (c + 1) * chunk)
            k_ref, v_ref = (ka_ref, va_ref) if c * chunk < part else (kb_ref, vb_ref)
            kat = c * chunk % part
            kc = k_ref[kat : kat + chunk, cols]
            dp = dot(do, v_ref[kat : kat + chunk, cols], NT)
            pc = p_s[cut, kcut]
            ds = (pc.astype(F32) * ((dp - delta) * linv)).astype(BF16)
            step = dot(ds, kc, NN)
            total = step if total is None else total + step
            dv = dot(dl, pc, TN)
            dk = dot(q, ds, TN)
            if b == 0:
                av_ref[:, kcut] = dv
                ak_ref[:, kcut] = dk
            else:
                av_ref[:, kcut] += dv
                ak_ref[:, kcut] += dk
        dq_ref[cut] = (jnp.where(own, total, 0.0) * half**-0.5).astype(BF16)
    live = live_keys(me_ref, len_ref, keys)
    dk_ref[...] = jnp.where(live, ak_ref[...], 0.0).astype(BF16)
    dv_ref[...] = jnp.where(live, av_ref[...], 0.0).astype(BF16)


def attend_back(head, me, valid_len, qa, qb, do, dl, cols, ka, kb, va, vb, p, block=512, chunk=512):
    rows = do.shape[0]
    part, width = ka.shape
    keys = 2 * part
    pair = 2 * (width // HEADS)
    smem = pl.BlockSpec(memory_space=pltpu.SMEM)
    vmem = pl.BlockSpec(memory_space=pltpu.VMEM)
    return call(
        functools.partial(attend_back_kernel, head=head, block=block, chunk=chunk),
        [sds((rows, pair), BF16), sds((pair // 2, keys), BF16), sds((pair // 2, keys), BF16)],
        flops=8 * rows * keys * width,
        moved=2 * rows * keys,
        vmem=46,
        in_specs=[smem, smem] + [vmem] * 9 + [pl.BlockSpec(memory_space=pltpu.HBM)],
        out_specs=[vmem] * 3,
        scratch_shapes=[
            pltpu.VMEM((pair // 2, keys), F32),
            pltpu.VMEM((pair // 2, keys), F32),
            pltpu.VMEM((rows, keys), BF16),
            pltpu.SemaphoreType.DMA((rows // block,)),
        ],
    )(me, valid_len, qa, qb, do, dl, cols, ka, kb, va, vb, p)


def weights_kernel(me_ref, na_ref, nb_ref, *refs):
    keep_ref, send_ref = refs[-2:]
    heads = [refs[3 * h : 3 * h + 3] for h in range(HEADS)]
    part, width = na_ref.shape
    length = part // 2
    dim = width // HEADS
    dq = sum(h[0][...].astype(F32) for h in heads[:2]), sum(h[0][...].astype(F32) for h in heads[2:])
    dq = jnp.concatenate(dq, axis=1).astype(BF16)
    gq = dot(na_ref[:length], dq[:length], TN) + dot(nb_ref[:length], dq[length:], TN)
    outs = [gq]
    for j in (1, 2):
        d = jnp.concatenate([h[j][...] for h in heads], axis=0)
        g = dot(d[:, :part], na_ref[...], NN) + dot(d[:, part:], nb_ref[...], NN)
        outs.append(jnp.transpose(g))
    half = 3 * width // 2

    def write(low_ref, high_ref):
        at = 0
        for piece in outs:
            first = max(0, min(width, half - at))
            if first:
                low_ref[at : at + first, :] = piece[:first].astype(BF16)
            if first < width:
                high_ref[at + first - half : at + width - half, :] = piece[first:].astype(BF16)
            at += width

    @pl.when(me_ref[0] % 2 == 0)
    def _():
        write(keep_ref, send_ref)

    @pl.when(me_ref[0] % 2 == 1)
    def _():
        write(send_ref, keep_ref)


def weights(me, na, nb, back):
    part, width = na.shape
    half = 3 * width // 2
    smem = pl.BlockSpec(memory_space=pltpu.SMEM)
    vmem = pl.BlockSpec(memory_space=pltpu.VMEM)
    return call(
        weights_kernel,
        [sds((half, width), BF16)] * 2,
        vmem=16,
        flops=10 * part * width * width,
        moved=16 * part * width,
        in_specs=[smem] + [vmem] * (2 + 3 * HEADS),
        out_specs=[vmem] * 2,
    )(me, na, nb, *[a for b in back for a in b])


def write3(ref, x):
    n = x.shape[0]
    high = x.astype(BF16)
    rest = x - high.astype(F32)
    mid = rest.astype(BF16)
    low = (rest - mid.astype(F32)).astype(BF16)
    ref[0:n] = high
    ref[n : 2 * n] = mid
    ref[2 * n : 3 * n] = low


def read3(x):
    n = x.shape[0] // 3
    return x[:n].astype(F32) + x[n : 2 * n].astype(F32) + x[2 * n :].astype(F32)


def normed_kernel(me_ref, xa_ref, xb_ref, pa_ref, pb_ref, w_ref, small_ref, *refs):
    own_ref, send_ref, three_ref = refs[-3:]
    heads = [refs[3 * h : 3 * h + 3] for h in range(HEADS)]
    length, width = xb_ref.shape
    cell = me_ref[0] // 2
    tt = (((0,), (1,)), ((), ()))
    w = w_ref[...]
    dq = sum(h[0][...].astype(F32) for h in heads[:2]), sum(h[0][...].astype(F32) for h in heads[2:])
    dq = jnp.concatenate(dq, axis=1).astype(BF16)
    dk = jnp.concatenate([h[1][...] for h in heads], axis=0)
    dv = jnp.concatenate([h[2][...] for h in heads], axis=0)
    total = jnp.zeros((1, width), F32)
    for b in range(4):
        cut = slice(b * length, (b + 1) * length)
        gn = dot(dk[:, cut], w[:, width : 2 * width], tt) + dot(dv[:, cut], w[:, 2 * width :], tt)
        at = slice(b // 2 * length, (b // 2 + 1) * length)
        if b % 2 == 0:
            gn += dot(dq[at], w[:, :width], NT)
        x = xa_ref[cell] if b == 0 else (pa_ref, xb_ref, pb_ref)[b - 1][...]
        xhat, _ = norm_parts(x.astype(F32))
        total += jnp.sum(gn * xhat, axis=0, keepdims=True)
        if b % 2 == 0:
            own_ref[at] = gn
        else:
            send_ref[at] = gn.astype(BF16)
    rows = small_ref.shape[0]
    keep = lax.broadcasted_iota(jnp.int32, (rows, 1), 0)
    small = jnp.where(keep < 9, small_ref[...], jnp.where(keep == 9, total, 0.0))
    write3(three_ref, small)


def normed_back(me, xa, xb, pa, pb, w, small, back):
    length, width = xb.shape
    rows = 2 * length
    smem = pl.BlockSpec(memory_space=pltpu.SMEM)
    vmem = pl.BlockSpec(memory_space=pltpu.VMEM)
    return call(
        normed_kernel,
        [sds((rows, width), F32), sds((rows, width), BF16), sds((3 * small.shape[0], width), BF16)],
        vmem=24,
        flops=12 * rows * width * width,
        moved=16 * rows * width,
        in_specs=[smem] + [vmem] * (6 + 3 * HEADS),
        out_specs=[vmem] * 3,
    )(me, xa, xb, pa, pb, w, small, *[a for b in back for a in b])


def tokens_kernel(me_ref, xa_ref, xb_ref, gain_ref, gres_ref, own_ref, got_ref, mine_ref, back_ref):
    length = mine_ref.shape[0]
    for b in range(2):
        cut = slice(b * length, (b + 1) * length)
        x = xa_ref[me_ref[0] // 2] if b == 0 else xb_ref[...]
        xhat, rstd = norm_parts(x.astype(F32))
        gn = own_ref[cut] + got_ref[cut].astype(F32)
        g = gres_ref[cut] + norm_back(gn, xhat, rstd, gain_ref[...])
        if b == 0:
            mine_ref[...] = g
        else:
            back_ref[...] = g.astype(BF16)


def tokens_back(me, xa, xb, gain, gres, own, got):
    length, width = xb.shape
    smem = pl.BlockSpec(memory_space=pltpu.SMEM)
    vmem = pl.BlockSpec(memory_space=pltpu.VMEM)
    return call(
        tokens_kernel,
        [sds((length, width), F32), sds((length, width), BF16)],
        vmem=12,
        flops=60 * length * width,
        moved=24 * length * width,
        in_specs=[smem] + [vmem] * 6,
        out_specs=[vmem] * 2,
    )(me, xa, xb, gain, gres, own, got)


def join_kernel(a_ref, b_ref, three_ref, o_ref):
    n = a_ref.shape[0]
    o_ref[:n] = (a_ref[...].astype(F32) + b_ref[...].astype(F32)).astype(BF16)
    o_ref[n:] = three_ref[...]


def merge_kernel(a_ref, b_ref, o_ref, *, small):
    n = a_ref.shape[0] - small
    o_ref[:n] = (a_ref[:n].astype(F32) + b_ref[:n].astype(F32)).astype(BF16)
    write3(o_ref.at[n:], read3(a_ref[n:]) + read3(b_ref[n:]))


def join(a, b, three):
    vmem = pl.BlockSpec(memory_space=pltpu.VMEM)
    shape = (a.shape[0] + three.shape[0], a.shape[1])
    return call(join_kernel, sds(shape, BF16), moved=6 * a.size, vmem=4, in_specs=[vmem] * 3, out_specs=vmem)(a, b, three)


def merge(a, b, small):
    vmem = pl.BlockSpec(memory_space=pltpu.VMEM)
    kernel = functools.partial(merge_kernel, small=small)
    return call(kernel, sds(a.shape, BF16), moved=6 * a.size, vmem=4, in_specs=[vmem] * 2, out_specs=vmem)(a, b)


def unpack_main_kernel(me_ref, own_ref, got_ref, down_ref, up_ref, out_ref):
    hidden, width = down_ref.shape

    def write(low_ref, high_ref):
        half = low_ref.shape[0]

        def rows(start, stop):
            if stop <= half:
                return low_ref[start:stop].astype(F32)
            return high_ref[start - half : stop - half].astype(F32)

        step = math.gcd(half, width)
        for at in range(0, hidden, step):
            down_ref[at : at + step] = rows(at, at + step)
        for j in range(hidden // width):
            for at in range(0, width, step):
                start = hidden + j * width + at
                up_ref[at : at + step, j * width : (j + 1) * width] = rows(start, start + step)
        for at in range(0, width, step):
            out_ref[at : at + step] = rows(2 * hidden + at, 2 * hidden + at + step)

    @pl.when(me_ref[0] % 2 == 0)
    def _():
        write(own_ref, got_ref)

    @pl.when(me_ref[0] % 2 == 1)
    def _():
        write(got_ref, own_ref)


def unpack_main(me, own, got, hidden):
    width = own.shape[1]
    smem = pl.BlockSpec(memory_space=pltpu.SMEM)
    vmem = pl.BlockSpec(memory_space=pltpu.VMEM)
    return call(
        unpack_main_kernel,
        [sds((hidden, width), F32), sds((width, hidden), F32), sds((width, width), F32)],
        vmem=12,
        moved=12 * hidden * width,
        in_specs=[smem, vmem, vmem],
        out_specs=[vmem] * 3,
    )(me, own, got)


def finish_kernel(me_ref, own_ref, got_ref, qkv_ref, gain1_ref, gain2_ref, dec_ref, sum_ref):
    width = gain1_ref.shape[1]
    half = 3 * width // 2

    def write(low_ref, high_ref):
        step = math.gcd(half, width)
        for j in range(3):
            for at in range(0, width, step):
                start = j * width + at
                ref, first = (low_ref, start) if start < half else (high_ref, start - half)
                qkv_ref[at : at + step, j * width : (j + 1) * width] = ref[first : first + step].astype(F32)

    @pl.when(me_ref[0] % 2 == 0)
    def _():
        write(own_ref, got_ref)

    @pl.when(me_ref[0] % 2 == 1)
    def _():
        write(got_ref, own_ref)

    small = read3(own_ref[half:]) + read3(got_ref[half:])
    gain1_ref[...] = small[9:10]
    gain2_ref[...] = small[8:9]
    dec_ref[...] = small[5:8]
    sums = jnp.sum(small, axis=1, keepdims=True)
    count = sums[4:5]
    rms = jnp.sqrt(sums[0:3] / (count * width))
    lane = lax.broadcasted_iota(jnp.int32, (1, 4), 1)
    out = jnp.where(lane == 0, sums[3:4] / count, 0.0)
    for j in range(3):
        out = jnp.where(lane == j + 1, rms[j : j + 1], out)
    sum_ref[...] = out


def finish(me, own, got):
    width = own.shape[1]
    smem = pl.BlockSpec(memory_space=pltpu.SMEM)
    vmem = pl.BlockSpec(memory_space=pltpu.VMEM)
    return call(
        finish_kernel,
        [sds((width, 3 * width), F32), sds((1, width), F32), sds((1, width), F32), sds((3, width), F32), sds((1, 4), F32)],
        vmem=8,
        moved=12 * 3 * width * width,
        in_specs=[smem] + [vmem] * 2,
        out_specs=[vmem] * 5,
    )(me, own, got)


AXES = ("cells", "slots")


def devices():
    return lax.axis_size("cells") * lax.axis_size("slots")


def swap(x, mask, odd=None):
    odd = mask if odd is None else odd
    return lax.ppermute(x, AXES, [(i, i ^ (odd if i % 2 else mask)) for i in range(devices())])


def routes():
    slots = lax.axis_size("slots")
    near, far = [slots, 2 * slots], []
    bit = 4 * slots
    while bit < devices():
        far.append(bit)
        bit *= 2
    return list(zip(near + far + [2], near[::-1] + [2] + far))


def after(x, *others):
    return lax.optimization_barrier((x, *others))[0]


def per_device(
    tokens,
    valid_len,
    library,
    gene_slot,
    counts,
    norm1_gain,
    w_qkv,
    w_out,
    norm2_gain,
    w_up,
    w_down,
    w_decoder,
):
    cells, length, width = tokens.shape
    hidden = w_up.shape[1]
    slot = lax.axis_index("slots")
    cell = slot // 2
    me = jnp.full((1,), slot, jnp.int32)
    pick = lambda a: lax.dynamic_index_in_dim(a, cell, 0, keepdims=False)
    other = lambda a: lax.dynamic_index_in_dim(a, 1 - cell, 0, keepdims=False)

    came = swap(other(tokens), 2)
    near = swap(pick(tokens), 1)
    mine_counts = pick(counts)[None]
    away_counts = other(counts)[None]
    tables = (mine_counts, swap(mine_counts, 1), swap(away_counts, 2), swap(away_counts, 3))
    gain1 = norm1_gain[None]
    gain2 = norm2_gain[None]

    na, qa, ka, va, ta = qkv(me, valid_len, tokens, near, gain1, w_qkv, 0)
    came = after(came, ta)
    far = swap(came, 1)
    p, nb, gres, keep, qb, kb, vb, _, do, dl, cols, send, small = layer(
        me, valid_len, library, tokens, came, far, gain1, w_qkv, qa, ka, va, ta,
        gain2, w_out, w_up, w_down, w_decoder, gene_slot, tables,
    )

    order = routes()
    number = lax.axis_index("cells") * lax.axis_size("slots") + slot
    sides = [jnp.where(slot % 2 == 0, number // even, number // odd) % 2 for even, odd in order[:2]]

    def halve(x, side):
        n = x.shape[0] // 2
        return lax.dynamic_slice_in_dim(x, side * n, n, 0), lax.dynamic_slice_in_dim(x, (1 - side) * n, n, 0)

    def whole(own, got, side):
        return jnp.where(side == 0, jnp.concatenate([own, got], 0), jnp.concatenate([got, own], 0))

    def back(h, p):
        return attend_back(h, me, valid_len, qa, qb, do, dl, cols, ka, kb, va, vb, p)

    got = swap(send, 1)
    backs = [back(0, p)]
    main = keep + after(got, backs[0][0])
    for i in range(2):
        mine, away = halve(main, sides[i])
        got = swap(away, *order[i])
        backs.append(back(1 + i, after(p, away)))
        main = mine + after(got, backs[-1][0])
    got = swap(main, *order[2])
    backs.append(back(3, after(p, main)))
    main = main + after(got, backs[-1][0])
    got = swap(main, *order[3])

    keep, send = weights(me, na, nb, backs)
    final_got = swap(send, 1)
    gn_own, gn_send, three = normed_back(me, tokens, came, near, far, w_qkv, small, backs)
    rows3 = three.shape[0]
    gn_got = swap(gn_send, 1)
    final = join(keep, final_got, three)
    final_got = swap(final, *order[0])
    main = main + after(got, final)
    for masks in order[4:]:
        main = main + swap(main, *masks)
    got = swap(main, *order[1])
    mine, away = tokens_back(me, tokens, came, gain1, gres, gn_own, gn_got)
    returned = swap(away, 2)
    final = merge(final, final_got, rows3)
    final_got = swap(final, *order[1])
    main = whole(main, after(got, final), sides[1])
    got = swap(main, *order[0])
    final = merge(final, final_got, rows3)
    final_got = swap(final, *order[2])
    main = whole(main, after(got, final), sides[0])
    got = swap(main, 1)
    final = merge(final, final_got, rows3)
    for masks in order[3:]:
        final_got = swap(final, *masks)
        final = merge(final, final_got, rows3)
    g_down, g_up, g_out = unpack_main(me, main, got, hidden)
    returned = returned.astype(F32)
    grad_tokens = jnp.where(cell == 0, jnp.stack([mine, returned]), jnp.stack([returned, mine]))
    g_qkv, g_gain1, g_gain2, g_dec, summary = finish(me, final, swap(final, 1))
    return (grad_tokens, g_gain1[0], g_qkv, g_out, g_gain2[0], g_up, g_down, g_dec, summary[0])


def solution(mesh):
    in_specs = (
        P("cells", "slots", None),
        P("cells"),
        P("cells"),
        P("cells", None),
        P("cells", "slots"),
        P(),
        P(),
        P(),
        P(),
        P(),
        P(),
        P(),
    )
    out_specs = (P("cells", "slots", None), P(), P(), P(), P(), P(), P(), P(), P())
    return jax.shard_map(
        per_device, mesh=mesh, in_specs=in_specs, out_specs=out_specs, check_vma=False
    )
```

```python
import functools
import math

import jax
import jax.numpy as jnp
from jax import lax
from jax.experimental import pallas as pl
from jax.experimental.pallas import tpu as pltpu
from jax.sharding import PartitionSpec as P

HEADS = 4
EPS = 1e-05
BACK_VMEM = 40
SMALL = 10
BF16 = jnp.bfloat16
F32 = jnp.float32
NN = (((1,), (0,)), ((), ()))
NT = (((1,), (1,)), ((), ()))
TN = (((0,), (0,)), ((), ()))
SCORE_BOUND = 60.0
ERFC_P = 0.325
ERFC_C = (
    -5.927487965082223e-05,
    0.18467549445148965,
    0.1708094188150158,
    0.2414269376514742,
    -0.07282782022580145,
    0.6147421737182138,
    -0.5684607599983035,
    0.5878333184067656,
    -0.15813953377061551,
)


def dot(a, b, dims):
    return lax.dot_general(a, b, dims, preferred_element_type=F32)


def call(kernel, out_shape, flops=0, moved=0, vmem=48, **kw):
    return pl.pallas_call(
        kernel,
        out_shape=out_shape,
        compiler_params=pltpu.CompilerParams(vmem_limit_bytes=vmem * 2**20),
        cost_estimate=pl.CostEstimate(flops=int(flops), bytes_accessed=int(moved), transcendentals=0),
        **kw,
    )


def sds(shape, dtype):
    return jax.ShapeDtypeStruct(shape, dtype)


def norm_parts(x):
    centred = x - jnp.mean(x, axis=-1, keepdims=True)
    rstd = lax.rsqrt(jnp.mean(centred * centred, axis=-1, keepdims=True) + EPS)
    return centred * rstd, rstd


def norm_back(gy, xhat, rstd, gain):
    gx = gy * gain
    first = jnp.mean(gx, axis=-1, keepdims=True)
    second = jnp.mean(gx * xhat, axis=-1, keepdims=True)
    return rstd * (gx - first - xhat * second)


def head_ones(width, lanes=None, step=None):
    rows = lax.broadcasted_iota(jnp.int32, (width, lanes or width), 0) // (width // HEADS)
    cols = lax.broadcasted_iota(jnp.int32, (width, lanes or width), 1) // (step or width // HEADS)
    return (rows == cols).astype(F32).astype(BF16)


def start_copies(pairs, sem):
    copies = [pltpu.make_async_copy(src, dst, sem.at[i]) for i, (src, dst) in enumerate(pairs)]
    for c in copies:
        c.start()
    return copies


def live_rows(me_ref, len_ref, block, length):
    place = (me_ref[0] ^ block) * length + lax.broadcasted_iota(jnp.int32, (length, 1), 0)
    return place < len_ref[me_ref[0] // 2]


def qkv_kernel(me_ref, len_ref, own_ref, pair_ref, gain_ref, w_ref, n_out, q_ref, k_ref, v_ref, top_ref, n_ref, n_sem, *, first):
    length, width = pair_ref.shape
    ones = head_ones(width)
    top_ref[...] = jnp.zeros_like(top_ref)
    for j in range(2):
        cut = slice(j * length, (j + 1) * length)
        if j == 1:
            x = pair_ref[...]
        elif first == 0:
            x = own_ref[me_ref[0] // 2]
        else:
            x = own_ref[...]
        xhat, _ = norm_parts(x.astype(F32))
        normed = (xhat * gain_ref[...]).astype(BF16)
        n_ref[cut] = normed
        live = live_rows(me_ref, len_ref, first + j, length).astype(F32).astype(BF16)
        skip = width if j == 1 else 0
        mixed = dot(normed, w_ref[:, skip:], NN).astype(BF16)
        if j == 0:
            q = mixed[:, :width] * BF16((width // HEADS) ** -0.5)
            q_ref[...] = q
            qf = q.astype(F32)
            top_ref[0:1, :] = jnp.max(dot((qf * qf).astype(BF16), ones, NN), axis=0, keepdims=True)
        k = mixed[:, width - skip : 2 * width - skip] * live
        k_ref[cut] = k
        v_ref[cut] = mixed[:, 2 * width - skip :] * live
        kf = k.astype(F32)
        top_ref[1 + j : 2 + j, :] = jnp.max(dot((kf * kf).astype(BF16), ones, NN), axis=0, keepdims=True)
    keep_n = pltpu.make_async_copy(n_ref, n_out, n_sem)
    keep_n.start()
    if first == 0:
        keep_n.wait()


def qkv(me, valid_len, own, pair, gain, w, first):
    length, width = pair.shape
    smem = pl.BlockSpec(memory_space=pltpu.SMEM)
    vmem = pl.BlockSpec(memory_space=pltpu.VMEM)
    hbm = pl.BlockSpec(memory_space=pltpu.HBM)
    rows = 2 * length
    return call(
        functools.partial(qkv_kernel, first=first),
        [
            pltpu.HBM((rows, width), BF16),
            sds((length, width), BF16),
            sds((rows, width), BF16),
            sds((rows, width), BF16),
            sds((8, width), F32),
        ],
        flops=6 * rows * width * width,
        moved=10 * rows * width,
        vmem=16,
        in_specs=[smem, smem] + [vmem] * 4,
        out_specs=[hbm] + [vmem] * 4,
        scratch_shapes=[pltpu.VMEM((rows, width), BF16), pltpu.SemaphoreType.DMA],
    )(me, valid_len, own, pair, gain, w)


def live_keys(me_ref, len_ref, keys):
    lane = lax.broadcasted_iota(jnp.int32, (1, keys), 1)
    length = keys // 4
    place = ((lane // length) ^ me_ref[0]) * length + lane % length
    return place < len_ref[me_ref[0] // 2]


def gelu_parts(x):
    down = 1.0 + (ERFC_P * math.sqrt(0.5)) * jnp.abs(x)
    t = pl.reciprocal(down, approx=True)
    t = t * (2.0 - t * down)
    poly = jnp.full_like(t, 0.5 * ERFC_C[-1])
    for c in ERFC_C[-2::-1]:
        poly = poly * t + 0.5 * c
    bell = jnp.exp2((x * x) * (-0.5 * math.log2(math.e)))
    tail = poly * bell
    cdf = jnp.where(x >= 0, 1.0 - tail, tail)
    return x * cdf, cdf + (x * (1.0 / math.sqrt(2.0 * math.pi))) * bell


def gamma_parts(x):
    large = x > 16.0
    small = jnp.minimum(x, 16.0)
    w = small * (small + 7.0)
    a, b, c = w + 6.0, w + 10.0, w + 12.0
    log_prod = jnp.log(w * a * (b * c))
    sum_inv = (2.0 * small + 7.0) * (1.0 / w + 1.0 / a + 1.0 / b + 1.0 / c)
    big = jnp.where(large, x, x + 8.0)
    log_big = jnp.log(big)
    inv = 1.0 / big
    inv2 = inv * inv
    lg = (big - 0.5) * log_big - big + 0.5 * math.log(2.0 * math.pi)
    lg = lg + inv * (1.0 / 12.0 - inv2 * (1.0 / 360.0 - inv2 * (1.0 / 1260.0)))
    dg = log_big - 0.5 * inv - inv2 * (1.0 / 12.0 - inv2 * (1.0 / 120.0 - inv2 * (1.0 / 252.0)))
    return jnp.where(large, lg, lg - log_prod), jnp.where(large, dg, dg - sum_inv)


def softplus(x):
    return jnp.maximum(x, 0.0) + jnp.log(1.0 + jnp.exp(-jnp.abs(x)))


def sigmoid(x):
    return 1.0 / (1.0 + jnp.exp(-x))


def zinb(m, t, p, y, scale):
    rate = scale * (softplus(m) + 0.05)
    theta = softplus(t) + 0.05
    total = theta + rate
    inv_total = 1.0 / total
    log_total = jnp.log(total)
    log_theta = jnp.log(theta)
    z0 = theta * (log_theta - log_total)
    pi = sigmoid(p)
    e0 = jnp.exp(z0)
    den = pi + (1.0 - pi) * e0
    inv_den = 1.0 / den
    some = y > 0
    yf = y.astype(F32)
    lg_sum, dg_sum = gamma_parts(yf + theta)
    lg_theta, dg_theta = gamma_parts(theta)
    lg_y, _ = gamma_parts(yf + 1.0)
    log_nb = lg_sum - lg_theta - lg_y + z0 + yf * (jnp.log(rate) - log_total)
    nll = jnp.where(some, softplus(p) - log_nb, -jnp.log(den))
    g_z0 = jnp.where(some, -1.0, -(1.0 - pi) * e0 * inv_den)
    share = theta * inv_total
    g_theta = g_z0 * (log_theta - log_total + 1.0 - share)
    g_theta = g_theta + jnp.where(some, dg_theta - dg_sum + yf * inv_total, 0.0)
    g_rate = jnp.where(some, yf * (inv_total - 1.0 / rate), 0.0) - g_z0 * share
    g_p = jnp.where(some, pi, -(1.0 - e0) * inv_den * pi * (1.0 - pi))
    return nll, g_rate * scale * sigmoid(m), g_theta * sigmoid(t), g_p


def split2(x):
    high = x.astype(BF16)
    return high, (x - high.astype(F32)).astype(BF16)


def layer_kernel(me_ref, len_ref, lib_ref, xa_ref, xb_ref, pb_ref, gain1_ref, w_ref, qa_ref, ka_ref, va_ref, ta_ref,
                 gain_ref, w_out_ref, w_up_ref, w_down_ref, w_dec_ref, gene_ref, c0_ref, c1_ref, c2_ref, c3_ref,
                 p_ref, nb_ref, gres_out, keep_out, q_s, kb_ref, vb_ref, do_ref, cols_ref, send_ref,
                 small_ref,
                 nb_s, nb_sem, gres_ref, keep_ref, out_sem, qb_ref, tb_ref, cols_s, x_s, p_s, p_sem, gt_s, aug_s, o_s, linv_s, res_s, n2_s, act_s, gp_s, dec_s, gd_s, w_s, table_s, ga_down, ga_up, ga_out,
                 *, block, tall):
    part, width = ka_ref.shape
    keys = 2 * part
    length = part // 2
    rows = part
    hidden = w_up_ref.shape[1]
    pair = 2 * (width // HEADS)
    half = pair // 2
    pairs = HEADS // 2
    me = me_ref[0]
    cell = me // 2
    valid_len = len_ref[cell]
    gain = gain_ref[...]
    small_ref[...] = jnp.zeros_like(small_ref)
    ga_down[...] = jnp.zeros_like(ga_down)
    ga_up[...] = jnp.zeros_like(ga_up)
    ga_out[...] = jnp.zeros_like(ga_out)
    lane = lax.broadcasted_iota(jnp.int32, (1, pair), 1)

    def rowsum(a):
        return jnp.sum(a, axis=0, keepdims=True)

    qkv_kernel(me_ref, len_ref, xb_ref, pb_ref, gain1_ref, w_ref, nb_ref, qb_ref, kb_ref, vb_ref, tb_ref, nb_s, nb_sem, first=2)

    live = live_keys(me_ref, len_ref, keys)
    mask = jnp.transpose(jnp.broadcast_to(live.astype(F32), (pair, keys))).astype(BF16)
    for j, ref in enumerate((va_ref, vb_ref)):
        cut = slice(j * part, (j + 1) * part)
        for g in range(pairs):
            v = ref[:, g * pair : (g + 1) * pair]
            aug_s[2 * g, cut] = jnp.where(lane < half, v, mask[cut])
            aug_s[2 * g + 1, cut] = jnp.where(lane < half, mask[cut], v)

    top_q = jnp.maximum(ta_ref[0:1], tb_ref[0:1])
    top_k = jnp.maximum(jnp.maximum(ta_ref[1:2], tb_ref[1:2]), jnp.maximum(ta_ref[2:3], tb_ref[2:3]))
    plain = jnp.max(top_q * top_k) * 1.05 < SCORE_BOUND * SCORE_BOUND

    q_s[0:length] = qa_ref[...]
    q_s[length:rows] = qb_ref[...]
    x_s[0:length] = xa_ref[cell]
    x_s[length:rows] = xb_ref[...]

    def copy(b, g):
        slot = (b * pairs + g) % 2
        rcut = pl.ds(pl.multiple_of(b * block, block), block)
        return pltpu.make_async_copy(p_s.at[slot], p_ref.at[pl.ds(2 * g, 2), rcut], p_sem.at[slot])

    def attend_block(b, g, safe):
        cut = pl.ds(pl.multiple_of(b * block, block), block)
        cols = slice(g * pair, (g + 1) * pair)
        slot = (b * pairs + g) % 2
        q = q_s[cut, cols]
        zero = jnp.zeros_like(q)
        outs = []
        for h in range(2):
            home = p_s.at[slot, h]
            qh = jnp.where(lane < half, q, zero) if h == 0 else jnp.where(lane < half, zero, q)
            if safe:
                s = jnp.concatenate([dot(qh, ref[:, cols], NT) for ref in (ka_ref, kb_ref)], axis=1)
                s = jnp.where(live, s, -1e30)
                p = jnp.exp(s - jnp.max(s, axis=1, keepdims=True)).astype(BF16)
                home[...] = p
                total = dot(p, aug_s[2 * g + h], NN)
            else:
                total = None
                for j, ref in enumerate((ka_ref, kb_ref)):
                    kcut = slice(j * part, (j + 1) * part)
                    p = jnp.exp(dot(qh, ref[:, cols], NT)).astype(BF16)
                    home[:, kcut] = p
                    o = dot(p, aug_s[2 * g + h, kcut], NN)
                    total = o if total is None else total + o
            outs.append(total)
        up = jnp.where(lane < half, outs[0], outs[1])
        down = pltpu.roll(jnp.where(lane < half, outs[1], outs[0]), half, 1)
        inverse = 1.0 / down
        o_s[cut, cols] = up * inverse
        linv_s[cut, cols] = inverse

    @pl.loop(0, rows // block)
    def _(b):
        for g in range(pairs):

            @pl.when(b > 0)
            def _():
                copy(b - 1, g).wait()

            pl.when(plain)(functools.partial(attend_block, b, g, False))
            pl.when(jnp.logical_not(plain))(functools.partial(attend_block, b, g, True))
            copy(b, g).start()

    @pl.loop(0, rows // tall)
    def _(b):
        start = pl.multiple_of(b * tall, tall)
        cut = pl.ds(start, tall)
        base = jnp.where(start < length, me * length + start, (me ^ 2) * length + start - length)
        valid = (base + lax.broadcasted_iota(jnp.int32, (tall, 1), 0) < valid_len).astype(F32)
        attn_out = dot(o_s[cut].astype(BF16), w_out_ref[...], NN)
        resid = x_s[cut].astype(F32) + attn_out
        res_s[cut] = resid
        xhat, _ = norm_parts(resid)
        normed = (xhat * gain).astype(BF16)
        n2_s[cut] = normed
        act, slope = gelu_parts(dot(normed, w_up_ref[...], NN))
        act = act.astype(BF16)
        act_s[cut] = act
        gp_s[cut] = slope
        mlp_out = dot(act, w_down_ref[...], NN)
        final = resid + mlp_out
        dec_s[cut] = final.astype(BF16)
        small_ref[0:1, :] += rowsum(valid * final * final)
        small_ref[1:2, :] += rowsum(valid * attn_out * attn_out)
        small_ref[2:3, :] += rowsum(valid * mlp_out * mlp_out)

    w_s[...] = jnp.zeros_like(w_s)
    w_s[0:3, :] = w_dec_ref[...].astype(F32)
    w_s[3:6, :] = w_dec_ref[...].astype(F32)
    w_twice = w_s[...].astype(BF16)
    decoded = dot(w_twice, dec_s[...], NT)
    for j, ref in enumerate((c0_ref, c1_ref, c2_ref, c3_ref)):
        for i in range(length // 128):
            table_s[j * (length // 128) + i : j * (length // 128) + i + 1, :] = ref[:, i * 128 : (i + 1) * 128].astype(F32)
    starts = (me * length, (me ^ 2) * length)
    gene = jnp.concatenate([gene_ref[pl.ds(cell, 1), pl.ds(pl.multiple_of(a, length), length)] for a in starts], axis=1)
    gene = ((gene // length) ^ me) * length + gene % length
    high = (lax.broadcasted_iota(jnp.int32, (table_s.shape[0], rows), 0) == gene // 128).astype(F32).astype(BF16)
    found = dot(table_s[...].astype(BF16), high, TN)
    low = lax.broadcasted_iota(jnp.int32, (128, rows), 0) == gene % 128
    observed = rowsum(jnp.where(low, found, 0.0))
    lane = lax.broadcasted_iota(jnp.int32, (1, rows), 1)
    places = jnp.where(lane < length, starts[0] + lane, starts[1] + lane - length)
    valid = (places < valid_len).astype(F32)
    scale = lib_ref[cell].astype(F32) / (4 * length)
    nll, g_m, g_t, g_p = zinb(decoded[0:1], decoded[1:2], decoded[2:3], observed, scale)
    nll = nll * valid
    for j in range(rows // width):
        small_ref[3:4, :] += nll[:, j * width : (j + 1) * width]
        small_ref[4:5, :] += valid[:, j * width : (j + 1) * width]
    gd_s[...] = jnp.zeros_like(gd_s)
    for j, g in enumerate((g_m, g_t, g_p)):
        gh, gl = split2(g * valid)
        gd_s[j : j + 1, :] = gh.astype(F32)
        gd_s[3 + j : 4 + j, :] = gl.astype(F32)
    gd = gd_s[...].astype(BF16)
    gw = dot(gd, dec_s[...], NN)
    small_ref[5:8, :] = gw[0:3] + gw[3:6]

    cols_s[...] = jnp.zeros_like(cols_s)
    heads = head_ones(width, 128, 1)
    for j in range(rows // tall):
        gt_s[j * 16 : (j + 1) * 16] = gd[:, j * tall : (j + 1) * tall]

    @pl.loop(0, rows // tall)
    def _(b):
        cut = pl.ds(pl.multiple_of(b * tall, tall), tall)
        g_final = dot(gt_s[pl.ds(pl.multiple_of(b * 16, 16), 16)], w_twice, TN).astype(BF16)
        ga_down[...] += dot(act_s[cut], g_final, TN)
        g_up = (dot(g_final, w_down_ref[...], NT) * gp_s[cut]).astype(BF16)
        ga_up[...] += dot(n2_s[cut], g_up, TN)
        g_normed = dot(g_up, w_up_ref[...], NT)
        xhat, rstd = norm_parts(res_s[cut])
        small_ref[8:9, :] += rowsum(g_normed * xhat)
        g_res = g_final.astype(F32) + norm_back(g_normed, xhat, rstd, gain)
        gres_ref[cut] = g_res
        g_attn = g_res.astype(BF16)
        o = o_s[cut]
        linv = linv_s[cut]
        ga_out[...] += dot(o.astype(BF16), g_attn, TN)
        do = dot(g_attn, w_out_ref[...], NT).astype(BF16)
        do_ref[cut] = do
        dof = do.astype(F32)
        ph, pl_ = split2(dof * o)
        cols_s[:, 0:HEADS] = (dot(ph, heads, NN) + dot(pl_, heads, NN))[:, 0:HEADS]
        for h in range(HEADS):
            cols_s[:, HEADS + h : HEADS + h + 1] = linv[:, h * half : h * half + 1]
        cols_ref[:, cut] = jnp.transpose(cols_s[...])[0 : 2 * HEADS]

    gres_copy = pltpu.make_async_copy(gres_ref, gres_out, out_sem.at[0])
    gres_copy.start()
    for g in range(pairs):
        copy(rows // block - 1, g).wait()
    pltpu.make_async_copy(nb_s, nb_ref, nb_sem).wait()

    def write(low_ref, high_ref):
        pieces = [ga_down[...]]
        pieces += [ga_up[:, j * width : (j + 1) * width] for j in range(hidden // width)]
        pieces += [ga_out[...]]
        at = 0
        half = low_ref.shape[0]
        for piece in pieces:
            n = piece.shape[0]
            first = max(0, min(n, half - at))
            if first:
                low_ref[at : at + first, :] = piece[:first].astype(BF16)
            if first < n:
                high_ref[at + first - half : at + n - half, :] = piece[first:].astype(BF16)
            at += n

    @pl.when(me % 2 == 0)
    def _():
        write(keep_ref, send_ref)

    @pl.when(me % 2 == 1)
    def _():
        write(send_ref, keep_ref)

    keep_copy = pltpu.make_async_copy(keep_ref, keep_out, out_sem.at[1])
    keep_copy.start()
    gres_copy.wait()
    keep_copy.wait()


def layer(me, valid_len, library, xa, xb, pb, gain1, w, qa, ka, va, ta, gain, w_out, w_up, w_down, w_dec, gene, tables, block=256, tall=512):
    part, width = ka.shape
    rows, keys, length = part, 2 * part, part // 2
    hidden = w_up.shape[1]
    pair = 2 * (width // HEADS)
    smem = pl.BlockSpec(memory_space=pltpu.SMEM)
    vmem = pl.BlockSpec(memory_space=pltpu.VMEM)
    half = (2 * hidden + width) // 2
    return call(
        functools.partial(layer_kernel, block=block, tall=tall),
        [
            pltpu.HBM((HEADS, rows, keys), BF16),
            pltpu.HBM((part, width), BF16),
            pltpu.HBM((rows, width), F32),
            pltpu.HBM((half, width), BF16),
            sds((rows, width), BF16),
            sds((part, width), BF16),
            sds((part, width), BF16),
            sds((rows, width), BF16),
            sds((2 * HEADS, rows), F32),
            sds((half, width), BF16),
            sds((16, width), F32),
        ],
        flops=24 * rows * width * hidden + 16 * rows * keys * width,
        vmem=46,
        in_specs=[smem] * 3 + [vmem] * 19,
        out_specs=[pl.BlockSpec(memory_space=pltpu.HBM)] * 4 + [vmem] * 7,
        scratch_shapes=[
            pltpu.VMEM((part, width), BF16),
            pltpu.SemaphoreType.DMA,
            pltpu.VMEM((rows, width), F32),
            pltpu.VMEM((half, width), BF16),
            pltpu.SemaphoreType.DMA((2,)),
            pltpu.VMEM((length, width), BF16),
            pltpu.VMEM((8, width), F32),
            pltpu.VMEM((tall, 128), F32),
            pltpu.VMEM((rows, width), BF16),
            pltpu.VMEM((2, 2, block, keys), BF16),
            pltpu.SemaphoreType.DMA((2,)),
            pltpu.VMEM((16 * rows // tall, tall), BF16),
            pltpu.VMEM((HEADS, keys, pair), BF16),
            pltpu.VMEM((rows, width), F32),
            pltpu.VMEM((rows, width), F32),
            pltpu.VMEM((rows, width), F32),
            pltpu.VMEM((rows, width), BF16),
            pltpu.VMEM((rows, hidden), BF16),
            pltpu.VMEM((rows, hidden), F32),
            pltpu.VMEM((rows, width), BF16),
            pltpu.VMEM((16, rows), F32),
            pltpu.VMEM((16, width), F32),
            pltpu.VMEM((rows // 64, 128), F32),
            pltpu.VMEM((hidden, width), F32),
            pltpu.VMEM((width, hidden), F32),
            pltpu.VMEM((width, width), F32),
        ],
    )(me, valid_len, library, xa, xb, pb, gain1, w, qa, ka, va, ta, gain, w_out, w_up, w_down, w_dec, gene, *tables)


def attend_back_kernel(me_ref, len_ref, q_ref, do_ref, cols_ref, ka_ref, kb_ref, va_ref, vb_ref, *refs, head, block, chunk):
    refs = list(refs)
    first, following = head == 0, head + 1 < HEADS
    p_ref = None if first else refs.pop(0)
    home_ref = refs.pop(0) if following else None
    dq_ref, dk_ref, dv_ref = refs[:3]
    next_ref = refs[3] if following else None
    ak_ref, av_ref = refs[3 + following : 5 + following]
    copies = []
    if first:
        p_ref, p_sem = refs[6:8]
        cuts = [slice(i, i + block) for i in range(0, do_ref.shape[0], block)]
        copies = start_copies([(home_ref.at[0, cut], p_ref.at[cut]) for cut in cuts], p_sem)
    if following:
        fetch = pltpu.make_async_copy(home_ref.at[head + 1], next_ref, refs[-1])
        fetch.start()
    part, width = ka_ref.shape
    keys = 2 * part
    rows = do_ref.shape[0]
    half = width // HEADS
    pair = 2 * half
    lane = lax.broadcasted_iota(jnp.int32, (1, pair), 1)
    lo = (head % 2) * half
    own = (lane < half) if head % 2 == 0 else (lane >= half)
    at0 = head // 2 * pair
    cols = slice(at0, at0 + pair)
    mine = slice(at0 + lo, at0 + lo + half)
    for b in range(rows // block):
        cut = slice(b * block, (b + 1) * block)
        q = q_ref[cut, mine]
        do = do_ref[cut, cols]
        do = jnp.where(own, do, jnp.zeros_like(do))
        both = jnp.transpose(cols_ref[:, cut])
        delta = both[:, head : head + 1]
        linv = both[:, HEADS + head : HEADS + head + 1]
        dl = (do_ref[cut, mine].astype(F32) * linv).astype(BF16)
        if first:
            copies[b].wait()
        total = None
        for c in range(keys // chunk):
            kcut = slice(c * chunk, (c + 1) * chunk)
            k_ref, v_ref = (ka_ref, va_ref) if c * chunk < part else (kb_ref, vb_ref)
            kat = c * chunk % part
            kc = k_ref[kat : kat + chunk, cols]
            dp = dot(do, v_ref[kat : kat + chunk, cols], NT)
            pc = p_ref[cut, kcut]
            ds = (pc.astype(F32) * ((dp - delta) * linv)).astype(BF16)
            step = dot(ds, kc, NN)
            total = step if total is None else total + step
            dv = dot(dl, pc, TN)
            dk = dot(q, ds, TN)
            if b == 0:
                av_ref[:, kcut] = dv
                ak_ref[:, kcut] = dk
            else:
                av_ref[:, kcut] += dv
                ak_ref[:, kcut] += dk
        dq_ref[cut] = (jnp.where(own, total, 0.0) * half**-0.5).astype(BF16)
    live = live_keys(me_ref, len_ref, keys)
    dk_ref[...] = jnp.where(live, ak_ref[...], 0.0).astype(BF16)
    dv_ref[...] = jnp.where(live, av_ref[...], 0.0).astype(BF16)
    if following:
        fetch.wait()


def attend_back(head, me, valid_len, q, do, cols, ka, kb, va, vb, p, home, block=512, chunk=512):
    rows = do.shape[0]
    part, width = ka.shape
    keys = 2 * part
    pair = 2 * (width // HEADS)
    smem = pl.BlockSpec(memory_space=pltpu.SMEM)
    vmem = pl.BlockSpec(memory_space=pltpu.VMEM)
    first, following = head == 0, head + 1 < HEADS
    return call(
        functools.partial(attend_back_kernel, head=head, block=block, chunk=chunk),
        [sds((rows, pair), BF16), sds((pair // 2, keys), BF16), sds((pair // 2, keys), BF16)]
        + [sds((rows, keys), BF16)] * following,
        flops=8 * rows * keys * width,
        moved=2 * rows * keys,
        vmem=BACK_VMEM,
        in_specs=[smem, smem] + [vmem] * (7 + (not first)) + [pl.BlockSpec(memory_space=pltpu.HBM)] * following,
        out_specs=[vmem] * (3 + following),
        scratch_shapes=[pltpu.VMEM((pair // 2, keys), F32), pltpu.VMEM((pair // 2, keys), F32)]
        + [pltpu.VMEM((rows, keys), BF16), pltpu.SemaphoreType.DMA((rows // block,))] * first
        + [pltpu.SemaphoreType.DMA] * following,
    )(me, valid_len, q, do, cols, ka, kb, va, vb, *([] if first else [p]), *([home] * following))


def weights_kernel(me_ref, na_ref, nb_ref, *refs):
    keep_ref, send_ref = refs[-2:]
    heads = [refs[3 * h : 3 * h + 3] for h in range(HEADS)]
    part, width = na_ref.shape
    length = part // 2
    dim = width // HEADS
    dq = sum(h[0][...].astype(F32) for h in heads[:2]), sum(h[0][...].astype(F32) for h in heads[2:])
    dq = jnp.concatenate(dq, axis=1).astype(BF16)
    gq = dot(na_ref[:length], dq[:length], TN) + dot(nb_ref[:length], dq[length:], TN)
    outs = [gq]
    for j in (1, 2):
        d = jnp.concatenate([h[j][...] for h in heads], axis=0)
        g = dot(d[:, :part], na_ref[...], NN) + dot(d[:, part:], nb_ref[...], NN)
        outs.append(jnp.transpose(g))
    half = 3 * width // 2

    def write(low_ref, high_ref):
        at = 0
        for piece in outs:
            first = max(0, min(width, half - at))
            if first:
                low_ref[at : at + first, :] = piece[:first].astype(BF16)
            if first < width:
                high_ref[at + first - half : at + width - half, :] = piece[first:].astype(BF16)
            at += width

    @pl.when(me_ref[0] % 2 == 0)
    def _():
        write(keep_ref, send_ref)

    @pl.when(me_ref[0] % 2 == 1)
    def _():
        write(send_ref, keep_ref)


def weights(me, na, nb, back):
    part, width = na.shape
    half = 3 * width // 2
    smem = pl.BlockSpec(memory_space=pltpu.SMEM)
    vmem = pl.BlockSpec(memory_space=pltpu.VMEM)
    return call(
        weights_kernel,
        [sds((half, width), BF16)] * 2,
        vmem=16,
        flops=10 * part * width * width,
        moved=16 * part * width,
        in_specs=[smem] + [vmem] * (2 + 3 * HEADS),
        out_specs=[vmem] * 2,
    )(me, na, nb, *[a for b in back for a in b])


def write3(ref, x):
    n = x.shape[0]
    high = x.astype(BF16).astype(F32)
    rest = x - high
    mid = rest.astype(BF16).astype(F32)
    pad = jnp.zeros((ref.shape[0] - 3 * n, x.shape[1]), F32)
    ref[...] = jnp.concatenate([high, mid, rest - mid, pad], axis=0).astype(BF16)


def read3(x):
    n = SMALL
    x = x[: 3 * n].astype(F32)
    return x[:n] + x[n : 2 * n] + x[2 * n :]


def normed_kernel(me_ref, xa_ref, xb_ref, pa_ref, pb_ref, w_ref, small_ref, *refs):
    own_ref, send_ref, three_ref = refs[-3:]
    heads = [refs[3 * h : 3 * h + 3] for h in range(HEADS)]
    length, width = xb_ref.shape
    cell = me_ref[0] // 2
    tt = (((0,), (1,)), ((), ()))
    w = w_ref[...]
    dq = sum(h[0][...].astype(F32) for h in heads[:2]), sum(h[0][...].astype(F32) for h in heads[2:])
    dq = jnp.concatenate(dq, axis=1).astype(BF16)
    dk = jnp.concatenate([h[1][...] for h in heads], axis=0)
    dv = jnp.concatenate([h[2][...] for h in heads], axis=0)
    total = jnp.zeros((1, width), F32)
    for b in range(4):
        cut = slice(b * length, (b + 1) * length)
        gn = dot(dk[:, cut], w[:, width : 2 * width], tt) + dot(dv[:, cut], w[:, 2 * width :], tt)
        at = slice(b // 2 * length, (b // 2 + 1) * length)
        if b % 2 == 0:
            gn += dot(dq[at], w[:, :width], NT)
        x = xa_ref[cell] if b == 0 else (pa_ref, xb_ref, pb_ref)[b - 1][...]
        xhat, _ = norm_parts(x.astype(F32))
        total += jnp.sum(gn * xhat, axis=0, keepdims=True)
        if b % 2 == 0:
            own_ref[at] = gn
        else:
            send_ref[at] = gn.astype(BF16)
    write3(three_ref, jnp.concatenate([small_ref[0 : SMALL - 1], total], axis=0))


def normed_back(me, xa, xb, pa, pb, w, small, back):
    length, width = xb.shape
    rows = 2 * length
    smem = pl.BlockSpec(memory_space=pltpu.SMEM)
    vmem = pl.BlockSpec(memory_space=pltpu.VMEM)
    return call(
        normed_kernel,
        [sds((rows, width), F32), sds((rows, width), BF16), sds((32, width), BF16)],
        vmem=24,
        flops=12 * rows * width * width,
        moved=16 * rows * width,
        in_specs=[smem] + [vmem] * (6 + 3 * HEADS),
        out_specs=[vmem] * 3,
    )(me, xa, xb, pa, pb, w, small, *[a for b in back for a in b])


def tokens_kernel(me_ref, xa_ref, xb_ref, gain_ref, gres_ref, own_ref, got_ref, mine_ref, back_ref):
    length = mine_ref.shape[0]
    for b in range(2):
        cut = slice(b * length, (b + 1) * length)
        x = xa_ref[me_ref[0] // 2] if b == 0 else xb_ref[...]
        xhat, rstd = norm_parts(x.astype(F32))
        gn = own_ref[cut] + got_ref[cut].astype(F32)
        g = gres_ref[cut] + norm_back(gn, xhat, rstd, gain_ref[...])
        if b == 0:
            mine_ref[...] = g
        else:
            back_ref[...] = g.astype(BF16)


def tokens_back(me, xa, xb, gain, gres, own, got):
    length, width = xb.shape
    smem = pl.BlockSpec(memory_space=pltpu.SMEM)
    vmem = pl.BlockSpec(memory_space=pltpu.VMEM)
    return call(
        tokens_kernel,
        [sds((length, width), F32), sds((length, width), BF16)],
        vmem=12,
        flops=60 * length * width,
        moved=24 * length * width,
        in_specs=[smem] + [vmem] * 6,
        out_specs=[vmem] * 2,
    )(me, xa, xb, gain, gres, own, got)


def join_kernel(a_ref, b_ref, three_ref, o_ref):
    n = a_ref.shape[0]
    o_ref[:n] = (a_ref[...].astype(F32) + b_ref[...].astype(F32)).astype(BF16)
    o_ref[n:] = three_ref[...]


def merge_kernel(a_ref, b_ref, o_ref, *, small):
    n = a_ref.shape[0] - small
    o_ref[:n] = (a_ref[:n].astype(F32) + b_ref[:n].astype(F32)).astype(BF16)
    write3(o_ref.at[n:], read3(a_ref[n:]) + read3(b_ref[n:]))


def join(a, b, three):
    vmem = pl.BlockSpec(memory_space=pltpu.VMEM)
    shape = (a.shape[0] + three.shape[0], a.shape[1])
    return call(join_kernel, sds(shape, BF16), moved=6 * a.size, vmem=4, in_specs=[vmem] * 3, out_specs=vmem)(a, b, three)


def merge(a, b, small):
    vmem = pl.BlockSpec(memory_space=pltpu.VMEM)
    kernel = functools.partial(merge_kernel, small=small)
    return call(kernel, sds(a.shape, BF16), moved=6 * a.size, vmem=4, in_specs=[vmem] * 2, out_specs=vmem)(a, b)


def unpack_main_kernel(me_ref, own_ref, got_ref, down_ref, up_ref, out_ref):
    hidden, width = down_ref.shape

    def write(low_ref, high_ref):
        half = low_ref.shape[0]

        def rows(start, stop):
            if stop <= half:
                return low_ref[start:stop].astype(F32)
            return high_ref[start - half : stop - half].astype(F32)

        step = math.gcd(half, width)
        for at in range(0, hidden, step):
            down_ref[at : at + step] = rows(at, at + step)
        for j in range(hidden // width):
            for at in range(0, width, step):
                start = hidden + j * width + at
                up_ref[at : at + step, j * width : (j + 1) * width] = rows(start, start + step)
        for at in range(0, width, step):
            out_ref[at : at + step] = rows(2 * hidden + at, 2 * hidden + at + step)

    @pl.when(me_ref[0] % 2 == 0)
    def _():
        write(own_ref, got_ref)

    @pl.when(me_ref[0] % 2 == 1)
    def _():
        write(got_ref, own_ref)


def unpack_main(me, own, got, hidden):
    width = own.shape[1]
    smem = pl.BlockSpec(memory_space=pltpu.SMEM)
    vmem = pl.BlockSpec(memory_space=pltpu.VMEM)
    return call(
        unpack_main_kernel,
        [sds((hidden, width), F32), sds((width, hidden), F32), sds((width, width), F32)],
        vmem=12,
        moved=12 * hidden * width,
        in_specs=[smem, vmem, vmem],
        out_specs=[vmem] * 3,
    )(me, own, got)


def finish_kernel(me_ref, own_ref, got_ref, qkv_ref, gain1_ref, gain2_ref, dec_ref, sum_ref):
    width = gain1_ref.shape[1]
    half = 3 * width // 2

    def write(low_ref, high_ref):
        step = math.gcd(half, width)
        for j in range(3):
            for at in range(0, width, step):
                start = j * width + at
                ref, first = (low_ref, start) if start < half else (high_ref, start - half)
                qkv_ref[at : at + step, j * width : (j + 1) * width] = ref[first : first + step].astype(F32)

    @pl.when(me_ref[0] % 2 == 0)
    def _():
        write(own_ref, got_ref)

    @pl.when(me_ref[0] % 2 == 1)
    def _():
        write(got_ref, own_ref)

    small = read3(own_ref[half:]) + read3(got_ref[half:])
    gain1_ref[...] = small[9:10]
    gain2_ref[...] = small[8:9]
    dec_ref[...] = small[5:8]
    sums = jnp.sum(small, axis=1, keepdims=True)
    count = sums[4:5]
    rms = jnp.sqrt(sums[0:3] / (count * width))
    lane = lax.broadcasted_iota(jnp.int32, (1, 4), 1)
    out = jnp.where(lane == 0, sums[3:4] / count, 0.0)
    for j in range(3):
        out = jnp.where(lane == j + 1, rms[j : j + 1], out)
    sum_ref[...] = out


def finish(me, own, got):
    width = own.shape[1]
    smem = pl.BlockSpec(memory_space=pltpu.SMEM)
    vmem = pl.BlockSpec(memory_space=pltpu.VMEM)
    return call(
        finish_kernel,
        [sds((width, 3 * width), F32), sds((1, width), F32), sds((1, width), F32), sds((3, width), F32), sds((1, 4), F32)],
        vmem=8,
        moved=12 * 3 * width * width,
        in_specs=[smem] + [vmem] * 2,
        out_specs=[vmem] * 5,
    )(me, own, got)


AXES = ("cells", "slots")


def devices():
    return lax.axis_size("cells") * lax.axis_size("slots")


def swap(x, mask, odd=None):
    odd = mask if odd is None else odd
    return lax.ppermute(x, AXES, [(i, i ^ (odd if i % 2 else mask)) for i in range(devices())])


def routes():
    slots = lax.axis_size("slots")
    near, far = [slots, 2 * slots], []
    bit = 4 * slots
    while bit < devices():
        far.append(bit)
        bit *= 2
    small = list(zip(near[:1] + far + near[1:] + [2], near[::-1] + [2] + far))
    large = list(zip([slots, 2] + near[1:] + far, [slots, 2] + far + near[1:]))
    return small, large


def after(x, *others):
    return lax.optimization_barrier((x, *others))[0]


def per_device(
    tokens,
    valid_len,
    library,
    gene_slot,
    counts,
    norm1_gain,
    w_qkv,
    w_out,
    norm2_gain,
    w_up,
    w_down,
    w_decoder,
):
    cells, length, width = tokens.shape
    hidden = w_up.shape[1]
    slot = lax.axis_index("slots")
    cell = slot // 2
    me = jnp.full((1,), slot, jnp.int32)
    pick = lambda a: lax.dynamic_index_in_dim(a, cell, 0, keepdims=False)
    other = lambda a: lax.dynamic_index_in_dim(a, 1 - cell, 0, keepdims=False)

    came = swap(other(tokens), 2)
    near = swap(pick(tokens), 1)
    mine_counts = pick(counts)[None]
    away_counts = other(counts)[None]
    tables = (mine_counts, swap(mine_counts, 1), swap(away_counts, 2), swap(away_counts, 3))
    gain1 = norm1_gain[None]
    gain2 = norm2_gain[None]

    na, qa, ka, va, ta = qkv(me, valid_len, tokens, near, gain1, w_qkv, 0)
    came = after(came, ta, *tables)
    far = swap(came, 1)
    home, nb, gres, keep, q, kb, vb, do, cols, send, small = layer(
        me, valid_len, library, tokens, came, far, gain1, w_qkv, qa, ka, va, ta,
        gain2, w_out, w_up, w_down, w_decoder, gene_slot, tables,
    )

    route, order = routes()
    number = lax.axis_index("cells") * lax.axis_size("slots") + slot
    sides = [jnp.where(slot % 2 == 0, number // even, number // odd) % 2 for even, odd in order[:2]]

    def halve(x, side):
        n = x.shape[0] // 2
        return lax.dynamic_slice_in_dim(x, side * n, n, 0), lax.dynamic_slice_in_dim(x, (1 - side) * n, n, 0)

    def whole(own, got, side):
        return jnp.where(side == 0, jnp.concatenate([own, got], 0), jnp.concatenate([got, own], 0))

    def back(h, p, *others):
        here = after(me, *others) if others else me
        outs = attend_back(h, here, valid_len, q, do, cols, ka, kb, va, vb, p, home)
        backs.append(outs[:3])
        return outs[-1]

    got = swap(send, 1)
    backs = []
    p = back(0, None)
    main = keep + after(got, backs[0][0])
    for i in range(2):
        mine, away = halve(main, sides[i])
        got = swap(away, *order[i])
        p = back(1 + i, p, away)
        main = mine + after(got, backs[-1][0])
    got = swap(main, *order[2])
    back(3, p, main)
    main = main + after(got, backs[-1][0])
    got = swap(main, *order[3])

    keep, send = weights(after(me, main), na, nb, backs)
    final_got = swap(send, 1)
    gn_own, gn_send, three = normed_back(me, tokens, came, near, far, w_qkv, small, backs)
    rows3 = three.shape[0]
    gn_got = swap(gn_send, 1)
    final = join(keep, final_got, three)
    final_got = swap(final, *route[0])
    main = main + after(got, final)
    for masks in order[4:]:
        main = main + swap(main, *masks)
    got = swap(main, *order[1])
    mine, away = tokens_back(me, tokens, came, gain1, gres, gn_own, gn_got)
    final = merge(final, final_got, rows3)

    final_got = swap(final, *route[1])
    returned = swap(after(away, final), 2)
    main = whole(main, after(got, final), sides[1])
    final = merge(final, after(final_got, away), rows3)

    final_got = swap(final, *route[2])
    got = swap(after(main, final), *order[0])
    final = merge(final, final_got, rows3)

    for masks in route[3:-1]:
        final = merge(final, swap(final, *masks), rows3)
    final_got = swap(final, *route[-1])
    main = whole(main, after(got, final), sides[0])
    returned = after(returned, final).astype(F32)
    grad_tokens = jnp.where(cell == 0, jnp.stack([mine, returned]), jnp.stack([returned, mine]))
    g_down, g_up, g_out = unpack_main(me, main, swap(main, 1), hidden)
    final = merge(final, after(final_got, g_out, grad_tokens), rows3)
    g_qkv, g_gain1, g_gain2, g_dec, summary = finish(me, final, swap(final, 1))
    return (grad_tokens, g_gain1[0], g_qkv, g_out, g_gain2[0], g_up, g_down, g_dec, summary[0])


def solution(mesh):
    in_specs = (
        P("cells", "slots", None),
        P("cells"),
        P("cells"),
        P("cells", None),
        P("cells", "slots"),
        P(),
        P(),
        P(),
        P(),
        P(),
        P(),
        P(),
    )
    out_specs = (P("cells", "slots", None), P(), P(), P(), P(), P(), P(), P(), P())
    return jax.shard_map(
        per_device, mesh=mesh, in_specs=in_specs, out_specs=out_specs, check_vma=False
    )
```

```python
import functools
import math

import jax
import jax.numpy as jnp
from jax import lax
from jax.experimental import pallas as pl
from jax.experimental.pallas import tpu as pltpu
from jax.sharding import PartitionSpec as P

HEADS = 4
EPS = 1e-05
BACK_VMEM = 40
SMALL = 10
BF16 = jnp.bfloat16
F32 = jnp.float32
NN = (((1,), (0,)), ((), ()))
NT = (((1,), (1,)), ((), ()))
TN = (((0,), (0,)), ((), ()))
SCORE_BOUND = 60.0
ERFC_P = 0.325
ERFC_C = (
    -5.927487965082223e-05,
    0.18467549445148965,
    0.1708094188150158,
    0.2414269376514742,
    -0.07282782022580145,
    0.6147421737182138,
    -0.5684607599983035,
    0.5878333184067656,
    -0.15813953377061551,
)


def dot(a, b, dims):
    return lax.dot_general(a, b, dims, preferred_element_type=F32)


def call(kernel, out_shape, flops=0, moved=0, vmem=48, **kw):
    return pl.pallas_call(
        kernel,
        out_shape=out_shape,
        compiler_params=pltpu.CompilerParams(vmem_limit_bytes=vmem * 2**20),
        cost_estimate=pl.CostEstimate(flops=int(flops), bytes_accessed=int(moved), transcendentals=0),
        **kw,
    )


def sds(shape, dtype):
    return jax.ShapeDtypeStruct(shape, dtype)


def norm_parts(x):
    centred = x - jnp.mean(x, axis=-1, keepdims=True)
    rstd = lax.rsqrt(jnp.mean(centred * centred, axis=-1, keepdims=True) + EPS)
    return centred * rstd, rstd


def norm_back(gy, xhat, rstd, gain):
    gx = gy * gain
    first = jnp.mean(gx, axis=-1, keepdims=True)
    second = jnp.mean(gx * xhat, axis=-1, keepdims=True)
    return rstd * (gx - first - xhat * second)


def head_ones(width, lanes=None, step=None):
    rows = lax.broadcasted_iota(jnp.int32, (width, lanes or width), 0) // (width // HEADS)
    cols = lax.broadcasted_iota(jnp.int32, (width, lanes or width), 1) // (step or width // HEADS)
    return (rows == cols).astype(F32).astype(BF16)


def start_copies(pairs, sem):
    copies = [pltpu.make_async_copy(src, dst, sem.at[i]) for i, (src, dst) in enumerate(pairs)]
    for c in copies:
        c.start()
    return copies


def live_rows(me_ref, len_ref, block, length):
    place = (me_ref[0] ^ block) * length + lax.broadcasted_iota(jnp.int32, (length, 1), 0)
    return place < len_ref[me_ref[0] // 2]


def qkv_kernel(me_ref, len_ref, own_ref, pair_ref, gain_ref, w_ref, n_out, q_ref, k_ref, v_ref, top_ref, n_ref, n_sem, *, first):
    length, width = pair_ref.shape
    ones = head_ones(width)
    top_ref[...] = jnp.zeros_like(top_ref)
    for j in range(2):
        cut = slice(j * length, (j + 1) * length)
        if j == 1:
            x = pair_ref[...]
        elif first == 0:
            x = own_ref[me_ref[0] // 2]
        else:
            x = own_ref[...]
        xhat, _ = norm_parts(x.astype(F32))
        normed = (xhat * gain_ref[...]).astype(BF16)
        n_ref[cut] = normed
        live = live_rows(me_ref, len_ref, first + j, length).astype(F32).astype(BF16)
        skip = width if j == 1 else 0
        mixed = dot(normed, w_ref[:, skip:], NN).astype(BF16)
        if j == 0:
            q = mixed[:, :width] * BF16((width // HEADS) ** -0.5)
            q_ref[...] = q
            qf = q.astype(F32)
            top_ref[0:1, :] = jnp.max(dot((qf * qf).astype(BF16), ones, NN), axis=0, keepdims=True)
        k = mixed[:, width - skip : 2 * width - skip] * live
        k_ref[cut] = k
        v_ref[cut] = mixed[:, 2 * width - skip :] * live
        kf = k.astype(F32)
        top_ref[1 + j : 2 + j, :] = jnp.max(dot((kf * kf).astype(BF16), ones, NN), axis=0, keepdims=True)
    keep_n = pltpu.make_async_copy(n_ref, n_out, n_sem)
    keep_n.start()
    if first == 0:
        keep_n.wait()


def qkv(me, valid_len, own, pair, gain, w, first):
    length, width = pair.shape
    smem = pl.BlockSpec(memory_space=pltpu.SMEM)
    vmem = pl.BlockSpec(memory_space=pltpu.VMEM)
    hbm = pl.BlockSpec(memory_space=pltpu.HBM)
    rows = 2 * length
    return call(
        functools.partial(qkv_kernel, first=first),
        [
            pltpu.HBM((rows, width), BF16),
            sds((length, width), BF16),
            sds((rows, width), BF16),
            sds((rows, width), BF16),
            sds((8, width), F32),
        ],
        flops=6 * rows * width * width,
        moved=10 * rows * width,
        vmem=16,
        in_specs=[smem, smem] + [vmem] * 4,
        out_specs=[hbm] + [vmem] * 4,
        scratch_shapes=[pltpu.VMEM((rows, width), BF16), pltpu.SemaphoreType.DMA],
    )(me, valid_len, own, pair, gain, w)


def live_keys(me_ref, len_ref, keys):
    lane = lax.broadcasted_iota(jnp.int32, (1, keys), 1)
    length = keys // 4
    place = ((lane // length) ^ me_ref[0]) * length + lane % length
    return place < len_ref[me_ref[0] // 2]


def gelu_parts(x):
    down = 1.0 + (ERFC_P * math.sqrt(0.5)) * jnp.abs(x)
    t = pl.reciprocal(down, approx=True)
    t = t * (2.0 - t * down)
    poly = jnp.full_like(t, 0.5 * ERFC_C[-1])
    for c in ERFC_C[-2::-1]:
        poly = poly * t + 0.5 * c
    bell = jnp.exp2((x * x) * (-0.5 * math.log2(math.e)))
    tail = poly * bell
    cdf = jnp.where(x >= 0, 1.0 - tail, tail)
    return x * cdf, cdf + (x * (1.0 / math.sqrt(2.0 * math.pi))) * bell


def gamma_parts(x):
    large = x > 16.0
    small = jnp.minimum(x, 16.0)
    w = small * (small + 7.0)
    a, b, c = w + 6.0, w + 10.0, w + 12.0
    log_prod = jnp.log(w * a * (b * c))
    sum_inv = (2.0 * small + 7.0) * (1.0 / w + 1.0 / a + 1.0 / b + 1.0 / c)
    big = jnp.where(large, x, x + 8.0)
    log_big = jnp.log(big)
    inv = 1.0 / big
    inv2 = inv * inv
    lg = (big - 0.5) * log_big - big + 0.5 * math.log(2.0 * math.pi)
    lg = lg + inv * (1.0 / 12.0 - inv2 * (1.0 / 360.0 - inv2 * (1.0 / 1260.0)))
    dg = log_big - 0.5 * inv - inv2 * (1.0 / 12.0 - inv2 * (1.0 / 120.0 - inv2 * (1.0 / 252.0)))
    return jnp.where(large, lg, lg - log_prod), jnp.where(large, dg, dg - sum_inv)


def softplus(x):
    return jnp.maximum(x, 0.0) + jnp.log(1.0 + jnp.exp(-jnp.abs(x)))


def sigmoid(x):
    return 1.0 / (1.0 + jnp.exp(-x))


def zinb(m, t, p, y, scale):
    rate = scale * (softplus(m) + 0.05)
    theta = softplus(t) + 0.05
    total = theta + rate
    inv_total = 1.0 / total
    log_total = jnp.log(total)
    log_theta = jnp.log(theta)
    z0 = theta * (log_theta - log_total)
    pi = sigmoid(p)
    e0 = jnp.exp(z0)
    den = pi + (1.0 - pi) * e0
    inv_den = 1.0 / den
    some = y > 0
    yf = y.astype(F32)
    lg_sum, dg_sum = gamma_parts(yf + theta)
    lg_theta, dg_theta = gamma_parts(theta)
    lg_y, _ = gamma_parts(yf + 1.0)
    log_nb = lg_sum - lg_theta - lg_y + z0 + yf * (jnp.log(rate) - log_total)
    nll = jnp.where(some, softplus(p) - log_nb, -jnp.log(den))
    g_z0 = jnp.where(some, -1.0, -(1.0 - pi) * e0 * inv_den)
    share = theta * inv_total
    g_theta = g_z0 * (log_theta - log_total + 1.0 - share)
    g_theta = g_theta + jnp.where(some, dg_theta - dg_sum + yf * inv_total, 0.0)
    g_rate = jnp.where(some, yf * (inv_total - 1.0 / rate), 0.0) - g_z0 * share
    g_p = jnp.where(some, pi, -(1.0 - e0) * inv_den * pi * (1.0 - pi))
    return nll, g_rate * scale * sigmoid(m), g_theta * sigmoid(t), g_p


def split2(x):
    high = x.astype(BF16)
    return high, (x - high.astype(F32)).astype(BF16)


def layer_kernel(me_ref, len_ref, lib_ref, xa_ref, xb_ref, pb_ref, gain1_ref, w_ref, qa_ref, ka_ref, va_ref, ta_ref,
                 gain_ref, w_out_ref, w_up_ref, w_down_ref, w_dec_ref, gene_ref, c0_ref, c1_ref, c2_ref, c3_ref,
                 p_ref, nb_ref, gres_out, keep_out, q_s, kb_ref, vb_ref, do_ref, cols_ref, send_ref,
                 small_ref,
                 nb_s, nb_sem, gres_ref, keep_ref, out_sem, qb_ref, tb_ref, cols_s, x_s, p_s, p_sem, gt_s, aug_s, o_s, linv_s, res_s, n2_s, act_s, gp_s, dec_s, gd_s, w_s, table_s, ga_down, ga_up, ga_out,
                 *, block, tall):
    part, width = ka_ref.shape
    keys = 2 * part
    length = part // 2
    rows = part
    hidden = w_up_ref.shape[1]
    pair = 2 * (width // HEADS)
    half = pair // 2
    pairs = HEADS // 2
    me = me_ref[0]
    cell = me // 2
    valid_len = len_ref[cell]
    gain = gain_ref[...]
    small_ref[...] = jnp.zeros_like(small_ref)
    ga_down[...] = jnp.zeros_like(ga_down)
    ga_up[...] = jnp.zeros_like(ga_up)
    ga_out[...] = jnp.zeros_like(ga_out)
    lane = lax.broadcasted_iota(jnp.int32, (1, pair), 1)

    def rowsum(a):
        return jnp.sum(a, axis=0, keepdims=True)

    qkv_kernel(me_ref, len_ref, xb_ref, pb_ref, gain1_ref, w_ref, nb_ref, qb_ref, kb_ref, vb_ref, tb_ref, nb_s, nb_sem, first=2)

    live = live_keys(me_ref, len_ref, keys)
    mask = jnp.transpose(jnp.broadcast_to(live.astype(F32), (pair, keys))).astype(BF16)
    for j, ref in enumerate((va_ref, vb_ref)):
        cut = slice(j * part, (j + 1) * part)
        for g in range(pairs):
            v = ref[:, g * pair : (g + 1) * pair]
            aug_s[2 * g, cut] = jnp.where(lane < half, v, mask[cut])
            aug_s[2 * g + 1, cut] = jnp.where(lane < half, mask[cut], v)

    top_q = jnp.maximum(ta_ref[0:1], tb_ref[0:1])
    top_k = jnp.maximum(jnp.maximum(ta_ref[1:2], tb_ref[1:2]), jnp.maximum(ta_ref[2:3], tb_ref[2:3]))
    plain = jnp.max(top_q * top_k) * 1.05 < SCORE_BOUND * SCORE_BOUND

    q_s[0:length] = qa_ref[...]
    q_s[length:rows] = qb_ref[...]
    x_s[0:length] = xa_ref[cell]
    x_s[length:rows] = xb_ref[...]

    def copy(b, g):
        slot = (b * pairs + g) % 2
        rcut = pl.ds(pl.multiple_of(b * block, block), block)
        return pltpu.make_async_copy(p_s.at[slot], p_ref.at[pl.ds(2 * g, 2), rcut], p_sem.at[slot])

    def attend_block(b, g, safe):
        cut = pl.ds(pl.multiple_of(b * block, block), block)
        cols = slice(g * pair, (g + 1) * pair)
        slot = (b * pairs + g) % 2
        q = q_s[cut, cols]
        zero = jnp.zeros_like(q)
        outs = []
        for h in range(2):
            home = p_s.at[slot, h]
            qh = jnp.where(lane < half, q, zero) if h == 0 else jnp.where(lane < half, zero, q)
            if safe:
                s = jnp.concatenate([dot(qh, ref[:, cols], NT) for ref in (ka_ref, kb_ref)], axis=1)
                s = jnp.where(live, s, -1e30)
                p = jnp.exp(s - jnp.max(s, axis=1, keepdims=True)).astype(BF16)
                home[...] = p
                total = dot(p, aug_s[2 * g + h], NN)
            else:
                total = None
                for j, ref in enumerate((ka_ref, kb_ref)):
                    kcut = slice(j * part, (j + 1) * part)
                    p = jnp.exp(dot(qh, ref[:, cols], NT)).astype(BF16)
                    home[:, kcut] = p
                    o = dot(p, aug_s[2 * g + h, kcut], NN)
                    total = o if total is None else total + o
            outs.append(total)
        up = jnp.where(lane < half, outs[0], outs[1])
        down = pltpu.roll(jnp.where(lane < half, outs[1], outs[0]), half, 1)
        inverse = 1.0 / down
        o_s[cut, cols] = up * inverse
        linv_s[cut, cols] = inverse

    @pl.loop(0, rows // block)
    def _(b):
        for g in range(pairs):

            @pl.when(b > 0)
            def _():
                copy(b - 1, g).wait()

            pl.when(plain)(functools.partial(attend_block, b, g, False))
            pl.when(jnp.logical_not(plain))(functools.partial(attend_block, b, g, True))
            copy(b, g).start()

    @pl.loop(0, rows // tall)
    def _(b):
        start = pl.multiple_of(b * tall, tall)
        cut = pl.ds(start, tall)
        base = jnp.where(start < length, me * length + start, (me ^ 2) * length + start - length)
        valid = (base + lax.broadcasted_iota(jnp.int32, (tall, 1), 0) < valid_len).astype(F32)
        attn_out = dot(o_s[cut].astype(BF16), w_out_ref[...], NN)
        resid = x_s[cut].astype(F32) + attn_out
        res_s[cut] = resid
        xhat, _ = norm_parts(resid)
        normed = (xhat * gain).astype(BF16)
        n2_s[cut] = normed
        act, slope = gelu_parts(dot(normed, w_up_ref[...], NN))
        act = act.astype(BF16)
        act_s[cut] = act
        gp_s[cut] = slope
        mlp_out = dot(act, w_down_ref[...], NN)
        final = resid + mlp_out
        dec_s[cut] = final.astype(BF16)
        small_ref[0:1, :] += rowsum(valid * final * final)
        small_ref[1:2, :] += rowsum(valid * attn_out * attn_out)
        small_ref[2:3, :] += rowsum(valid * mlp_out * mlp_out)

    w_s[...] = jnp.zeros_like(w_s)
    w_s[0:3, :] = w_dec_ref[...].astype(F32)
    w_s[3:6, :] = w_dec_ref[...].astype(F32)
    w_twice = w_s[...].astype(BF16)
    decoded = dot(w_twice, dec_s[...], NT)
    for j, ref in enumerate((c0_ref, c1_ref, c2_ref, c3_ref)):
        for i in range(length // 128):
            table_s[j * (length // 128) + i : j * (length // 128) + i + 1, :] = ref[:, i * 128 : (i + 1) * 128].astype(F32)
    starts = (me * length, (me ^ 2) * length)
    gene = jnp.concatenate([gene_ref[pl.ds(cell, 1), pl.ds(pl.multiple_of(a, length), length)] for a in starts], axis=1)
    gene = ((gene // length) ^ me) * length + gene % length
    high = (lax.broadcasted_iota(jnp.int32, (table_s.shape[0], rows), 0) == gene // 128).astype(F32).astype(BF16)
    found = dot(table_s[...].astype(BF16), high, TN)
    low = lax.broadcasted_iota(jnp.int32, (128, rows), 0) == gene % 128
    observed = rowsum(jnp.where(low, found, 0.0))
    lane = lax.broadcasted_iota(jnp.int32, (1, rows), 1)
    places = jnp.where(lane < length, starts[0] + lane, starts[1] + lane - length)
    valid = (places < valid_len).astype(F32)
    scale = lib_ref[cell].astype(F32) / (4 * length)
    nll, g_m, g_t, g_p = zinb(decoded[0:1], decoded[1:2], decoded[2:3], observed, scale)
    nll = nll * valid
    for j in range(rows // width):
        small_ref[3:4, :] += nll[:, j * width : (j + 1) * width]
        small_ref[4:5, :] += valid[:, j * width : (j + 1) * width]
    gd_s[...] = jnp.zeros_like(gd_s)
    for j, g in enumerate((g_m, g_t, g_p)):
        gh, gl = split2(g * valid)
        gd_s[j : j + 1, :] = gh.astype(F32)
        gd_s[3 + j : 4 + j, :] = gl.astype(F32)
    gd = gd_s[...].astype(BF16)
    gw = dot(gd, dec_s[...], NN)
    small_ref[5:8, :] = gw[0:3] + gw[3:6]

    cols_s[...] = jnp.zeros_like(cols_s)
    heads = head_ones(width, 128, 1)
    for j in range(rows // tall):
        gt_s[j * 16 : (j + 1) * 16] = gd[:, j * tall : (j + 1) * tall]

    @pl.loop(0, rows // tall)
    def _(b):
        cut = pl.ds(pl.multiple_of(b * tall, tall), tall)
        g_final = dot(gt_s[pl.ds(pl.multiple_of(b * 16, 16), 16)], w_twice, TN).astype(BF16)
        ga_down[...] += dot(act_s[cut], g_final, TN)
        g_up = (dot(g_final, w_down_ref[...], NT) * gp_s[cut]).astype(BF16)
        ga_up[...] += dot(n2_s[cut], g_up, TN)
        g_normed = dot(g_up, w_up_ref[...], NT)
        xhat, rstd = norm_parts(res_s[cut])
        small_ref[8:9, :] += rowsum(g_normed * xhat)
        g_res = g_final.astype(F32) + norm_back(g_normed, xhat, rstd, gain)
        gres_ref[cut] = g_res
        g_attn = g_res.astype(BF16)
        o = o_s[cut]
        linv = linv_s[cut]
        ga_out[...] += dot(o.astype(BF16), g_attn, TN)
        do = dot(g_attn, w_out_ref[...], NT).astype(BF16)
        do_ref[cut] = do
        dof = do.astype(F32)
        ph, pl_ = split2(dof * o)
        cols_s[:, 0:HEADS] = (dot(ph, heads, NN) + dot(pl_, heads, NN))[:, 0:HEADS]
        for h in range(HEADS):
            cols_s[:, HEADS + h : HEADS + h + 1] = linv[:, h * half : h * half + 1]
        cols_ref[:, cut] = jnp.transpose(cols_s[...])[0 : 2 * HEADS]

    gres_copy = pltpu.make_async_copy(gres_ref, gres_out, out_sem.at[0])
    gres_copy.start()
    for g in range(pairs):
        copy(rows // block - 1, g).wait()
    pltpu.make_async_copy(nb_s, nb_ref, nb_sem).wait()

    def write(low_ref, high_ref):
        pieces = [ga_down[...]]
        pieces += [ga_up[:, j * width : (j + 1) * width] for j in range(hidden // width)]
        pieces += [ga_out[...]]
        at = 0
        half = low_ref.shape[0]
        for piece in pieces:
            n = piece.shape[0]
            first = max(0, min(n, half - at))
            if first:
                low_ref[at : at + first, :] = piece[:first].astype(BF16)
            if first < n:
                high_ref[at + first - half : at + n - half, :] = piece[first:].astype(BF16)
            at += n

    @pl.when(me % 2 == 0)
    def _():
        write(keep_ref, send_ref)

    @pl.when(me % 2 == 1)
    def _():
        write(send_ref, keep_ref)

    keep_copy = pltpu.make_async_copy(keep_ref, keep_out, out_sem.at[1])
    keep_copy.start()
    gres_copy.wait()
    keep_copy.wait()


def layer(me, valid_len, library, xa, xb, pb, gain1, w, qa, ka, va, ta, gain, w_out, w_up, w_down, w_dec, gene, tables, block=256, tall=512):
    part, width = ka.shape
    rows, keys, length = part, 2 * part, part // 2
    hidden = w_up.shape[1]
    pair = 2 * (width // HEADS)
    smem = pl.BlockSpec(memory_space=pltpu.SMEM)
    vmem = pl.BlockSpec(memory_space=pltpu.VMEM)
    half = (2 * hidden + width) // 2
    return call(
        functools.partial(layer_kernel, block=block, tall=tall),
        [
            pltpu.HBM((HEADS, rows, keys), BF16),
            pltpu.HBM((part, width), BF16),
            pltpu.HBM((rows, width), F32),
            pltpu.HBM((half, width), BF16),
            sds((rows, width), BF16),
            sds((part, width), BF16),
            sds((part, width), BF16),
            sds((rows, width), BF16),
            sds((2 * HEADS, rows), F32),
            sds((half, width), BF16),
            sds((16, width), F32),
        ],
        flops=24 * rows * width * hidden + 16 * rows * keys * width,
        vmem=46,
        in_specs=[smem] * 3 + [vmem] * 19,
        out_specs=[pl.BlockSpec(memory_space=pltpu.HBM)] * 4 + [vmem] * 7,
        scratch_shapes=[
            pltpu.VMEM((part, width), BF16),
            pltpu.SemaphoreType.DMA,
            pltpu.VMEM((rows, width), F32),
            pltpu.VMEM((half, width), BF16),
            pltpu.SemaphoreType.DMA((2,)),
            pltpu.VMEM((length, width), BF16),
            pltpu.VMEM((8, width), F32),
            pltpu.VMEM((tall, 128), F32),
            pltpu.VMEM((rows, width), BF16),
            pltpu.VMEM((2, 2, block, keys), BF16),
            pltpu.SemaphoreType.DMA((2,)),
            pltpu.VMEM((16 * rows // tall, tall), BF16),
            pltpu.VMEM((HEADS, keys, pair), BF16),
            pltpu.VMEM((rows, width), F32),
            pltpu.VMEM((rows, width), F32),
            pltpu.VMEM((rows, width), F32),
            pltpu.VMEM((rows, width), BF16),
            pltpu.VMEM((rows, hidden), BF16),
            pltpu.VMEM((rows, hidden), F32),
            pltpu.VMEM((rows, width), BF16),
            pltpu.VMEM((16, rows), F32),
            pltpu.VMEM((16, width), F32),
            pltpu.VMEM((rows // 64, 128), F32),
            pltpu.VMEM((hidden, width), F32),
            pltpu.VMEM((width, hidden), F32),
            pltpu.VMEM((width, width), F32),
        ],
    )(me, valid_len, library, xa, xb, pb, gain1, w, qa, ka, va, ta, gain, w_out, w_up, w_down, w_dec, gene, *tables)


def attend_back_kernel(me_ref, len_ref, q_ref, do_ref, cols_ref, ka_ref, kb_ref, va_ref, vb_ref, *refs, head, block, chunk):
    refs = list(refs)
    first, following = head == 0, head + 1 < HEADS
    p_ref = None if first else refs.pop(0)
    home_ref = refs.pop(0) if following else None
    dq_ref, dk_ref, dv_ref = refs[:3]
    next_ref = refs[3] if following else None
    ak_ref, av_ref = refs[3 + following : 5 + following]
    copies = []
    if first:
        p_ref, p_sem = refs[6:8]
        cuts = [slice(i, i + block) for i in range(0, do_ref.shape[0], block)]
        copies = start_copies([(home_ref.at[0, cut], p_ref.at[cut]) for cut in cuts], p_sem)
    if following:
        fetch = pltpu.make_async_copy(home_ref.at[head + 1], next_ref, refs[-1])
        fetch.start()
    part, width = ka_ref.shape
    keys = 2 * part
    rows = do_ref.shape[0]
    half = width // HEADS
    pair = 2 * half
    lane = lax.broadcasted_iota(jnp.int32, (1, pair), 1)
    lo = (head % 2) * half
    own = (lane < half) if head % 2 == 0 else (lane >= half)
    at0 = head // 2 * pair
    cols = slice(at0, at0 + pair)
    mine = slice(at0 + lo, at0 + lo + half)
    for b in range(rows // block):
        cut = slice(b * block, (b + 1) * block)
        q = q_ref[cut, mine]
        do = do_ref[cut, cols]
        do = jnp.where(own, do, jnp.zeros_like(do))
        both = jnp.transpose(cols_ref[:, cut])
        delta = both[:, head : head + 1]
        linv = both[:, HEADS + head : HEADS + head + 1]
        dl = (do_ref[cut, mine].astype(F32) * linv).astype(BF16)
        if first:
            copies[b].wait()
        total = None
        for c in range(keys // chunk):
            kcut = slice(c * chunk, (c + 1) * chunk)
            k_ref, v_ref = (ka_ref, va_ref) if c * chunk < part else (kb_ref, vb_ref)
            kat = c * chunk % part
            kc = k_ref[kat : kat + chunk, cols]
            dp = dot(do, v_ref[kat : kat + chunk, cols], NT)
            pc = p_ref[cut, kcut]
            ds = (pc.astype(F32) * ((dp - delta) * linv)).astype(BF16)
            step = dot(ds, kc, NN)
            total = step if total is None else total + step
            dv = dot(dl, pc, TN)
            dk = dot(q, ds, TN)
            if b == 0:
                av_ref[:, kcut] = dv
                ak_ref[:, kcut] = dk
            else:
                av_ref[:, kcut] += dv
                ak_ref[:, kcut] += dk
        dq_ref[cut] = (jnp.where(own, total, 0.0) * half**-0.5).astype(BF16)
    live = live_keys(me_ref, len_ref, keys)
    dk_ref[...] = jnp.where(live, ak_ref[...], 0.0).astype(BF16)
    dv_ref[...] = jnp.where(live, av_ref[...], 0.0).astype(BF16)
    if following:
        fetch.wait()


def attend_back(head, me, valid_len, q, do, cols, ka, kb, va, vb, p, home, block=512, chunk=512):
    rows = do.shape[0]
    part, width = ka.shape
    keys = 2 * part
    pair = 2 * (width // HEADS)
    smem = pl.BlockSpec(memory_space=pltpu.SMEM)
    vmem = pl.BlockSpec(memory_space=pltpu.VMEM)
    first, following = head == 0, head + 1 < HEADS
    return call(
        functools.partial(attend_back_kernel, head=head, block=block, chunk=chunk),
        [sds((rows, pair), BF16), sds((pair // 2, keys), BF16), sds((pair // 2, keys), BF16)]
        + [sds((rows, keys), BF16)] * following,
        flops=8 * rows * keys * width,
        moved=2 * rows * keys,
        vmem=BACK_VMEM,
        in_specs=[smem, smem] + [vmem] * (7 + (not first)) + [pl.BlockSpec(memory_space=pltpu.HBM)] * following,
        out_specs=[vmem] * (3 + following),
        scratch_shapes=[pltpu.VMEM((pair // 2, keys), F32), pltpu.VMEM((pair // 2, keys), F32)]
        + [pltpu.VMEM((rows, keys), BF16), pltpu.SemaphoreType.DMA((rows // block,))] * first
        + [pltpu.SemaphoreType.DMA] * following,
    )(me, valid_len, q, do, cols, ka, kb, va, vb, *([] if first else [p]), *([home] * following))


def weights_kernel(me_ref, na_ref, nb_ref, *refs):
    keep_ref, send_ref = refs[-2:]
    heads = [refs[3 * h : 3 * h + 3] for h in range(HEADS)]
    part, width = na_ref.shape
    length = part // 2
    dim = width // HEADS
    dq = sum(h[0][...].astype(F32) for h in heads[:2]), sum(h[0][...].astype(F32) for h in heads[2:])
    dq = jnp.concatenate(dq, axis=1).astype(BF16)
    gq = dot(na_ref[:length], dq[:length], TN) + dot(nb_ref[:length], dq[length:], TN)
    outs = [gq]
    for j in (1, 2):
        d = jnp.concatenate([h[j][...] for h in heads], axis=0)
        g = dot(d[:, :part], na_ref[...], NN) + dot(d[:, part:], nb_ref[...], NN)
        outs.append(jnp.transpose(g))
    half = 3 * width // 2

    def write(low_ref, high_ref):
        at = 0
        for piece in outs:
            first = max(0, min(width, half - at))
            if first:
                low_ref[at : at + first, :] = piece[:first].astype(BF16)
            if first < width:
                high_ref[at + first - half : at + width - half, :] = piece[first:].astype(BF16)
            at += width

    @pl.when(me_ref[0] % 2 == 0)
    def _():
        write(keep_ref, send_ref)

    @pl.when(me_ref[0] % 2 == 1)
    def _():
        write(send_ref, keep_ref)


def weights(me, na, nb, back):
    part, width = na.shape
    half = 3 * width // 2
    smem = pl.BlockSpec(memory_space=pltpu.SMEM)
    vmem = pl.BlockSpec(memory_space=pltpu.VMEM)
    return call(
        weights_kernel,
        [sds((half, width), BF16)] * 2,
        vmem=16,
        flops=10 * part * width * width,
        moved=16 * part * width,
        in_specs=[smem] + [vmem] * (2 + 3 * HEADS),
        out_specs=[vmem] * 2,
    )(me, na, nb, *[a for b in back for a in b])


def write3(ref, x):
    n = x.shape[0]
    high = x.astype(BF16).astype(F32)
    rest = x - high
    mid = rest.astype(BF16).astype(F32)
    pad = jnp.zeros((ref.shape[0] - 3 * n, x.shape[1]), F32)
    ref[...] = jnp.concatenate([high, mid, rest - mid, pad], axis=0).astype(BF16)


def read3(x):
    n = SMALL
    x = x[: 3 * n].astype(F32)
    return x[:n] + x[n : 2 * n] + x[2 * n :]


def normed_kernel(me_ref, xa_ref, xb_ref, pa_ref, pb_ref, w_ref, small_ref, *refs):
    own_ref, send_ref, three_ref = refs[-3:]
    heads = [refs[3 * h : 3 * h + 3] for h in range(HEADS)]
    length, width = xb_ref.shape
    cell = me_ref[0] // 2
    tt = (((0,), (1,)), ((), ()))
    w = w_ref[...]
    dq = sum(h[0][...].astype(F32) for h in heads[:2]), sum(h[0][...].astype(F32) for h in heads[2:])
    dq = jnp.concatenate(dq, axis=1).astype(BF16)
    dk = jnp.concatenate([h[1][...] for h in heads], axis=0)
    dv = jnp.concatenate([h[2][...] for h in heads], axis=0)
    total = jnp.zeros((1, width), F32)
    for b in range(4):
        cut = slice(b * length, (b + 1) * length)
        gn = dot(dk[:, cut], w[:, width : 2 * width], tt) + dot(dv[:, cut], w[:, 2 * width :], tt)
        at = slice(b // 2 * length, (b // 2 + 1) * length)
        if b % 2 == 0:
            gn += dot(dq[at], w[:, :width], NT)
        x = xa_ref[cell] if b == 0 else (pa_ref, xb_ref, pb_ref)[b - 1][...]
        xhat, _ = norm_parts(x.astype(F32))
        total += jnp.sum(gn * xhat, axis=0, keepdims=True)
        if b % 2 == 0:
            own_ref[at] = gn
        else:
            send_ref[at] = gn.astype(BF16)
    write3(three_ref, jnp.concatenate([small_ref[0 : SMALL - 1], total], axis=0))


def normed_back(me, xa, xb, pa, pb, w, small, back):
    length, width = xb.shape
    rows = 2 * length
    smem = pl.BlockSpec(memory_space=pltpu.SMEM)
    vmem = pl.BlockSpec(memory_space=pltpu.VMEM)
    return call(
        normed_kernel,
        [sds((rows, width), F32), sds((rows, width), BF16), sds((32, width), BF16)],
        vmem=24,
        flops=12 * rows * width * width,
        moved=16 * rows * width,
        in_specs=[smem] + [vmem] * (6 + 3 * HEADS),
        out_specs=[vmem] * 3,
    )(me, xa, xb, pa, pb, w, small, *[a for b in back for a in b])


def tokens_kernel(me_ref, xa_ref, xb_ref, gain_ref, gres_ref, own_ref, got_ref, mine_ref, back_ref):
    length = mine_ref.shape[0]
    for b in range(2):
        cut = slice(b * length, (b + 1) * length)
        x = xa_ref[me_ref[0] // 2] if b == 0 else xb_ref[...]
        xhat, rstd = norm_parts(x.astype(F32))
        gn = own_ref[cut] + got_ref[cut].astype(F32)
        g = gres_ref[cut] + norm_back(gn, xhat, rstd, gain_ref[...])
        if b == 0:
            mine_ref[...] = g
        else:
            back_ref[...] = g.astype(BF16)


def tokens_back(me, xa, xb, gain, gres, own, got):
    length, width = xb.shape
    smem = pl.BlockSpec(memory_space=pltpu.SMEM)
    vmem = pl.BlockSpec(memory_space=pltpu.VMEM)
    return call(
        tokens_kernel,
        [sds((length, width), F32), sds((length, width), BF16)],
        vmem=12,
        flops=60 * length * width,
        moved=24 * length * width,
        in_specs=[smem] + [vmem] * 6,
        out_specs=[vmem] * 2,
    )(me, xa, xb, gain, gres, own, got)


def join_kernel(a_ref, b_ref, three_ref, o_ref):
    n = a_ref.shape[0]
    o_ref[:n] = (a_ref[...].astype(F32) + b_ref[...].astype(F32)).astype(BF16)
    o_ref[n:] = three_ref[...]


def merge_kernel(a_ref, b_ref, o_ref, *, small):
    n = a_ref.shape[0] - small
    o_ref[:n] = (a_ref[:n].astype(F32) + b_ref[:n].astype(F32)).astype(BF16)
    write3(o_ref.at[n:], read3(a_ref[n:]) + read3(b_ref[n:]))


def join(a, b, three):
    vmem = pl.BlockSpec(memory_space=pltpu.VMEM)
    shape = (a.shape[0] + three.shape[0], a.shape[1])
    return call(join_kernel, sds(shape, BF16), moved=6 * a.size, vmem=4, in_specs=[vmem] * 3, out_specs=vmem)(a, b, three)


def merge(a, b, small):
    vmem = pl.BlockSpec(memory_space=pltpu.VMEM)
    kernel = functools.partial(merge_kernel, small=small)
    return call(kernel, sds(a.shape, BF16), moved=6 * a.size, vmem=4, in_specs=[vmem] * 2, out_specs=vmem)(a, b)


def unpack_main_kernel(me_ref, own_ref, got_ref, down_ref, up_ref, out_ref):
    hidden, width = down_ref.shape

    def write(low_ref, high_ref):
        half = low_ref.shape[0]

        def rows(start, stop):
            if stop <= half:
                return low_ref[start:stop].astype(F32)
            return high_ref[start - half : stop - half].astype(F32)

        step = math.gcd(half, width)
        for at in range(0, hidden, step):
            down_ref[at : at + step] = rows(at, at + step)
        for j in range(hidden // width):
            for at in range(0, width, step):
                start = hidden + j * width + at
                up_ref[at : at + step, j * width : (j + 1) * width] = rows(start, start + step)
        for at in range(0, width, step):
            out_ref[at : at + step] = rows(2 * hidden + at, 2 * hidden + at + step)

    @pl.when(me_ref[0] % 2 == 0)
    def _():
        write(own_ref, got_ref)

    @pl.when(me_ref[0] % 2 == 1)
    def _():
        write(got_ref, own_ref)


def unpack_main(me, own, got, hidden):
    width = own.shape[1]
    smem = pl.BlockSpec(memory_space=pltpu.SMEM)
    vmem = pl.BlockSpec(memory_space=pltpu.VMEM)
    return call(
        unpack_main_kernel,
        [sds((hidden, width), F32), sds((width, hidden), F32), sds((width, width), F32)],
        vmem=12,
        moved=12 * hidden * width,
        in_specs=[smem, vmem, vmem],
        out_specs=[vmem] * 3,
    )(me, own, got)


def finish_kernel(me_ref, own_ref, got_ref, qkv_ref, gain1_ref, gain2_ref, dec_ref, sum_ref):
    width = gain1_ref.shape[1]
    half = 3 * width // 2

    def write(low_ref, high_ref):
        step = math.gcd(half, width)
        for j in range(3):
            for at in range(0, width, step):
                start = j * width + at
                ref, first = (low_ref, start) if start < half else (high_ref, start - half)
                qkv_ref[at : at + step, j * width : (j + 1) * width] = ref[first : first + step].astype(F32)

    @pl.when(me_ref[0] % 2 == 0)
    def _():
        write(own_ref, got_ref)

    @pl.when(me_ref[0] % 2 == 1)
    def _():
        write(got_ref, own_ref)

    small = read3(own_ref[half:]) + read3(got_ref[half:])
    gain1_ref[...] = small[9:10]
    gain2_ref[...] = small[8:9]
    dec_ref[...] = small[5:8]
    sums = jnp.sum(small, axis=1, keepdims=True)
    count = sums[4:5]
    rms = jnp.sqrt(sums[0:3] / (count * width))
    lane = lax.broadcasted_iota(jnp.int32, (1, 4), 1)
    out = jnp.where(lane == 0, sums[3:4] / count, 0.0)
    for j in range(3):
        out = jnp.where(lane == j + 1, rms[j : j + 1], out)
    sum_ref[...] = out


def finish(me, own, got):
    width = own.shape[1]
    smem = pl.BlockSpec(memory_space=pltpu.SMEM)
    vmem = pl.BlockSpec(memory_space=pltpu.VMEM)
    return call(
        finish_kernel,
        [sds((width, 3 * width), F32), sds((1, width), F32), sds((1, width), F32), sds((3, width), F32), sds((1, 4), F32)],
        vmem=8,
        moved=12 * 3 * width * width,
        in_specs=[smem] + [vmem] * 2,
        out_specs=[vmem] * 5,
    )(me, own, got)


AXES = ("cells", "slots")


def devices():
    return lax.axis_size("cells") * lax.axis_size("slots")


def swap(x, mask, odd=None):
    odd = mask if odd is None else odd
    return lax.ppermute(x, AXES, [(i, i ^ (odd if i % 2 else mask)) for i in range(devices())])


def routes():
    slots = lax.axis_size("slots")
    near, far = [slots, 2 * slots], []
    bit = 4 * slots
    while bit < devices():
        far.append(bit)
        bit *= 2
    small = list(zip(near[:1] + far + near[1:] + [2], near[::-1] + [2] + far))
    large = list(zip([slots, 2] + near[1:] + far, [slots, 2] + far + near[1:]))
    return small, large


def after(x, *others):
    return lax.optimization_barrier((x, *others))[0]


def per_device(
    tokens,
    valid_len,
    library,
    gene_slot,
    counts,
    norm1_gain,
    w_qkv,
    w_out,
    norm2_gain,
    w_up,
    w_down,
    w_decoder,
):
    cells, length, width = tokens.shape
    hidden = w_up.shape[1]
    slot = lax.axis_index("slots")
    cell = slot // 2
    me = jnp.full((1,), slot, jnp.int32)
    pick = lambda a: lax.dynamic_index_in_dim(a, cell, 0, keepdims=False)
    other = lambda a: lax.dynamic_index_in_dim(a, 1 - cell, 0, keepdims=False)

    came = swap(other(tokens), 2)
    near = swap(pick(tokens), 1)
    mine_counts = pick(counts)[None]
    away_counts = other(counts)[None]
    tables = (mine_counts, swap(mine_counts, 1), swap(away_counts, 2), swap(away_counts, 3))
    gain1 = norm1_gain[None]
    gain2 = norm2_gain[None]

    na, qa, ka, va, ta = qkv(me, valid_len, tokens, near, gain1, w_qkv, 0)
    came = after(came, ta, *tables)
    far = swap(came, 1)
    home, nb, gres, keep, q, kb, vb, do, cols, send, small = layer(
        me, valid_len, library, tokens, came, far, gain1, w_qkv, qa, ka, va, ta,
        gain2, w_out, w_up, w_down, w_decoder, gene_slot, tables,
    )

    route, order = routes()
    number = lax.axis_index("cells") * lax.axis_size("slots") + slot
    sides = [jnp.where(slot % 2 == 0, number // even, number // odd) % 2 for even, odd in order[:2]]

    def halve(x, side):
        n = x.shape[0] // 2
        return lax.dynamic_slice_in_dim(x, side * n, n, 0), lax.dynamic_slice_in_dim(x, (1 - side) * n, n, 0)

    def whole(own, got, side):
        return jnp.where(side == 0, jnp.concatenate([own, got], 0), jnp.concatenate([got, own], 0))

    def back(h, p, *others):
        here = after(me, *others) if others else me
        outs = attend_back(h, here, valid_len, q, do, cols, ka, kb, va, vb, p, home)
        backs.append(outs[:3])
        return outs[-1]

    got = swap(send, 1)
    backs = []
    p = back(0, None)
    main = keep + after(got, backs[0][0])
    for i in range(2):
        mine, away = halve(main, sides[i])
        got = swap(away, *order[i])
        p = back(1 + i, p, away)
        main = mine + after(got, backs[-1][0])
    got = swap(main, *order[2])
    back(3, p, main)
    main = main + after(got, backs[-1][0])
    got = swap(main, *order[3])

    keep, send = weights(after(me, main), na, nb, backs)
    final_got = swap(send, 1)
    gn_own, gn_send, three = normed_back(me, tokens, came, near, far, w_qkv, small, backs)
    rows3 = three.shape[0]
    gn_got = swap(gn_send, 1)
    final = join(keep, final_got, three)
    final_got = swap(final, *route[0])
    main = main + after(got, final)
    for masks in order[4:]:
        main = main + swap(main, *masks)
    got = swap(main, *order[1])
    mine, away = tokens_back(me, tokens, came, gain1, gres, gn_own, gn_got)
    final = merge(final, final_got, rows3)

    final_got = swap(final, *route[1])
    returned = swap(after(away, final), 2)
    main = whole(main, after(got, final), sides[1])
    final = merge(final, after(final_got, away), rows3)

    final_got = swap(final, *route[2])
    got = swap(after(main, final), *order[0])
    final = merge(final, final_got, rows3)

    for masks in route[3:-1]:
        final = merge(final, swap(final, *masks), rows3)
    final_got = swap(final, *route[-1])
    main = whole(main, after(got, final), sides[0])
    returned = after(returned, final).astype(F32)
    grad_tokens = jnp.where(cell == 0, jnp.stack([mine, returned]), jnp.stack([returned, mine]))
    main_got = swap(main, 1)
    final = merge(final, after(final_got, grad_tokens), rows3)
    g_qkv, g_gain1, g_gain2, g_dec, summary = finish(me, final, swap(final, 1))
    g_down, g_up, g_out = unpack_main(after(me, summary), main, main_got, hidden)
    return (grad_tokens, g_gain1[0], g_qkv, g_out, g_gain2[0], g_up, g_down, g_dec, summary[0])


def solution(mesh):
    in_specs = (
        P("cells", "slots", None),
        P("cells"),
        P("cells"),
        P("cells", None),
        P("cells", "slots"),
        P(),
        P(),
        P(),
        P(),
        P(),
        P(),
        P(),
    )
    out_specs = (P("cells", "slots", None), P(), P(), P(), P(), P(), P(), P(), P())
    return jax.shard_map(
        per_device, mesh=mesh, in_specs=in_specs, out_specs=out_specs, check_vma=False
    )
```

```python
import functools
import math

import jax
import jax.numpy as jnp
from jax import lax
from jax.experimental import pallas as pl
from jax.experimental.pallas import tpu as pltpu
from jax.sharding import PartitionSpec as P

HEADS = 4
EPS = 1e-05
BACK_VMEM = 40
SMALL = 10
BF16 = jnp.bfloat16
F32 = jnp.float32
NN = (((1,), (0,)), ((), ()))
NT = (((1,), (1,)), ((), ()))
TN = (((0,), (0,)), ((), ()))
SCORE_BOUND = 60.0
ERFC_P = 0.325
ERFC_C = (
    -5.927487965082223e-05,
    0.18467549445148965,
    0.1708094188150158,
    0.2414269376514742,
    -0.07282782022580145,
    0.6147421737182138,
    -0.5684607599983035,
    0.5878333184067656,
    -0.15813953377061551,
)


def dot(a, b, dims):
    return lax.dot_general(a, b, dims, preferred_element_type=F32)


def call(kernel, out_shape, flops=0, moved=0, vmem=48, **kw):
    return pl.pallas_call(
        kernel,
        out_shape=out_shape,
        compiler_params=pltpu.CompilerParams(vmem_limit_bytes=vmem * 2**20),
        cost_estimate=pl.CostEstimate(flops=int(flops), bytes_accessed=int(moved), transcendentals=0),
        **kw,
    )


def sds(shape, dtype):
    return jax.ShapeDtypeStruct(shape, dtype)


def norm_parts(x):
    centred = x - jnp.mean(x, axis=-1, keepdims=True)
    rstd = lax.rsqrt(jnp.mean(centred * centred, axis=-1, keepdims=True) + EPS)
    return centred * rstd, rstd


def norm_back(gy, xhat, rstd, gain):
    gx = gy * gain
    first = jnp.mean(gx, axis=-1, keepdims=True)
    second = jnp.mean(gx * xhat, axis=-1, keepdims=True)
    return rstd * (gx - first - xhat * second)


def head_ones(width, lanes=None, step=None):
    rows = lax.broadcasted_iota(jnp.int32, (width, lanes or width), 0) // (width // HEADS)
    cols = lax.broadcasted_iota(jnp.int32, (width, lanes or width), 1) // (step or width // HEADS)
    return (rows == cols).astype(F32).astype(BF16)


def start_copies(pairs, sem):
    copies = [pltpu.make_async_copy(src, dst, sem.at[i]) for i, (src, dst) in enumerate(pairs)]
    for c in copies:
        c.start()
    return copies


def live_rows(me_ref, len_ref, block, length):
    place = (me_ref[0] ^ block) * length + lax.broadcasted_iota(jnp.int32, (length, 1), 0)
    return place < len_ref[me_ref[0] // 2]


def qkv_kernel(me_ref, len_ref, own_ref, pair_ref, gain_ref, w_ref, n_out, q_ref, k_ref, v_ref, top_ref, n_ref, n_sem, *, first):
    length, width = pair_ref.shape
    ones = head_ones(width)
    top_ref[...] = jnp.zeros_like(top_ref)
    for j in range(2):
        cut = slice(j * length, (j + 1) * length)
        if j == 1:
            x = pair_ref[...]
        elif first == 0:
            x = own_ref[me_ref[0] // 2]
        else:
            x = own_ref[...]
        xhat, _ = norm_parts(x.astype(F32))
        normed = (xhat * gain_ref[...]).astype(BF16)
        n_ref[cut] = normed
        live = live_rows(me_ref, len_ref, first + j, length).astype(F32).astype(BF16)
        skip = width if j == 1 else 0
        mixed = dot(normed, w_ref[:, skip:], NN).astype(BF16)
        if j == 0:
            q = mixed[:, :width] * BF16((width // HEADS) ** -0.5)
            q_ref[...] = q
            qf = q.astype(F32)
            top_ref[0:1, :] = jnp.max(dot((qf * qf).astype(BF16), ones, NN), axis=0, keepdims=True)
        k = mixed[:, width - skip : 2 * width - skip] * live
        k_ref[cut] = k
        v_ref[cut] = mixed[:, 2 * width - skip :] * live
        kf = k.astype(F32)
        top_ref[1 + j : 2 + j, :] = jnp.max(dot((kf * kf).astype(BF16), ones, NN), axis=0, keepdims=True)
    keep_n = pltpu.make_async_copy(n_ref, n_out, n_sem)
    keep_n.start()
    if first == 0:
        keep_n.wait()


def qkv(me, valid_len, own, pair, gain, w, first):
    length, width = pair.shape
    smem = pl.BlockSpec(memory_space=pltpu.SMEM)
    vmem = pl.BlockSpec(memory_space=pltpu.VMEM)
    hbm = pl.BlockSpec(memory_space=pltpu.HBM)
    rows = 2 * length
    return call(
        functools.partial(qkv_kernel, first=first),
        [
            pltpu.HBM((rows, width), BF16),
            sds((length, width), BF16),
            sds((rows, width), BF16),
            sds((rows, width), BF16),
            sds((8, width), F32),
        ],
        flops=6 * rows * width * width,
        moved=10 * rows * width,
        vmem=16,
        in_specs=[smem, smem] + [vmem] * 4,
        out_specs=[hbm] + [vmem] * 4,
        scratch_shapes=[pltpu.VMEM((rows, width), BF16), pltpu.SemaphoreType.DMA],
    )(me, valid_len, own, pair, gain, w)


def live_keys(me_ref, len_ref, keys):
    lane = lax.broadcasted_iota(jnp.int32, (1, keys), 1)
    length = keys // 4
    place = ((lane // length) ^ me_ref[0]) * length + lane % length
    return place < len_ref[me_ref[0] // 2]


def gelu_parts(x):
    down = 1.0 + (ERFC_P * math.sqrt(0.5)) * jnp.abs(x)
    t = pl.reciprocal(down, approx=True)
    t = t * (2.0 - t * down)
    poly = jnp.full_like(t, 0.5 * ERFC_C[-1])
    for c in ERFC_C[-2::-1]:
        poly = poly * t + 0.5 * c
    bell = jnp.exp2((x * x) * (-0.5 * math.log2(math.e)))
    tail = poly * bell
    cdf = jnp.where(x >= 0, 1.0 - tail, tail)
    return x * cdf, cdf + (x * (1.0 / math.sqrt(2.0 * math.pi))) * bell


def gamma_parts(x):
    large = x > 16.0
    small = jnp.minimum(x, 16.0)
    w = small * (small + 7.0)
    a, b, c = w + 6.0, w + 10.0, w + 12.0
    log_prod = jnp.log(w * a * (b * c))
    sum_inv = (2.0 * small + 7.0) * (1.0 / w + 1.0 / a + 1.0 / b + 1.0 / c)
    big = jnp.where(large, x, x + 8.0)
    log_big = jnp.log(big)
    inv = 1.0 / big
    inv2 = inv * inv
    lg = (big - 0.5) * log_big - big + 0.5 * math.log(2.0 * math.pi)
    lg = lg + inv * (1.0 / 12.0 - inv2 * (1.0 / 360.0 - inv2 * (1.0 / 1260.0)))
    dg = log_big - 0.5 * inv - inv2 * (1.0 / 12.0 - inv2 * (1.0 / 120.0 - inv2 * (1.0 / 252.0)))
    return jnp.where(large, lg, lg - log_prod), jnp.where(large, dg, dg - sum_inv)


def softplus(x):
    return jnp.maximum(x, 0.0) + jnp.log(1.0 + jnp.exp(-jnp.abs(x)))


def sigmoid(x):
    return 1.0 / (1.0 + jnp.exp(-x))


def zinb(m, t, p, y, scale):
    rate = scale * (softplus(m) + 0.05)
    theta = softplus(t) + 0.05
    total = theta + rate
    inv_total = 1.0 / total
    log_total = jnp.log(total)
    log_theta = jnp.log(theta)
    z0 = theta * (log_theta - log_total)
    pi = sigmoid(p)
    e0 = jnp.exp(z0)
    den = pi + (1.0 - pi) * e0
    inv_den = 1.0 / den
    some = y > 0
    yf = y.astype(F32)
    lg_sum, dg_sum = gamma_parts(yf + theta)
    lg_theta, dg_theta = gamma_parts(theta)
    lg_y, _ = gamma_parts(yf + 1.0)
    log_nb = lg_sum - lg_theta - lg_y + z0 + yf * (jnp.log(rate) - log_total)
    nll = jnp.where(some, softplus(p) - log_nb, -jnp.log(den))
    g_z0 = jnp.where(some, -1.0, -(1.0 - pi) * e0 * inv_den)
    share = theta * inv_total
    g_theta = g_z0 * (log_theta - log_total + 1.0 - share)
    g_theta = g_theta + jnp.where(some, dg_theta - dg_sum + yf * inv_total, 0.0)
    g_rate = jnp.where(some, yf * (inv_total - 1.0 / rate), 0.0) - g_z0 * share
    g_p = jnp.where(some, pi, -(1.0 - e0) * inv_den * pi * (1.0 - pi))
    return nll, g_rate * scale * sigmoid(m), g_theta * sigmoid(t), g_p


def split2(x):
    high = x.astype(BF16)
    return high, (x - high.astype(F32)).astype(BF16)


def layer_kernel(me_ref, len_ref, lib_ref, xa_ref, xb_ref, pb_ref, gain1_ref, w_ref, qa_ref, ka_ref, va_ref, ta_ref,
                 gain_ref, w_out_ref, w_up_ref, w_down_ref, w_dec_ref, gene_ref, c0_ref, c1_ref, c2_ref, c3_ref,
                 p_ref, nb_ref, gres_out, keep_out, q_s, kb_ref, vb_ref, do_ref, cols_ref, send_ref,
                 small_ref,
                 nb_s, nb_sem, gres_ref, keep_ref, out_sem, qb_ref, tb_ref, cols_s, x_s, p_s, p_sem, gt_s, aug_s, o_s, linv_s, res_s, n2_s, act_s, gp_s, dec_s, gd_s, w_s, table_s, ga_down, ga_up, ga_out,
                 *, block, tall):
    part, width = ka_ref.shape
    keys = 2 * part
    length = part // 2
    rows = part
    hidden = w_up_ref.shape[1]
    pair = 2 * (width // HEADS)
    half = pair // 2
    pairs = HEADS // 2
    me = me_ref[0]
    cell = me // 2
    valid_len = len_ref[cell]
    gain = gain_ref[...]
    small_ref[...] = jnp.zeros_like(small_ref)
    ga_down[...] = jnp.zeros_like(ga_down)
    ga_up[...] = jnp.zeros_like(ga_up)
    ga_out[...] = jnp.zeros_like(ga_out)
    lane = lax.broadcasted_iota(jnp.int32, (1, pair), 1)

    def rowsum(a):
        return jnp.sum(a, axis=0, keepdims=True)

    qkv_kernel(me_ref, len_ref, xb_ref, pb_ref, gain1_ref, w_ref, nb_ref, qb_ref, kb_ref, vb_ref, tb_ref, nb_s, nb_sem, first=2)

    live = live_keys(me_ref, len_ref, keys)
    mask = jnp.transpose(jnp.broadcast_to(live.astype(F32), (pair, keys))).astype(BF16)
    for j, ref in enumerate((va_ref, vb_ref)):
        cut = slice(j * part, (j + 1) * part)
        for g in range(pairs):
            v = ref[:, g * pair : (g + 1) * pair]
            aug_s[2 * g, cut] = jnp.where(lane < half, v, mask[cut])
            aug_s[2 * g + 1, cut] = jnp.where(lane < half, mask[cut], v)

    top_q = jnp.maximum(ta_ref[0:1], tb_ref[0:1])
    top_k = jnp.maximum(jnp.maximum(ta_ref[1:2], tb_ref[1:2]), jnp.maximum(ta_ref[2:3], tb_ref[2:3]))
    plain = jnp.max(top_q * top_k) * 1.05 < SCORE_BOUND * SCORE_BOUND

    q_s[0:length] = qa_ref[...]
    q_s[length:rows] = qb_ref[...]
    x_s[0:length] = xa_ref[cell]
    x_s[length:rows] = xb_ref[...]

    def copy(b, g):
        slot = (b * pairs + g) % 2
        rcut = pl.ds(pl.multiple_of(b * block, block), block)
        return pltpu.make_async_copy(p_s.at[slot], p_ref.at[pl.ds(2 * g, 2), rcut], p_sem.at[slot])

    def attend_block(b, g, safe):
        cut = pl.ds(pl.multiple_of(b * block, block), block)
        cols = slice(g * pair, (g + 1) * pair)
        slot = (b * pairs + g) % 2
        q = q_s[cut, cols]
        zero = jnp.zeros_like(q)
        outs = []
        for h in range(2):
            home = p_s.at[slot, h]
            qh = jnp.where(lane < half, q, zero) if h == 0 else jnp.where(lane < half, zero, q)
            if safe:
                s = jnp.concatenate([dot(qh, ref[:, cols], NT) for ref in (ka_ref, kb_ref)], axis=1)
                s = jnp.where(live, s, -1e30)
                p = jnp.exp(s - jnp.max(s, axis=1, keepdims=True)).astype(BF16)
                home[...] = p
                total = dot(p, aug_s[2 * g + h], NN)
            else:
                total = None
                for j, ref in enumerate((ka_ref, kb_ref)):
                    kcut = slice(j * part, (j + 1) * part)
                    p = jnp.exp(dot(qh, ref[:, cols], NT)).astype(BF16)
                    home[:, kcut] = p
                    o = dot(p, aug_s[2 * g + h, kcut], NN)
                    total = o if total is None else total + o
            outs.append(total)
        up = jnp.where(lane < half, outs[0], outs[1])
        down = pltpu.roll(jnp.where(lane < half, outs[1], outs[0]), half, 1)
        inverse = 1.0 / down
        o_s[cut, cols] = up * inverse
        linv_s[cut, cols] = inverse

    @pl.loop(0, rows // block)
    def _(b):
        for g in range(pairs):

            @pl.when(b > 0)
            def _():
                copy(b - 1, g).wait()

            pl.when(plain)(functools.partial(attend_block, b, g, False))
            pl.when(jnp.logical_not(plain))(functools.partial(attend_block, b, g, True))
            copy(b, g).start()

    @pl.loop(0, rows // tall)
    def _(b):
        start = pl.multiple_of(b * tall, tall)
        cut = pl.ds(start, tall)
        base = jnp.where(start < length, me * length + start, (me ^ 2) * length + start - length)
        valid = (base + lax.broadcasted_iota(jnp.int32, (tall, 1), 0) < valid_len).astype(F32)
        attn_out = dot(o_s[cut].astype(BF16), w_out_ref[...], NN)
        resid = x_s[cut].astype(F32) + attn_out
        res_s[cut] = resid
        xhat, _ = norm_parts(resid)
        normed = (xhat * gain).astype(BF16)
        n2_s[cut] = normed
        act, slope = gelu_parts(dot(normed, w_up_ref[...], NN))
        act = act.astype(BF16)
        act_s[cut] = act
        gp_s[cut] = slope
        mlp_out = dot(act, w_down_ref[...], NN)
        final = resid + mlp_out
        dec_s[cut] = final.astype(BF16)
        small_ref[0:1, :] += rowsum(valid * final * final)
        small_ref[1:2, :] += rowsum(valid * attn_out * attn_out)
        small_ref[2:3, :] += rowsum(valid * mlp_out * mlp_out)

    w_s[...] = jnp.zeros_like(w_s)
    w_s[0:3, :] = w_dec_ref[...].astype(F32)
    w_s[3:6, :] = w_dec_ref[...].astype(F32)
    w_twice = w_s[...].astype(BF16)
    decoded = dot(w_twice, dec_s[...], NT)
    for j, ref in enumerate((c0_ref, c1_ref, c2_ref, c3_ref)):
        for i in range(length // 128):
            table_s[j * (length // 128) + i : j * (length // 128) + i + 1, :] = ref[:, i * 128 : (i + 1) * 128].astype(F32)
    starts = (me * length, (me ^ 2) * length)
    gene = jnp.concatenate([gene_ref[pl.ds(cell, 1), pl.ds(pl.multiple_of(a, length), length)] for a in starts], axis=1)
    gene = ((gene // length) ^ me) * length + gene % length
    high = (lax.broadcasted_iota(jnp.int32, (table_s.shape[0], rows), 0) == gene // 128).astype(F32).astype(BF16)
    found = dot(table_s[...].astype(BF16), high, TN)
    low = lax.broadcasted_iota(jnp.int32, (128, rows), 0) == gene % 128
    observed = rowsum(jnp.where(low, found, 0.0))
    lane = lax.broadcasted_iota(jnp.int32, (1, rows), 1)
    places = jnp.where(lane < length, starts[0] + lane, starts[1] + lane - length)
    valid = (places < valid_len).astype(F32)
    scale = lib_ref[cell].astype(F32) / (4 * length)
    nll, g_m, g_t, g_p = zinb(decoded[0:1], decoded[1:2], decoded[2:3], observed, scale)
    nll = nll * valid
    for j in range(rows // width):
        small_ref[3:4, :] += nll[:, j * width : (j + 1) * width]
        small_ref[4:5, :] += valid[:, j * width : (j + 1) * width]
    gd_s[...] = jnp.zeros_like(gd_s)
    for j, g in enumerate((g_m, g_t, g_p)):
        gh, gl = split2(g * valid)
        gd_s[j : j + 1, :] = gh.astype(F32)
        gd_s[3 + j : 4 + j, :] = gl.astype(F32)
    gd = gd_s[...].astype(BF16)
    gw = dot(gd, dec_s[...], NN)
    small_ref[5:8, :] = gw[0:3] + gw[3:6]

    cols_s[...] = jnp.zeros_like(cols_s)
    heads = head_ones(width, 128, 1)
    for j in range(rows // tall):
        gt_s[j * 16 : (j + 1) * 16] = gd[:, j * tall : (j + 1) * tall]

    @pl.loop(0, rows // tall)
    def _(b):
        cut = pl.ds(pl.multiple_of(b * tall, tall), tall)
        g_final = dot(gt_s[pl.ds(pl.multiple_of(b * 16, 16), 16)], w_twice, TN).astype(BF16)
        ga_down[...] += dot(act_s[cut], g_final, TN)
        g_up = (dot(g_final, w_down_ref[...], NT) * gp_s[cut]).astype(BF16)
        ga_up[...] += dot(n2_s[cut], g_up, TN)
        g_normed = dot(g_up, w_up_ref[...], NT)
        xhat, rstd = norm_parts(res_s[cut])
        small_ref[8:9, :] += rowsum(g_normed * xhat)
        g_res = g_final.astype(F32) + norm_back(g_normed, xhat, rstd, gain)
        gres_ref[cut] = g_res
        g_attn = g_res.astype(BF16)
        o = o_s[cut]
        linv = linv_s[cut]
        ga_out[...] += dot(o.astype(BF16), g_attn, TN)
        do = dot(g_attn, w_out_ref[...], NT).astype(BF16)
        do_ref[cut] = do
        dof = do.astype(F32)
        ph, pl_ = split2(dof * o)
        cols_s[:, 0:HEADS] = (dot(ph, heads, NN) + dot(pl_, heads, NN))[:, 0:HEADS]
        for h in range(HEADS):
            cols_s[:, HEADS + h : HEADS + h + 1] = linv[:, h * half : h * half + 1]
        cols_ref[:, cut] = jnp.transpose(cols_s[...])[0 : 2 * HEADS]

    gres_copy = pltpu.make_async_copy(gres_ref, gres_out, out_sem.at[0])
    gres_copy.start()
    for g in range(pairs):
        copy(rows // block - 1, g).wait()
    pltpu.make_async_copy(nb_s, nb_ref, nb_sem).wait()

    def write(low_ref, high_ref):
        pieces = [ga_down[...]]
        pieces += [ga_up[:, j * width : (j + 1) * width] for j in range(hidden // width)]
        pieces += [ga_out[...]]
        at = 0
        half = low_ref.shape[0]
        for piece in pieces:
            n = piece.shape[0]
            first = max(0, min(n, half - at))
            if first:
                low_ref[at : at + first, :] = piece[:first].astype(BF16)
            if first < n:
                high_ref[at + first - half : at + n - half, :] = piece[first:].astype(BF16)
            at += n

    @pl.when(me % 2 == 0)
    def _():
        write(keep_ref, send_ref)

    @pl.when(me % 2 == 1)
    def _():
        write(send_ref, keep_ref)

    keep_copy = pltpu.make_async_copy(keep_ref, keep_out, out_sem.at[1])
    keep_copy.start()
    gres_copy.wait()
    keep_copy.wait()


def layer(me, valid_len, library, xa, xb, pb, gain1, w, qa, ka, va, ta, gain, w_out, w_up, w_down, w_dec, gene, tables, block=256, tall=512):
    part, width = ka.shape
    rows, keys, length = part, 2 * part, part // 2
    hidden = w_up.shape[1]
    pair = 2 * (width // HEADS)
    smem = pl.BlockSpec(memory_space=pltpu.SMEM)
    vmem = pl.BlockSpec(memory_space=pltpu.VMEM)
    half = (2 * hidden + width) // 2
    return call(
        functools.partial(layer_kernel, block=block, tall=tall),
        [
            pltpu.HBM((HEADS, rows, keys), BF16),
            pltpu.HBM((part, width), BF16),
            pltpu.HBM((rows, width), F32),
            pltpu.HBM((half, width), BF16),
            sds((rows, width), BF16),
            sds((part, width), BF16),
            sds((part, width), BF16),
            sds((rows, width), BF16),
            sds((2 * HEADS, rows), F32),
            sds((half, width), BF16),
            sds((16, width), F32),
        ],
        flops=24 * rows * width * hidden + 16 * rows * keys * width,
        vmem=46,
        in_specs=[smem] * 3 + [vmem] * 19,
        out_specs=[pl.BlockSpec(memory_space=pltpu.HBM)] * 4 + [vmem] * 7,
        scratch_shapes=[
            pltpu.VMEM((part, width), BF16),
            pltpu.SemaphoreType.DMA,
            pltpu.VMEM((rows, width), F32),
            pltpu.VMEM((half, width), BF16),
            pltpu.SemaphoreType.DMA((2,)),
            pltpu.VMEM((length, width), BF16),
            pltpu.VMEM((8, width), F32),
            pltpu.VMEM((tall, 128), F32),
            pltpu.VMEM((rows, width), BF16),
            pltpu.VMEM((2, 2, block, keys), BF16),
            pltpu.SemaphoreType.DMA((2,)),
            pltpu.VMEM((16 * rows // tall, tall), BF16),
            pltpu.VMEM((HEADS, keys, pair), BF16),
            pltpu.VMEM((rows, width), F32),
            pltpu.VMEM((rows, width), F32),
            pltpu.VMEM((rows, width), F32),
            pltpu.VMEM((rows, width), BF16),
            pltpu.VMEM((rows, hidden), BF16),
            pltpu.VMEM((rows, hidden), F32),
            pltpu.VMEM((rows, width), BF16),
            pltpu.VMEM((16, rows), F32),
            pltpu.VMEM((16, width), F32),
            pltpu.VMEM((rows // 64, 128), F32),
            pltpu.VMEM((hidden, width), F32),
            pltpu.VMEM((width, hidden), F32),
            pltpu.VMEM((width, width), F32),
        ],
    )(me, valid_len, library, xa, xb, pb, gain1, w, qa, ka, va, ta, gain, w_out, w_up, w_down, w_dec, gene, *tables)


def attend_back_kernel(me_ref, len_ref, q_ref, do_ref, cols_ref, ka_ref, kb_ref, va_ref, vb_ref, *refs, head, block, chunk):
    refs = list(refs)
    first, following = head == 0, head + 1 < HEADS
    p_ref = None if first else refs.pop(0)
    home_ref = refs.pop(0) if following else None
    dq_ref, dk_ref, dv_ref = refs[:3]
    next_ref = refs[3] if following else None
    ak_ref, av_ref = refs[3 + following : 5 + following]
    copies = []
    if first:
        p_ref, p_sem = refs[6:8]
        cuts = [slice(i, i + block) for i in range(0, do_ref.shape[0], block)]
        copies = start_copies([(home_ref.at[0, cut], p_ref.at[cut]) for cut in cuts], p_sem)
    if following:
        fetch = pltpu.make_async_copy(home_ref.at[head + 1], next_ref, refs[-1])
        fetch.start()
    part, width = ka_ref.shape
    keys = 2 * part
    rows = do_ref.shape[0]
    half = width // HEADS
    pair = 2 * half
    lane = lax.broadcasted_iota(jnp.int32, (1, pair), 1)
    lo = (head % 2) * half
    own = (lane < half) if head % 2 == 0 else (lane >= half)
    at0 = head // 2 * pair
    cols = slice(at0, at0 + pair)
    mine = slice(at0 + lo, at0 + lo + half)
    for b in range(rows // block):
        cut = slice(b * block, (b + 1) * block)
        q = q_ref[cut, mine]
        do = do_ref[cut, cols]
        do = jnp.where(own, do, jnp.zeros_like(do))
        both = jnp.transpose(cols_ref[:, cut])
        delta = both[:, head : head + 1]
        linv = both[:, HEADS + head : HEADS + head + 1]
        dl = (do_ref[cut, mine].astype(F32) * linv).astype(BF16)
        if first:
            copies[b].wait()
        total = None
        for c in range(keys // chunk):
            kcut = slice(c * chunk, (c + 1) * chunk)
            k_ref, v_ref = (ka_ref, va_ref) if c * chunk < part else (kb_ref, vb_ref)
            kat = c * chunk % part
            kc = k_ref[kat : kat + chunk, cols]
            dp = dot(do, v_ref[kat : kat + chunk, cols], NT)
            pc = p_ref[cut, kcut]
            ds = (pc.astype(F32) * ((dp - delta) * linv)).astype(BF16)
            step = dot(ds, kc, NN)
            total = step if total is None else total + step
            dv = dot(dl, pc, TN)
            dk = dot(q, ds, TN)
            if b == 0:
                av_ref[:, kcut] = dv
                ak_ref[:, kcut] = dk
            else:
                av_ref[:, kcut] += dv
                ak_ref[:, kcut] += dk
        dq_ref[cut] = (jnp.where(own, total, 0.0) * half**-0.5).astype(BF16)
    live = live_keys(me_ref, len_ref, keys)
    dk_ref[...] = jnp.where(live, ak_ref[...], 0.0).astype(BF16)
    dv_ref[...] = jnp.where(live, av_ref[...], 0.0).astype(BF16)
    if following:
        fetch.wait()


def attend_back(head, me, valid_len, q, do, cols, ka, kb, va, vb, p, home, block=512, chunk=512):
    rows = do.shape[0]
    part, width = ka.shape
    keys = 2 * part
    pair = 2 * (width // HEADS)
    smem = pl.BlockSpec(memory_space=pltpu.SMEM)
    vmem = pl.BlockSpec(memory_space=pltpu.VMEM)
    first, following = head == 0, head + 1 < HEADS
    return call(
        functools.partial(attend_back_kernel, head=head, block=block, chunk=chunk),
        [sds((rows, pair), BF16), sds((pair // 2, keys), BF16), sds((pair // 2, keys), BF16)]
        + [sds((rows, keys), BF16)] * following,
        flops=8 * rows * keys * width,
        moved=2 * rows * keys,
        vmem=BACK_VMEM,
        in_specs=[smem, smem] + [vmem] * (7 + (not first)) + [pl.BlockSpec(memory_space=pltpu.HBM)] * following,
        out_specs=[vmem] * (3 + following),
        scratch_shapes=[pltpu.VMEM((pair // 2, keys), F32), pltpu.VMEM((pair // 2, keys), F32)]
        + [pltpu.VMEM((rows, keys), BF16), pltpu.SemaphoreType.DMA((rows // block,))] * first
        + [pltpu.SemaphoreType.DMA] * following,
    )(me, valid_len, q, do, cols, ka, kb, va, vb, *([] if first else [p]), *([home] * following))


def weights_kernel(me_ref, na_ref, nb_ref, *refs):
    keep_ref, send_ref = refs[-2:]
    heads = [refs[3 * h : 3 * h + 3] for h in range(HEADS)]
    part, width = na_ref.shape
    length = part // 2
    dim = width // HEADS
    dq = sum(h[0][...].astype(F32) for h in heads[:2]), sum(h[0][...].astype(F32) for h in heads[2:])
    dq = jnp.concatenate(dq, axis=1).astype(BF16)
    gq = dot(na_ref[:length], dq[:length], TN) + dot(nb_ref[:length], dq[length:], TN)
    outs = [gq]
    for j in (1, 2):
        d = jnp.concatenate([h[j][...] for h in heads], axis=0)
        g = dot(d[:, :part], na_ref[...], NN) + dot(d[:, part:], nb_ref[...], NN)
        outs.append(jnp.transpose(g))
    half = 3 * width // 2

    def write(low_ref, high_ref):
        at = 0
        for piece in outs:
            first = max(0, min(width, half - at))
            if first:
                low_ref[at : at + first, :] = piece[:first].astype(BF16)
            if first < width:
                high_ref[at + first - half : at + width - half, :] = piece[first:].astype(BF16)
            at += width

    @pl.when(me_ref[0] % 2 == 0)
    def _():
        write(keep_ref, send_ref)

    @pl.when(me_ref[0] % 2 == 1)
    def _():
        write(send_ref, keep_ref)


def weights(me, na, nb, back):
    part, width = na.shape
    half = 3 * width // 2
    smem = pl.BlockSpec(memory_space=pltpu.SMEM)
    vmem = pl.BlockSpec(memory_space=pltpu.VMEM)
    return call(
        weights_kernel,
        [sds((half, width), BF16)] * 2,
        vmem=16,
        flops=10 * part * width * width,
        moved=16 * part * width,
        in_specs=[smem] + [vmem] * (2 + 3 * HEADS),
        out_specs=[vmem] * 2,
    )(me, na, nb, *[a for b in back for a in b])


def write3(ref, x):
    n = x.shape[0]
    high = x.astype(BF16).astype(F32)
    rest = x - high
    mid = rest.astype(BF16).astype(F32)
    pad = jnp.zeros((ref.shape[0] - 3 * n, x.shape[1]), F32)
    ref[...] = jnp.concatenate([high, mid, rest - mid, pad], axis=0).astype(BF16)


def read3(x):
    n = SMALL
    x = x[: 3 * n].astype(F32)
    return x[:n] + x[n : 2 * n] + x[2 * n :]


def normed_kernel(me_ref, xa_ref, xb_ref, pa_ref, pb_ref, w_ref, small_ref, *refs):
    own_ref, send_ref, three_ref = refs[-3:]
    heads = [refs[3 * h : 3 * h + 3] for h in range(HEADS)]
    length, width = xb_ref.shape
    cell = me_ref[0] // 2
    tt = (((0,), (1,)), ((), ()))
    w = w_ref[...]
    dq = sum(h[0][...].astype(F32) for h in heads[:2]), sum(h[0][...].astype(F32) for h in heads[2:])
    dq = jnp.concatenate(dq, axis=1).astype(BF16)
    dk = jnp.concatenate([h[1][...] for h in heads], axis=0)
    dv = jnp.concatenate([h[2][...] for h in heads], axis=0)
    total = jnp.zeros((1, width), F32)
    for b in range(4):
        cut = slice(b * length, (b + 1) * length)
        gn = dot(dk[:, cut], w[:, width : 2 * width], tt) + dot(dv[:, cut], w[:, 2 * width :], tt)
        at = slice(b // 2 * length, (b // 2 + 1) * length)
        if b % 2 == 0:
            gn += dot(dq[at], w[:, :width], NT)
        x = xa_ref[cell] if b == 0 else (pa_ref, xb_ref, pb_ref)[b - 1][...]
        xhat, _ = norm_parts(x.astype(F32))
        total += jnp.sum(gn * xhat, axis=0, keepdims=True)
        if b % 2 == 0:
            own_ref[at] = gn
        else:
            send_ref[at] = gn.astype(BF16)
    write3(three_ref, jnp.concatenate([small_ref[0 : SMALL - 1], total], axis=0))


def normed_back(me, xa, xb, pa, pb, w, small, back):
    length, width = xb.shape
    rows = 2 * length
    smem = pl.BlockSpec(memory_space=pltpu.SMEM)
    vmem = pl.BlockSpec(memory_space=pltpu.VMEM)
    return call(
        normed_kernel,
        [sds((rows, width), F32), sds((rows, width), BF16), sds((32, width), BF16)],
        vmem=24,
        flops=12 * rows * width * width,
        moved=16 * rows * width,
        in_specs=[smem] + [vmem] * (6 + 3 * HEADS),
        out_specs=[vmem] * 3,
    )(me, xa, xb, pa, pb, w, small, *[a for b in back for a in b])


def tokens_kernel(me_ref, xa_ref, xb_ref, gain_ref, gres_ref, own_ref, got_ref, mine_ref, back_ref):
    length = mine_ref.shape[0]
    for b in range(2):
        cut = slice(b * length, (b + 1) * length)
        x = xa_ref[me_ref[0] // 2] if b == 0 else xb_ref[...]
        xhat, rstd = norm_parts(x.astype(F32))
        gn = own_ref[cut] + got_ref[cut].astype(F32)
        g = gres_ref[cut] + norm_back(gn, xhat, rstd, gain_ref[...])
        if b == 0:
            mine_ref[...] = g
        else:
            back_ref[...] = g.astype(BF16)


def tokens_back(me, xa, xb, gain, gres, own, got):
    length, width = xb.shape
    smem = pl.BlockSpec(memory_space=pltpu.SMEM)
    vmem = pl.BlockSpec(memory_space=pltpu.VMEM)
    return call(
        tokens_kernel,
        [sds((length, width), F32), sds((length, width), BF16)],
        vmem=12,
        flops=60 * length * width,
        moved=24 * length * width,
        in_specs=[smem] + [vmem] * 6,
        out_specs=[vmem] * 2,
    )(me, xa, xb, gain, gres, own, got)


def join_kernel(a_ref, b_ref, three_ref, o_ref):
    n = a_ref.shape[0]
    o_ref[:n] = (a_ref[...].astype(F32) + b_ref[...].astype(F32)).astype(BF16)
    o_ref[n:] = three_ref[...]


def merge_kernel(a_ref, b_ref, o_ref, *, small):
    n = a_ref.shape[0] - small
    o_ref[:n] = (a_ref[:n].astype(F32) + b_ref[:n].astype(F32)).astype(BF16)
    write3(o_ref.at[n:], read3(a_ref[n:]) + read3(b_ref[n:]))


def join(a, b, three):
    vmem = pl.BlockSpec(memory_space=pltpu.VMEM)
    shape = (a.shape[0] + three.shape[0], a.shape[1])
    return call(join_kernel, sds(shape, BF16), moved=6 * a.size, vmem=4, in_specs=[vmem] * 3, out_specs=vmem)(a, b, three)


def merge(a, b, small):
    vmem = pl.BlockSpec(memory_space=pltpu.VMEM)
    kernel = functools.partial(merge_kernel, small=small)
    return call(kernel, sds(a.shape, BF16), moved=6 * a.size, vmem=4, in_specs=[vmem] * 2, out_specs=vmem)(a, b)


def unpack_main_kernel(me_ref, own_ref, got_ref, down_ref, up_ref, out_ref):
    hidden, width = down_ref.shape

    def write(low_ref, high_ref):
        half = low_ref.shape[0]

        def rows(start, stop):
            if stop <= half:
                return low_ref[start:stop].astype(F32)
            return high_ref[start - half : stop - half].astype(F32)

        step = math.gcd(half, width)
        for at in range(0, hidden, step):
            down_ref[at : at + step] = rows(at, at + step)
        for j in range(hidden // width):
            for at in range(0, width, step):
                start = hidden + j * width + at
                up_ref[at : at + step, j * width : (j + 1) * width] = rows(start, start + step)
        for at in range(0, width, step):
            out_ref[at : at + step] = rows(2 * hidden + at, 2 * hidden + at + step)

    @pl.when(me_ref[0] % 2 == 0)
    def _():
        write(own_ref, got_ref)

    @pl.when(me_ref[0] % 2 == 1)
    def _():
        write(got_ref, own_ref)


def unpack_main(me, own, got, hidden):
    width = own.shape[1]
    smem = pl.BlockSpec(memory_space=pltpu.SMEM)
    vmem = pl.BlockSpec(memory_space=pltpu.VMEM)
    return call(
        unpack_main_kernel,
        [sds((hidden, width), F32), sds((width, hidden), F32), sds((width, width), F32)],
        vmem=12,
        moved=12 * hidden * width,
        in_specs=[smem, vmem, vmem],
        out_specs=[vmem] * 3,
    )(me, own, got)


def finish_kernel(me_ref, own_ref, got_ref, qkv_ref, gain1_ref, gain2_ref, dec_ref, sum_ref):
    width = gain1_ref.shape[1]
    half = 3 * width // 2

    def write(low_ref, high_ref):
        step = math.gcd(half, width)
        for j in range(3):
            for at in range(0, width, step):
                start = j * width + at
                ref, first = (low_ref, start) if start < half else (high_ref, start - half)
                qkv_ref[at : at + step, j * width : (j + 1) * width] = ref[first : first + step].astype(F32)

    @pl.when(me_ref[0] % 2 == 0)
    def _():
        write(own_ref, got_ref)

    @pl.when(me_ref[0] % 2 == 1)
    def _():
        write(got_ref, own_ref)

    small = read3(own_ref[half:]) + read3(got_ref[half:])
    gain1_ref[...] = small[9:10]
    gain2_ref[...] = small[8:9]
    dec_ref[...] = small[5:8]
    sums = jnp.sum(small, axis=1, keepdims=True)
    count = sums[4:5]
    rms = jnp.sqrt(sums[0:3] / (count * width))
    lane = lax.broadcasted_iota(jnp.int32, (1, 4), 1)
    out = jnp.where(lane == 0, sums[3:4] / count, 0.0)
    for j in range(3):
        out = jnp.where(lane == j + 1, rms[j : j + 1], out)
    sum_ref[...] = out


def finish(me, own, got):
    width = own.shape[1]
    smem = pl.BlockSpec(memory_space=pltpu.SMEM)
    vmem = pl.BlockSpec(memory_space=pltpu.VMEM)
    return call(
        finish_kernel,
        [sds((width, 3 * width), F32), sds((1, width), F32), sds((1, width), F32), sds((3, width), F32), sds((1, 4), F32)],
        vmem=8,
        moved=12 * 3 * width * width,
        in_specs=[smem] + [vmem] * 2,
        out_specs=[vmem] * 5,
    )(me, own, got)


AXES = ("cells", "slots")


def devices():
    return lax.axis_size("cells") * lax.axis_size("slots")


def swap(x, mask, odd=None):
    odd = mask if odd is None else odd
    return lax.ppermute(x, AXES, [(i, i ^ (odd if i % 2 else mask)) for i in range(devices())])


def routes():
    slots = lax.axis_size("slots")
    near, far = [slots, 2 * slots], []
    bit = 4 * slots
    while bit < devices():
        far.append(bit)
        bit *= 2
    small = list(zip(near[:1] + far + near[1:] + [2], near[::-1] + [2] + far))
    large = list(zip([slots, 2] + near[1:] + far, [slots, 2] + far + near[1:]))
    return small, large


def after(x, *others):
    return lax.optimization_barrier((x, *others))[0]


def per_device(
    tokens,
    valid_len,
    library,
    gene_slot,
    counts,
    norm1_gain,
    w_qkv,
    w_out,
    norm2_gain,
    w_up,
    w_down,
    w_decoder,
):
    cells, length, width = tokens.shape
    hidden = w_up.shape[1]
    slot = lax.axis_index("slots")
    cell = slot // 2
    me = jnp.full((1,), slot, jnp.int32)
    pick = lambda a: lax.dynamic_index_in_dim(a, cell, 0, keepdims=False)
    other = lambda a: lax.dynamic_index_in_dim(a, 1 - cell, 0, keepdims=False)

    came = swap(other(tokens), 2)
    near = swap(pick(tokens), 1)
    mine_counts = pick(counts)[None]
    away_counts = other(counts)[None]
    tables = (mine_counts, swap(mine_counts, 1), swap(away_counts, 2), swap(away_counts, 3))
    gain1 = norm1_gain[None]
    gain2 = norm2_gain[None]

    na, qa, ka, va, ta = qkv(me, valid_len, tokens, near, gain1, w_qkv, 0)
    came = after(came, ta, *tables)
    far = swap(came, 1)
    home, nb, gres, keep, q, kb, vb, do, cols, send, small = layer(
        me, valid_len, library, tokens, came, far, gain1, w_qkv, qa, ka, va, ta,
        gain2, w_out, w_up, w_down, w_decoder, gene_slot, tables,
    )

    route, order = routes()
    number = lax.axis_index("cells") * lax.axis_size("slots") + slot
    sides = [jnp.where(slot % 2 == 0, number // even, number // odd) % 2 for even, odd in order[:2]]

    def halve(x, side):
        n = x.shape[0] // 2
        return lax.dynamic_slice_in_dim(x, side * n, n, 0), lax.dynamic_slice_in_dim(x, (1 - side) * n, n, 0)

    def whole(own, got, side):
        return jnp.where(side == 0, jnp.concatenate([own, got], 0), jnp.concatenate([got, own], 0))

    def back(h, p, *others):
        here = after(me, *others) if others else me
        outs = attend_back(h, here, valid_len, q, do, cols, ka, kb, va, vb, p, home)
        backs.append(outs[:3])
        return outs[-1]

    got = swap(send, 1)
    backs = []
    p = back(0, None)
    main = keep + after(got, backs[0][0])
    for i in range(2):
        mine, away = halve(main, sides[i])
        got = swap(away, *order[i])
        p = back(1 + i, p, away)
        main = mine + after(got, backs[-1][0])
    got = swap(main, *order[2])
    back(3, p, main)
    main = main + after(got, backs[-1][0])
    got = swap(main, *order[3])

    keep, send = weights(after(me, main), na, nb, backs)
    final_got = swap(send, 1)
    gn_own, gn_send, three = normed_back(me, tokens, came, near, far, w_qkv, small, backs)
    rows3 = three.shape[0]
    gn_got = swap(gn_send, 1)
    final = join(keep, final_got, three)

    final_got = swap(final, *route[0])
    mine, away = tokens_back(me, tokens, came, gain1, gres, gn_own, gn_got)
    final = merge(final, after(final_got, away), rows3)

    final_got = swap(final, *route[1])
    returned = swap(away, 2)
    main = main + after(got, final)
    for masks in order[4:]:
        main = main + swap(main, *masks)
    got = swap(main, *order[1])
    final = merge(final, final_got, rows3)

    final_got = swap(final, *route[2])
    main = whole(main, after(got, final), sides[1])
    got = swap(main, *order[0])
    final = merge(final, after(final_got, main), rows3)

    for masks in route[3:-1]:
        final = merge(final, swap(final, *masks), rows3)
    final_got = swap(final, *route[-1])
    main = whole(main, after(got, final), sides[0])
    returned = after(returned, final).astype(F32)
    grad_tokens = jnp.where(cell == 0, jnp.stack([mine, returned]), jnp.stack([returned, mine]))
    g_down, g_up, g_out = unpack_main(me, main, swap(main, 1), hidden)
    final = merge(final, after(final_got, g_out, grad_tokens), rows3)
    g_qkv, g_gain1, g_gain2, g_dec, summary = finish(me, final, swap(final, 1))
    return (grad_tokens, g_gain1[0], g_qkv, g_out, g_gain2[0], g_up, g_down, g_dec, summary[0])


def solution(mesh):
    in_specs = (
        P("cells", "slots", None),
        P("cells"),
        P("cells"),
        P("cells", None),
        P("cells", "slots"),
        P(),
        P(),
        P(),
        P(),
        P(),
        P(),
        P(),
    )
    out_specs = (P("cells", "slots", None), P(), P(), P(), P(), P(), P(), P(), P())
    return jax.shard_map(
        per_device, mesh=mesh, in_specs=in_specs, out_specs=out_specs, check_vma=False
    )
```

```python
import functools
import math

import jax
import jax.numpy as jnp
from jax import lax
from jax.experimental import pallas as pl
from jax.experimental.pallas import tpu as pltpu
from jax.sharding import PartitionSpec as P

HEADS = 4
EPS = 1e-05
BACK_VMEM = 40
SMALL = 10
BF16 = jnp.bfloat16
F32 = jnp.float32
NN = (((1,), (0,)), ((), ()))
NT = (((1,), (1,)), ((), ()))
TN = (((0,), (0,)), ((), ()))
SCORE_BOUND = 60.0
ERFC_P = 0.325
ERFC_C = (
    -5.927487965082223e-05,
    0.18467549445148965,
    0.1708094188150158,
    0.2414269376514742,
    -0.07282782022580145,
    0.6147421737182138,
    -0.5684607599983035,
    0.5878333184067656,
    -0.15813953377061551,
)


def dot(a, b, dims):
    return lax.dot_general(a, b, dims, preferred_element_type=F32)


def call(kernel, out_shape, flops=0, moved=0, vmem=48, **kw):
    return pl.pallas_call(
        kernel,
        out_shape=out_shape,
        compiler_params=pltpu.CompilerParams(vmem_limit_bytes=vmem * 2**20),
        cost_estimate=pl.CostEstimate(flops=int(flops), bytes_accessed=int(moved), transcendentals=0),
        **kw,
    )


def sds(shape, dtype):
    return jax.ShapeDtypeStruct(shape, dtype)


def norm_parts(x):
    centred = x - jnp.mean(x, axis=-1, keepdims=True)
    rstd = lax.rsqrt(jnp.mean(centred * centred, axis=-1, keepdims=True) + EPS)
    return centred * rstd, rstd


def norm_back(gy, xhat, rstd, gain):
    gx = gy * gain
    first = jnp.mean(gx, axis=-1, keepdims=True)
    second = jnp.mean(gx * xhat, axis=-1, keepdims=True)
    return rstd * (gx - first - xhat * second)


def head_ones(width, lanes=None, step=None):
    rows = lax.broadcasted_iota(jnp.int32, (width, lanes or width), 0) // (width // HEADS)
    cols = lax.broadcasted_iota(jnp.int32, (width, lanes or width), 1) // (step or width // HEADS)
    return (rows == cols).astype(F32).astype(BF16)


def start_copies(pairs, sem):
    copies = [pltpu.make_async_copy(src, dst, sem.at[i]) for i, (src, dst) in enumerate(pairs)]
    for c in copies:
        c.start()
    return copies


def live_rows(me_ref, len_ref, block, length):
    place = (me_ref[0] ^ block) * length + lax.broadcasted_iota(jnp.int32, (length, 1), 0)
    return place < len_ref[me_ref[0] // 2]


def qkv_kernel(me_ref, len_ref, own_ref, pair_ref, gain_ref, w_ref, n_out, q_ref, k_ref, v_ref, top_ref, n_ref, n_sem, *, first):
    length, width = pair_ref.shape
    ones = head_ones(width)
    top_ref[...] = jnp.zeros_like(top_ref)
    for j in range(2):
        cut = slice(j * length, (j + 1) * length)
        if j == 1:
            x = pair_ref[...]
        elif first == 0:
            x = own_ref[me_ref[0] // 2]
        else:
            x = own_ref[...]
        xhat, _ = norm_parts(x.astype(F32))
        normed = (xhat * gain_ref[...]).astype(BF16)
        n_ref[cut] = normed
        live = live_rows(me_ref, len_ref, first + j, length).astype(F32).astype(BF16)
        skip = width if j == 1 else 0
        mixed = dot(normed, w_ref[:, skip:], NN).astype(BF16)
        if j == 0:
            q = mixed[:, :width] * BF16((width // HEADS) ** -0.5)
            q_ref[...] = q
            qf = q.astype(F32)
            top_ref[0:1, :] = jnp.max(dot((qf * qf).astype(BF16), ones, NN), axis=0, keepdims=True)
        k = mixed[:, width - skip : 2 * width - skip] * live
        k_ref[cut] = k
        v_ref[cut] = mixed[:, 2 * width - skip :] * live
        kf = k.astype(F32)
        top_ref[1 + j : 2 + j, :] = jnp.max(dot((kf * kf).astype(BF16), ones, NN), axis=0, keepdims=True)
    keep_n = pltpu.make_async_copy(n_ref, n_out, n_sem)
    keep_n.start()
    if first == 0:
        keep_n.wait()


def qkv(me, valid_len, own, pair, gain, w, first):
    length, width = pair.shape
    smem = pl.BlockSpec(memory_space=pltpu.SMEM)
    vmem = pl.BlockSpec(memory_space=pltpu.VMEM)
    hbm = pl.BlockSpec(memory_space=pltpu.HBM)
    rows = 2 * length
    return call(
        functools.partial(qkv_kernel, first=first),
        [
            pltpu.HBM((rows, width), BF16),
            sds((length, width), BF16),
            sds((rows, width), BF16),
            sds((rows, width), BF16),
            sds((8, width), F32),
        ],
        flops=6 * rows * width * width,
        moved=10 * rows * width,
        vmem=16,
        in_specs=[smem, smem] + [vmem] * 4,
        out_specs=[hbm] + [vmem] * 4,
        scratch_shapes=[pltpu.VMEM((rows, width), BF16), pltpu.SemaphoreType.DMA],
    )(me, valid_len, own, pair, gain, w)


def live_keys(me_ref, len_ref, keys):
    lane = lax.broadcasted_iota(jnp.int32, (1, keys), 1)
    length = keys // 4
    place = ((lane // length) ^ me_ref[0]) * length + lane % length
    return place < len_ref[me_ref[0] // 2]


def gelu_parts(x):
    down = 1.0 + (ERFC_P * math.sqrt(0.5)) * jnp.abs(x)
    t = pl.reciprocal(down, approx=True)
    t = t * (2.0 - t * down)
    poly = jnp.full_like(t, 0.5 * ERFC_C[-1])
    for c in ERFC_C[-2::-1]:
        poly = poly * t + 0.5 * c
    bell = jnp.exp2((x * x) * (-0.5 * math.log2(math.e)))
    tail = poly * bell
    cdf = jnp.where(x >= 0, 1.0 - tail, tail)
    return x * cdf, cdf + (x * (1.0 / math.sqrt(2.0 * math.pi))) * bell


def gamma_parts(x):
    large = x > 16.0
    small = jnp.minimum(x, 16.0)
    w = small * (small + 7.0)
    a, b, c = w + 6.0, w + 10.0, w + 12.0
    log_prod = jnp.log(w * a * (b * c))
    sum_inv = (2.0 * small + 7.0) * (1.0 / w + 1.0 / a + 1.0 / b + 1.0 / c)
    big = jnp.where(large, x, x + 8.0)
    log_big = jnp.log(big)
    inv = 1.0 / big
    inv2 = inv * inv
    lg = (big - 0.5) * log_big - big + 0.5 * math.log(2.0 * math.pi)
    lg = lg + inv * (1.0 / 12.0 - inv2 * (1.0 / 360.0 - inv2 * (1.0 / 1260.0)))
    dg = log_big - 0.5 * inv - inv2 * (1.0 / 12.0 - inv2 * (1.0 / 120.0 - inv2 * (1.0 / 252.0)))
    return jnp.where(large, lg, lg - log_prod), jnp.where(large, dg, dg - sum_inv)


def softplus(x):
    return jnp.maximum(x, 0.0) + jnp.log(1.0 + jnp.exp(-jnp.abs(x)))


def sigmoid(x):
    return 1.0 / (1.0 + jnp.exp(-x))


def zinb(m, t, p, y, scale):
    rate = scale * (softplus(m) + 0.05)
    theta = softplus(t) + 0.05
    total = theta + rate
    inv_total = 1.0 / total
    log_total = jnp.log(total)
    log_theta = jnp.log(theta)
    z0 = theta * (log_theta - log_total)
    pi = sigmoid(p)
    e0 = jnp.exp(z0)
    den = pi + (1.0 - pi) * e0
    inv_den = 1.0 / den
    some = y > 0
    yf = y.astype(F32)
    lg_sum, dg_sum = gamma_parts(yf + theta)
    lg_theta, dg_theta = gamma_parts(theta)
    lg_y, _ = gamma_parts(yf + 1.0)
    log_nb = lg_sum - lg_theta - lg_y + z0 + yf * (jnp.log(rate) - log_total)
    nll = jnp.where(some, softplus(p) - log_nb, -jnp.log(den))
    g_z0 = jnp.where(some, -1.0, -(1.0 - pi) * e0 * inv_den)
    share = theta * inv_total
    g_theta = g_z0 * (log_theta - log_total + 1.0 - share)
    g_theta = g_theta + jnp.where(some, dg_theta - dg_sum + yf * inv_total, 0.0)
    g_rate = jnp.where(some, yf * (inv_total - 1.0 / rate), 0.0) - g_z0 * share
    g_p = jnp.where(some, pi, -(1.0 - e0) * inv_den * pi * (1.0 - pi))
    return nll, g_rate * scale * sigmoid(m), g_theta * sigmoid(t), g_p


def split2(x):
    high = x.astype(BF16)
    return high, (x - high.astype(F32)).astype(BF16)


def layer_kernel(me_ref, len_ref, lib_ref, xa_ref, xb_ref, pb_ref, gain1_ref, w_ref, qa_ref, ka_ref, va_ref, ta_ref,
                 gain_ref, w_out_ref, w_up_ref, w_down_ref, w_dec_ref, gene_ref, c0_ref, c1_ref, c2_ref, c3_ref,
                 p_ref, nb_ref, gres_out, keep_out, q_s, kb_ref, vb_ref, do_ref, cols_ref, send_ref,
                 small_ref,
                 nb_s, nb_sem, gres_ref, keep_ref, out_sem, qb_ref, tb_ref, cols_s, x_s, p_s, p_sem, gt_s, aug_s, o_s, linv_s, res_s, n2_s, act_s, gp_s, dec_s, gd_s, w_s, table_s, ga_down, ga_up, ga_out,
                 *, block, tall):
    part, width = ka_ref.shape
    keys = 2 * part
    length = part // 2
    rows = part
    hidden = w_up_ref.shape[1]
    pair = 2 * (width // HEADS)
    half = pair // 2
    pairs = HEADS // 2
    me = me_ref[0]
    cell = me // 2
    valid_len = len_ref[cell]
    gain = gain_ref[...]
    small_ref[...] = jnp.zeros_like(small_ref)
    ga_down[...] = jnp.zeros_like(ga_down)
    ga_up[...] = jnp.zeros_like(ga_up)
    ga_out[...] = jnp.zeros_like(ga_out)
    lane = lax.broadcasted_iota(jnp.int32, (1, pair), 1)

    def rowsum(a):
        return jnp.sum(a, axis=0, keepdims=True)

    qkv_kernel(me_ref, len_ref, xb_ref, pb_ref, gain1_ref, w_ref, nb_ref, qb_ref, kb_ref, vb_ref, tb_ref, nb_s, nb_sem, first=2)

    live = live_keys(me_ref, len_ref, keys)
    mask = jnp.transpose(jnp.broadcast_to(live.astype(F32), (pair, keys))).astype(BF16)
    for j, ref in enumerate((va_ref, vb_ref)):
        cut = slice(j * part, (j + 1) * part)
        for g in range(pairs):
            v = ref[:, g * pair : (g + 1) * pair]
            aug_s[2 * g, cut] = jnp.where(lane < half, v, mask[cut])
            aug_s[2 * g + 1, cut] = jnp.where(lane < half, mask[cut], v)

    top_q = jnp.maximum(ta_ref[0:1], tb_ref[0:1])
    top_k = jnp.maximum(jnp.maximum(ta_ref[1:2], tb_ref[1:2]), jnp.maximum(ta_ref[2:3], tb_ref[2:3]))
    plain = jnp.max(top_q * top_k) * 1.05 < SCORE_BOUND * SCORE_BOUND

    q_s[0:length] = qa_ref[...]
    q_s[length:rows] = qb_ref[...]
    x_s[0:length] = xa_ref[cell]
    x_s[length:rows] = xb_ref[...]

    def copy(b, g):
        slot = (b * pairs + g) % 2
        rcut = pl.ds(pl.multiple_of(b * block, block), block)
        return pltpu.make_async_copy(p_s.at[slot], p_ref.at[pl.ds(2 * g, 2), rcut], p_sem.at[slot])

    def attend_block(b, g, safe):
        cut = pl.ds(pl.multiple_of(b * block, block), block)
        cols = slice(g * pair, (g + 1) * pair)
        slot = (b * pairs + g) % 2
        q = q_s[cut, cols]
        zero = jnp.zeros_like(q)
        outs = []
        for h in range(2):
            home = p_s.at[slot, h]
            qh = jnp.where(lane < half, q, zero) if h == 0 else jnp.where(lane < half, zero, q)
            if safe:
                s = jnp.concatenate([dot(qh, ref[:, cols], NT) for ref in (ka_ref, kb_ref)], axis=1)
                s = jnp.where(live, s, -1e30)
                p = jnp.exp(s - jnp.max(s, axis=1, keepdims=True)).astype(BF16)
                home[...] = p
                total = dot(p, aug_s[2 * g + h], NN)
            else:
                total = None
                for j, ref in enumerate((ka_ref, kb_ref)):
                    kcut = slice(j * part, (j + 1) * part)
                    p = jnp.exp(dot(qh, ref[:, cols], NT)).astype(BF16)
                    home[:, kcut] = p
                    o = dot(p, aug_s[2 * g + h, kcut], NN)
                    total = o if total is None else total + o
            outs.append(total)
        up = jnp.where(lane < half, outs[0], outs[1])
        down = pltpu.roll(jnp.where(lane < half, outs[1], outs[0]), half, 1)
        inverse = 1.0 / down
        o_s[cut, cols] = up * inverse
        linv_s[cut, cols] = inverse

    @pl.loop(0, rows // block)
    def _(b):
        for g in range(pairs):

            @pl.when(b > 0)
            def _():
                copy(b - 1, g).wait()

            pl.when(plain)(functools.partial(attend_block, b, g, False))
            pl.when(jnp.logical_not(plain))(functools.partial(attend_block, b, g, True))
            copy(b, g).start()

    @pl.loop(0, rows // tall)
    def _(b):
        start = pl.multiple_of(b * tall, tall)
        cut = pl.ds(start, tall)
        base = jnp.where(start < length, me * length + start, (me ^ 2) * length + start - length)
        valid = (base + lax.broadcasted_iota(jnp.int32, (tall, 1), 0) < valid_len).astype(F32)
        attn_out = dot(o_s[cut].astype(BF16), w_out_ref[...], NN)
        resid = x_s[cut].astype(F32) + attn_out
        res_s[cut] = resid
        xhat, _ = norm_parts(resid)
        normed = (xhat * gain).astype(BF16)
        n2_s[cut] = normed
        act, slope = gelu_parts(dot(normed, w_up_ref[...], NN))
        act = act.astype(BF16)
        act_s[cut] = act
        gp_s[cut] = slope
        mlp_out = dot(act, w_down_ref[...], NN)
        final = resid + mlp_out
        dec_s[cut] = final.astype(BF16)
        small_ref[0:1, :] += rowsum(valid * final * final)
        small_ref[1:2, :] += rowsum(valid * attn_out * attn_out)
        small_ref[2:3, :] += rowsum(valid * mlp_out * mlp_out)

    w_s[...] = jnp.zeros_like(w_s)
    w_s[0:3, :] = w_dec_ref[...].astype(F32)
    w_s[3:6, :] = w_dec_ref[...].astype(F32)
    w_twice = w_s[...].astype(BF16)
    decoded = dot(w_twice, dec_s[...], NT)
    for j, ref in enumerate((c0_ref, c1_ref, c2_ref, c3_ref)):
        for i in range(length // 128):
            table_s[j * (length // 128) + i : j * (length // 128) + i + 1, :] = ref[:, i * 128 : (i + 1) * 128].astype(F32)
    starts = (me * length, (me ^ 2) * length)
    gene = jnp.concatenate([gene_ref[pl.ds(cell, 1), pl.ds(pl.multiple_of(a, length), length)] for a in starts], axis=1)
    gene = ((gene // length) ^ me) * length + gene % length
    high = (lax.broadcasted_iota(jnp.int32, (table_s.shape[0], rows), 0) == gene // 128).astype(F32).astype(BF16)
    found = dot(table_s[...].astype(BF16), high, TN)
    low = lax.broadcasted_iota(jnp.int32, (128, rows), 0) == gene % 128
    observed = rowsum(jnp.where(low, found, 0.0))
    lane = lax.broadcasted_iota(jnp.int32, (1, rows), 1)
    places = jnp.where(lane < length, starts[0] + lane, starts[1] + lane - length)
    valid = (places < valid_len).astype(F32)
    scale = lib_ref[cell].astype(F32) / (4 * length)
    nll, g_m, g_t, g_p = zinb(decoded[0:1], decoded[1:2], decoded[2:3], observed, scale)
    nll = nll * valid
    for j in range(rows // width):
        small_ref[3:4, :] += nll[:, j * width : (j + 1) * width]
        small_ref[4:5, :] += valid[:, j * width : (j + 1) * width]
    gd_s[...] = jnp.zeros_like(gd_s)
    for j, g in enumerate((g_m, g_t, g_p)):
        gh, gl = split2(g * valid)
        gd_s[j : j + 1, :] = gh.astype(F32)
        gd_s[3 + j : 4 + j, :] = gl.astype(F32)
    gd = gd_s[...].astype(BF16)
    gw = dot(gd, dec_s[...], NN)
    small_ref[5:8, :] = gw[0:3] + gw[3:6]

    cols_s[...] = jnp.zeros_like(cols_s)
    heads = head_ones(width, 128, 1)
    for j in range(rows // tall):
        gt_s[j * 16 : (j + 1) * 16] = gd[:, j * tall : (j + 1) * tall]

    @pl.loop(0, rows // tall)
    def _(b):
        cut = pl.ds(pl.multiple_of(b * tall, tall), tall)
        g_final = dot(gt_s[pl.ds(pl.multiple_of(b * 16, 16), 16)], w_twice, TN).astype(BF16)
        ga_down[...] += dot(act_s[cut], g_final, TN)
        g_up = (dot(g_final, w_down_ref[...], NT) * gp_s[cut]).astype(BF16)
        ga_up[...] += dot(n2_s[cut], g_up, TN)
        g_normed = dot(g_up, w_up_ref[...], NT)
        xhat, rstd = norm_parts(res_s[cut])
        small_ref[8:9, :] += rowsum(g_normed * xhat)
        g_res = g_final.astype(F32) + norm_back(g_normed, xhat, rstd, gain)
        gres_ref[cut] = g_res
        g_attn = g_res.astype(BF16)
        o = o_s[cut]
        linv = linv_s[cut]
        ga_out[...] += dot(o.astype(BF16), g_attn, TN)
        do = dot(g_attn, w_out_ref[...], NT).astype(BF16)
        do_ref[cut] = do
        dof = do.astype(F32)
        ph, pl_ = split2(dof * o)
        cols_s[:, 0:HEADS] = (dot(ph, heads, NN) + dot(pl_, heads, NN))[:, 0:HEADS]
        for h in range(HEADS):
            cols_s[:, HEADS + h : HEADS + h + 1] = linv[:, h * half : h * half + 1]
        cols_ref[:, cut] = jnp.transpose(cols_s[...])[0 : 2 * HEADS]

    gres_copy = pltpu.make_async_copy(gres_ref, gres_out, out_sem.at[0])
    gres_copy.start()
    for g in range(pairs):
        copy(rows // block - 1, g).wait()
    pltpu.make_async_copy(nb_s, nb_ref, nb_sem).wait()

    def write(low_ref, high_ref):
        pieces = [ga_down[...]]
        pieces += [ga_up[:, j * width : (j + 1) * width] for j in range(hidden // width)]
        pieces += [ga_out[...]]
        at = 0
        half = low_ref.shape[0]
        for piece in pieces:
            n = piece.shape[0]
            first = max(0, min(n, half - at))
            if first:
                low_ref[at : at + first, :] = piece[:first].astype(BF16)
            if first < n:
                high_ref[at + first - half : at + n - half, :] = piece[first:].astype(BF16)
            at += n

    @pl.when(me % 2 == 0)
    def _():
        write(keep_ref, send_ref)

    @pl.when(me % 2 == 1)
    def _():
        write(send_ref, keep_ref)

    keep_copy = pltpu.make_async_copy(keep_ref, keep_out, out_sem.at[1])
    keep_copy.start()
    gres_copy.wait()
    keep_copy.wait()


def layer(me, valid_len, library, xa, xb, pb, gain1, w, qa, ka, va, ta, gain, w_out, w_up, w_down, w_dec, gene, tables, block=256, tall=512):
    part, width = ka.shape
    rows, keys, length = part, 2 * part, part // 2
    hidden = w_up.shape[1]
    pair = 2 * (width // HEADS)
    smem = pl.BlockSpec(memory_space=pltpu.SMEM)
    vmem = pl.BlockSpec(memory_space=pltpu.VMEM)
    half = (2 * hidden + width) // 2
    return call(
        functools.partial(layer_kernel, block=block, tall=tall),
        [
            pltpu.HBM((HEADS, rows, keys), BF16),
            pltpu.HBM((part, width), BF16),
            pltpu.HBM((rows, width), F32),
            pltpu.HBM((half, width), BF16),
            sds((rows, width), BF16),
            sds((part, width), BF16),
            sds((part, width), BF16),
            sds((rows, width), BF16),
            sds((2 * HEADS, rows), F32),
            sds((half, width), BF16),
            sds((16, width), F32),
        ],
        flops=24 * rows * width * hidden + 16 * rows * keys * width,
        vmem=46,
        in_specs=[smem] * 3 + [vmem] * 19,
        out_specs=[pl.BlockSpec(memory_space=pltpu.HBM)] * 4 + [vmem] * 7,
        scratch_shapes=[
            pltpu.VMEM((part, width), BF16),
            pltpu.SemaphoreType.DMA,
            pltpu.VMEM((rows, width), F32),
            pltpu.VMEM((half, width), BF16),
            pltpu.SemaphoreType.DMA((2,)),
            pltpu.VMEM((length, width), BF16),
            pltpu.VMEM((8, width), F32),
            pltpu.VMEM((tall, 128), F32),
            pltpu.VMEM((rows, width), BF16),
            pltpu.VMEM((2, 2, block, keys), BF16),
            pltpu.SemaphoreType.DMA((2,)),
            pltpu.VMEM((16 * rows // tall, tall), BF16),
            pltpu.VMEM((HEADS, keys, pair), BF16),
            pltpu.VMEM((rows, width), F32),
            pltpu.VMEM((rows, width), F32),
            pltpu.VMEM((rows, width), F32),
            pltpu.VMEM((rows, width), BF16),
            pltpu.VMEM((rows, hidden), BF16),
            pltpu.VMEM((rows, hidden), F32),
            pltpu.VMEM((rows, width), BF16),
            pltpu.VMEM((16, rows), F32),
            pltpu.VMEM((16, width), F32),
            pltpu.VMEM((rows // 64, 128), F32),
            pltpu.VMEM((hidden, width), F32),
            pltpu.VMEM((width, hidden), F32),
            pltpu.VMEM((width, width), F32),
        ],
    )(me, valid_len, library, xa, xb, pb, gain1, w, qa, ka, va, ta, gain, w_out, w_up, w_down, w_dec, gene, *tables)


def attend_back_kernel(me_ref, len_ref, q_ref, do_ref, cols_ref, ka_ref, kb_ref, va_ref, vb_ref, *refs, head, block, chunk):
    refs = list(refs)
    first, following = head == 0, head + 1 < HEADS
    p_ref = None if first else refs.pop(0)
    home_ref = refs.pop(0) if following else None
    dq_ref, dk_ref, dv_ref = refs[:3]
    next_ref = refs[3] if following else None
    ak_ref, av_ref = refs[3 + following : 5 + following]
    copies = []
    if first:
        p_ref, p_sem = refs[6:8]
        cuts = [slice(i, i + block) for i in range(0, do_ref.shape[0], block)]
        copies = start_copies([(home_ref.at[0, cut], p_ref.at[cut]) for cut in cuts], p_sem)
    if following:
        fetch = pltpu.make_async_copy(home_ref.at[head + 1], next_ref, refs[-1])
        fetch.start()
    part, width = ka_ref.shape
    keys = 2 * part
    rows = do_ref.shape[0]
    half = width // HEADS
    pair = 2 * half
    lane = lax.broadcasted_iota(jnp.int32, (1, pair), 1)
    lo = (head % 2) * half
    own = (lane < half) if head % 2 == 0 else (lane >= half)
    at0 = head // 2 * pair
    cols = slice(at0, at0 + pair)
    mine = slice(at0 + lo, at0 + lo + half)
    for b in range(rows // block):
        cut = slice(b * block, (b + 1) * block)
        q = q_ref[cut, mine]
        do = do_ref[cut, cols]
        do = jnp.where(own, do, jnp.zeros_like(do))
        both = jnp.transpose(cols_ref[:, cut])
        delta = both[:, head : head + 1]
        linv = both[:, HEADS + head : HEADS + head + 1]
        dl = (do_ref[cut, mine].astype(F32) * linv).astype(BF16)
        if first:
            copies[b].wait()
        total = None
        for c in range(keys // chunk):
            kcut = slice(c * chunk, (c + 1) * chunk)
            k_ref, v_ref = (ka_ref, va_ref) if c * chunk < part else (kb_ref, vb_ref)
            kat = c * chunk % part
            kc = k_ref[kat : kat + chunk, cols]
            dp = dot(do, v_ref[kat : kat + chunk, cols], NT)
            pc = p_ref[cut, kcut]
            ds = (pc.astype(F32) * ((dp - delta) * linv)).astype(BF16)
            step = dot(ds, kc, NN)
            total = step if total is None else total + step
            dv = dot(dl, pc, TN)
            dk = dot(q, ds, TN)
            if b == 0:
                av_ref[:, kcut] = dv
                ak_ref[:, kcut] = dk
            else:
                av_ref[:, kcut] += dv
                ak_ref[:, kcut] += dk
        dq_ref[cut] = (jnp.where(own, total, 0.0) * half**-0.5).astype(BF16)
    live = live_keys(me_ref, len_ref, keys)
    dk_ref[...] = jnp.where(live, ak_ref[...], 0.0).astype(BF16)
    dv_ref[...] = jnp.where(live, av_ref[...], 0.0).astype(BF16)
    if following:
        fetch.wait()


def attend_back(head, me, valid_len, q, do, cols, ka, kb, va, vb, p, home, block=512, chunk=512):
    rows = do.shape[0]
    part, width = ka.shape
    keys = 2 * part
    pair = 2 * (width // HEADS)
    smem = pl.BlockSpec(memory_space=pltpu.SMEM)
    vmem = pl.BlockSpec(memory_space=pltpu.VMEM)
    first, following = head == 0, head + 1 < HEADS
    return call(
        functools.partial(attend_back_kernel, head=head, block=block, chunk=chunk),
        [sds((rows, pair), BF16), sds((pair // 2, keys), BF16), sds((pair // 2, keys), BF16)]
        + [sds((rows, keys), BF16)] * following,
        flops=8 * rows * keys * width,
        moved=2 * rows * keys,
        vmem=BACK_VMEM,
        in_specs=[smem, smem] + [vmem] * (7 + (not first)) + [pl.BlockSpec(memory_space=pltpu.HBM)] * following,
        out_specs=[vmem] * (3 + following),
        scratch_shapes=[pltpu.VMEM((pair // 2, keys), F32), pltpu.VMEM((pair // 2, keys), F32)]
        + [pltpu.VMEM((rows, keys), BF16), pltpu.SemaphoreType.DMA((rows // block,))] * first
        + [pltpu.SemaphoreType.DMA] * following,
    )(me, valid_len, q, do, cols, ka, kb, va, vb, *([] if first else [p]), *([home] * following))


def weights_kernel(me_ref, na_ref, nb_ref, *refs):
    keep_ref, send_ref = refs[-2:]
    heads = [refs[3 * h : 3 * h + 3] for h in range(HEADS)]
    part, width = na_ref.shape
    length = part // 2
    dim = width // HEADS
    dq = sum(h[0][...].astype(F32) for h in heads[:2]), sum(h[0][...].astype(F32) for h in heads[2:])
    dq = jnp.concatenate(dq, axis=1).astype(BF16)
    gq = dot(na_ref[:length], dq[:length], TN) + dot(nb_ref[:length], dq[length:], TN)
    outs = [gq]
    for j in (1, 2):
        d = jnp.concatenate([h[j][...] for h in heads], axis=0)
        g = dot(d[:, :part], na_ref[...], NN) + dot(d[:, part:], nb_ref[...], NN)
        outs.append(jnp.transpose(g))
    half = 3 * width // 2

    def write(low_ref, high_ref):
        at = 0
        for piece in outs:
            first = max(0, min(width, half - at))
            if first:
                low_ref[at : at + first, :] = piece[:first].astype(BF16)
            if first < width:
                high_ref[at + first - half : at + width - half, :] = piece[first:].astype(BF16)
            at += width

    @pl.when(me_ref[0] % 2 == 0)
    def _():
        write(keep_ref, send_ref)

    @pl.when(me_ref[0] % 2 == 1)
    def _():
        write(send_ref, keep_ref)


def weights(me, na, nb, back):
    part, width = na.shape
    half = 3 * width // 2
    smem = pl.BlockSpec(memory_space=pltpu.SMEM)
    vmem = pl.BlockSpec(memory_space=pltpu.VMEM)
    return call(
        weights_kernel,
        [sds((half, width), BF16)] * 2,
        vmem=16,
        flops=10 * part * width * width,
        moved=16 * part * width,
        in_specs=[smem] + [vmem] * (2 + 3 * HEADS),
        out_specs=[vmem] * 2,
    )(me, na, nb, *[a for b in back for a in b])


def write3(ref, x):
    n = x.shape[0]
    high = x.astype(BF16).astype(F32)
    rest = x - high
    mid = rest.astype(BF16).astype(F32)
    pad = jnp.zeros((ref.shape[0] - 3 * n, x.shape[1]), F32)
    ref[...] = jnp.concatenate([high, mid, rest - mid, pad], axis=0).astype(BF16)


def read3(x):
    n = SMALL
    x = x[: 3 * n].astype(F32)
    return x[:n] + x[n : 2 * n] + x[2 * n :]


def normed_kernel(me_ref, xa_ref, xb_ref, pa_ref, pb_ref, w_ref, small_ref, *refs):
    own_ref, send_ref, three_ref = refs[-3:]
    heads = [refs[3 * h : 3 * h + 3] for h in range(HEADS)]
    length, width = xb_ref.shape
    cell = me_ref[0] // 2
    tt = (((0,), (1,)), ((), ()))
    w = w_ref[...]
    dq = sum(h[0][...].astype(F32) for h in heads[:2]), sum(h[0][...].astype(F32) for h in heads[2:])
    dq = jnp.concatenate(dq, axis=1).astype(BF16)
    dk = jnp.concatenate([h[1][...] for h in heads], axis=0)
    dv = jnp.concatenate([h[2][...] for h in heads], axis=0)
    total = jnp.zeros((1, width), F32)
    for b in range(4):
        cut = slice(b * length, (b + 1) * length)
        gn = dot(dk[:, cut], w[:, width : 2 * width], tt) + dot(dv[:, cut], w[:, 2 * width :], tt)
        at = slice(b // 2 * length, (b // 2 + 1) * length)
        if b % 2 == 0:
            gn += dot(dq[at], w[:, :width], NT)
        x = xa_ref[cell] if b == 0 else (pa_ref, xb_ref, pb_ref)[b - 1][...]
        xhat, _ = norm_parts(x.astype(F32))
        total += jnp.sum(gn * xhat, axis=0, keepdims=True)
        if b % 2 == 0:
            own_ref[at] = gn
        else:
            send_ref[at] = gn.astype(BF16)
    write3(three_ref, jnp.concatenate([small_ref[0 : SMALL - 1], total], axis=0))


def normed_back(me, xa, xb, pa, pb, w, small, back):
    length, width = xb.shape
    rows = 2 * length
    smem = pl.BlockSpec(memory_space=pltpu.SMEM)
    vmem = pl.BlockSpec(memory_space=pltpu.VMEM)
    return call(
        normed_kernel,
        [sds((rows, width), F32), sds((rows, width), BF16), sds((32, width), BF16)],
        vmem=24,
        flops=12 * rows * width * width,
        moved=16 * rows * width,
        in_specs=[smem] + [vmem] * (6 + 3 * HEADS),
        out_specs=[vmem] * 3,
    )(me, xa, xb, pa, pb, w, small, *[a for b in back for a in b])


def tokens_kernel(me_ref, xa_ref, xb_ref, gain_ref, gres_ref, own_ref, got_ref, mine_ref, back_ref):
    length = mine_ref.shape[0]
    for b in range(2):
        cut = slice(b * length, (b + 1) * length)
        x = xa_ref[me_ref[0] // 2] if b == 0 else xb_ref[...]
        xhat, rstd = norm_parts(x.astype(F32))
        gn = own_ref[cut] + got_ref[cut].astype(F32)
        g = gres_ref[cut] + norm_back(gn, xhat, rstd, gain_ref[...])
        if b == 0:
            mine_ref[...] = g
        else:
            back_ref[...] = g.astype(BF16)


def tokens_back(me, xa, xb, gain, gres, own, got):
    length, width = xb.shape
    smem = pl.BlockSpec(memory_space=pltpu.SMEM)
    vmem = pl.BlockSpec(memory_space=pltpu.VMEM)
    return call(
        tokens_kernel,
        [sds((length, width), F32), sds((length, width), BF16)],
        vmem=12,
        flops=60 * length * width,
        moved=24 * length * width,
        in_specs=[smem] + [vmem] * 6,
        out_specs=[vmem] * 2,
    )(me, xa, xb, gain, gres, own, got)


def join_kernel(a_ref, b_ref, three_ref, o_ref):
    n = a_ref.shape[0]
    o_ref[:n] = (a_ref[...].astype(F32) + b_ref[...].astype(F32)).astype(BF16)
    o_ref[n:] = three_ref[...]


def merge_kernel(a_ref, b_ref, o_ref, *, small):
    n = a_ref.shape[0] - small
    o_ref[:n] = (a_ref[:n].astype(F32) + b_ref[:n].astype(F32)).astype(BF16)
    write3(o_ref.at[n:], read3(a_ref[n:]) + read3(b_ref[n:]))


def join(a, b, three):
    vmem = pl.BlockSpec(memory_space=pltpu.VMEM)
    shape = (a.shape[0] + three.shape[0], a.shape[1])
    return call(join_kernel, sds(shape, BF16), moved=6 * a.size, vmem=4, in_specs=[vmem] * 3, out_specs=vmem)(a, b, three)


def merge(a, b, small):
    vmem = pl.BlockSpec(memory_space=pltpu.VMEM)
    kernel = functools.partial(merge_kernel, small=small)
    return call(kernel, sds(a.shape, BF16), moved=6 * a.size, vmem=4, in_specs=[vmem] * 2, out_specs=vmem)(a, b)


def unpack_main_kernel(me_ref, own_ref, got_ref, down_ref, up_ref, out_ref):
    hidden, width = down_ref.shape

    def write(low_ref, high_ref):
        half = low_ref.shape[0]

        def rows(start, stop):
            if stop <= half:
                return low_ref[start:stop].astype(F32)
            return high_ref[start - half : stop - half].astype(F32)

        step = math.gcd(half, width)
        for at in range(0, hidden, step):
            down_ref[at : at + step] = rows(at, at + step)
        for j in range(hidden // width):
            for at in range(0, width, step):
                start = hidden + j * width + at
                up_ref[at : at + step, j * width : (j + 1) * width] = rows(start, start + step)
        for at in range(0, width, step):
            out_ref[at : at + step] = rows(2 * hidden + at, 2 * hidden + at + step)

    @pl.when(me_ref[0] % 2 == 0)
    def _():
        write(own_ref, got_ref)

    @pl.when(me_ref[0] % 2 == 1)
    def _():
        write(got_ref, own_ref)


def unpack_main(me, own, got, hidden):
    width = own.shape[1]
    smem = pl.BlockSpec(memory_space=pltpu.SMEM)
    vmem = pl.BlockSpec(memory_space=pltpu.VMEM)
    return call(
        unpack_main_kernel,
        [sds((hidden, width), F32), sds((width, hidden), F32), sds((width, width), F32)],
        vmem=12,
        moved=12 * hidden * width,
        in_specs=[smem, vmem, vmem],
        out_specs=[vmem] * 3,
    )(me, own, got)


def finish_kernel(me_ref, own_ref, got_ref, qkv_ref, gain1_ref, gain2_ref, dec_ref, sum_ref):
    width = gain1_ref.shape[1]
    half = 3 * width // 2

    def write(low_ref, high_ref):
        step = math.gcd(half, width)
        for j in range(3):
            for at in range(0, width, step):
                start = j * width + at
                ref, first = (low_ref, start) if start < half else (high_ref, start - half)
                qkv_ref[at : at + step, j * width : (j + 1) * width] = ref[first : first + step].astype(F32)

    @pl.when(me_ref[0] % 2 == 0)
    def _():
        write(own_ref, got_ref)

    @pl.when(me_ref[0] % 2 == 1)
    def _():
        write(got_ref, own_ref)

    small = read3(own_ref[half:]) + read3(got_ref[half:])
    gain1_ref[...] = small[9:10]
    gain2_ref[...] = small[8:9]
    dec_ref[...] = small[5:8]
    sums = jnp.sum(small, axis=1, keepdims=True)
    count = sums[4:5]
    rms = jnp.sqrt(sums[0:3] / (count * width))
    lane = lax.broadcasted_iota(jnp.int32, (1, 4), 1)
    out = jnp.where(lane == 0, sums[3:4] / count, 0.0)
    for j in range(3):
        out = jnp.where(lane == j + 1, rms[j : j + 1], out)
    sum_ref[...] = out


def finish(me, own, got):
    width = own.shape[1]
    smem = pl.BlockSpec(memory_space=pltpu.SMEM)
    vmem = pl.BlockSpec(memory_space=pltpu.VMEM)
    return call(
        finish_kernel,
        [sds((width, 3 * width), F32), sds((1, width), F32), sds((1, width), F32), sds((3, width), F32), sds((1, 4), F32)],
        vmem=8,
        moved=12 * 3 * width * width,
        in_specs=[smem] + [vmem] * 2,
        out_specs=[vmem] * 5,
    )(me, own, got)


AXES = ("cells", "slots")


def devices():
    return lax.axis_size("cells") * lax.axis_size("slots")


def swap(x, mask, odd=None):
    odd = mask if odd is None else odd
    return lax.ppermute(x, AXES, [(i, i ^ (odd if i % 2 else mask)) for i in range(devices())])


def routes():
    slots = lax.axis_size("slots")
    near, far = [slots, 2 * slots], []
    bit = 4 * slots
    while bit < devices():
        far.append(bit)
        bit *= 2
    small = list(zip(near[:1] + far + near[1:] + [2], near[::-1] + [2] + far))
    large = list(zip([slots, 2] + near[1:] + far, [slots, 2] + far + near[1:]))
    return small, large


def after(x, *others):
    return lax.optimization_barrier((x, *others))[0]


def per_device(
    tokens,
    valid_len,
    library,
    gene_slot,
    counts,
    norm1_gain,
    w_qkv,
    w_out,
    norm2_gain,
    w_up,
    w_down,
    w_decoder,
):
    cells, length, width = tokens.shape
    hidden = w_up.shape[1]
    slot = lax.axis_index("slots")
    cell = slot // 2
    me = jnp.full((1,), slot, jnp.int32)
    pick = lambda a: lax.dynamic_index_in_dim(a, cell, 0, keepdims=False)
    other = lambda a: lax.dynamic_index_in_dim(a, 1 - cell, 0, keepdims=False)

    came = swap(other(tokens), 2)
    near = swap(pick(tokens), 1)
    mine_counts = pick(counts)[None]
    away_counts = other(counts)[None]
    tables = (mine_counts, swap(mine_counts, 1), swap(away_counts, 2), swap(away_counts, 3))
    gain1 = norm1_gain[None]
    gain2 = norm2_gain[None]

    na, qa, ka, va, ta = qkv(me, valid_len, tokens, near, gain1, w_qkv, 0)
    came = after(came, ta, *tables)
    far = swap(came, 1)
    home, nb, gres, keep, q, kb, vb, do, cols, send, small = layer(
        me, valid_len, library, tokens, came, far, gain1, w_qkv, qa, ka, va, ta,
        gain2, w_out, w_up, w_down, w_decoder, gene_slot, tables,
    )

    route, order = routes()
    number = lax.axis_index("cells") * lax.axis_size("slots") + slot
    sides = [jnp.where(slot % 2 == 0, number // even, number // odd) % 2 for even, odd in order[:2]]

    def halve(x, side):
        n = x.shape[0] // 2
        return lax.dynamic_slice_in_dim(x, side * n, n, 0), lax.dynamic_slice_in_dim(x, (1 - side) * n, n, 0)

    def whole(own, got, side):
        return jnp.where(side == 0, jnp.concatenate([own, got], 0), jnp.concatenate([got, own], 0))

    def back(h, p, *others):
        here = after(me, *others) if others else me
        outs = attend_back(h, here, valid_len, q, do, cols, ka, kb, va, vb, p, home, block=do.shape[0] // (2 if h == 0 else 1))
        backs.append(outs[:3])
        return outs[-1]

    got = swap(send, 1)
    backs = []
    p = back(0, None)
    main = keep + after(got, backs[0][0])
    for i in range(2):
        mine, away = halve(main, sides[i])
        got = swap(away, *order[i])
        p = back(1 + i, p, away)
        main = mine + after(got, backs[-1][0])
    got = swap(main, *order[2])
    back(3, p, main)
    main = main + after(got, backs[-1][0])
    got = swap(main, *order[3])

    keep, send = weights(after(me, main), na, nb, backs)
    final_got = swap(send, 1)
    gn_own, gn_send, three = normed_back(me, tokens, came, near, far, w_qkv, small, backs)
    rows3 = three.shape[0]
    gn_got = swap(gn_send, 1)
    final = join(keep, final_got, three)

    final_got = swap(final, *route[0])
    mine, away = tokens_back(me, tokens, came, gain1, gres, gn_own, gn_got)
    final = merge(final, after(final_got, away), rows3)

    final_got = swap(final, *route[1])
    returned = swap(away, 2)
    main = main + after(got, final)
    for masks in order[4:]:
        main = main + swap(main, *masks)
    got = swap(main, *order[1])
    final = merge(final, final_got, rows3)

    final_got = swap(final, *route[2])
    main = whole(main, after(got, final), sides[1])
    got = swap(main, *order[0])
    final = merge(final, after(final_got, main), rows3)

    for masks in route[3:-1]:
        final = merge(final, swap(final, *masks), rows3)
    final_got = swap(final, *route[-1])
    main = whole(main, after(got, final), sides[0])
    returned = after(returned, final).astype(F32)
    grad_tokens = jnp.where(cell == 0, jnp.stack([mine, returned]), jnp.stack([returned, mine]))
    g_down, g_up, g_out = unpack_main(me, main, swap(main, 1), hidden)
    final = merge(final, after(final_got, g_out, grad_tokens), rows3)
    g_qkv, g_gain1, g_gain2, g_dec, summary = finish(me, final, swap(final, 1))
    return (grad_tokens, g_gain1[0], g_qkv, g_out, g_gain2[0], g_up, g_down, g_dec, summary[0])


def solution(mesh):
    in_specs = (
        P("cells", "slots", None),
        P("cells"),
        P("cells"),
        P("cells", None),
        P("cells", "slots"),
        P(),
        P(),
        P(),
        P(),
        P(),
        P(),
        P(),
    )
    out_specs = (P("cells", "slots", None), P(), P(), P(), P(), P(), P(), P(), P())
    return jax.shard_map(
        per_device, mesh=mesh, in_specs=in_specs, out_specs=out_specs, check_vma=False
    )
```
